256 devices in a mesh: gx: 16 (over z_hi, x), gz: 8 (over y, core), ga: 2 (over z_lo).
Axes of the slice: x: 4, y: 4, z: 8 (z_hi: 4, z_lo: 2; z = z_hi * 2 + z_lo), core: 2. Of those that a mesh axis runs over, the one named last changes fastest.
Arguments:
- fields: float32 [5, 512, 32, 2048], P(None, 'gx', 'ga', 'gz'), may hold values from -6 to 6
- diffusivity: float32 [5], replicated, may hold values from 0.05 to 0.5
- subsample_offsets: int32 [3], replicated, may hold values from 0 to 3
- column_id: int32 [1], replicated, may hold values from 0 to 15
- pod_basis: float32 [64, 3, 128, 8, 512], P(None, None, ('gx', 'gz'), 'ga'), may hold values from -12 to 12
- held_block: float32 [16, 3, 128, 8, 512], P(None, None, ('gx', 'gz'), 'ga'), may hold values from -24 to 24
Outputs:
- fields_out: float32 [5, 512, 32, 2048], P(None, 'gx', 'ga', 'gz')
- coefficients: float32 [64, 16], replicated
- r_factor: float32 [16, 16], replicated
- new_columns: float32 [16, 3, 128, 8, 512], P(None, None, ('gx', 'gz'), 'ga')
The draws below stay inside these ranges and needn't reach their ends.
All inputs are finite; a program needn't handle non-finite values.
Results may differ from the reference program's by a relative error of at most 0.000087.
Values sent between devices are 32-bit elements; how exact they have to be, the bound alone decides.
No kernel may reach another device: no remote copies, remote signals or barrier semaphores. Data moves between devices by JAX's collectives and lax.ppermute only.
A program may use at most 192 MiB of HBM per device.

```python
import math
import jax
import jax.numpy as jnp
from jax import lax

FIELDS = 5
STRIDE = 4
RANK = 64
COLS = 16
CX = 32
NX = 512
NY = 32
NZ = 2048
SXG = 128
SYG = 8
SZG = 512
ROWS = 1572864
N_GX = 16


def common_modes(key):
    return jnp.clip(jax.random.normal(key, (RANK, 3, SXG, SYG, SZG), jnp.float32), -6.0, 6.0)


def draw_pod_basis(key, part):
    modes = common_modes(key)
    key = jax.random.fold_in(key, 7)
    spread = 0.3
    scales = jnp.exp(jax.random.uniform(key, (RANK, 1, 1, 1, 1), jnp.float32, -spread, spread))
    return modes * scales


def draw_held_block(key, part):
    modes = common_modes(key)
    key = jax.random.fold_in(key, 9)
    key_first, key_second, key_noise = jax.random.split(key, 3)
    first_weight = jax.random.uniform(key_first, (COLS, 1, 1, 1, 1), jnp.float32, 0.5, 1.5)
    second_weight = jax.random.uniform(key_second, (COLS, 1, 1, 1, 1), jnp.float32, 0.5, 1.5)
    shape = (COLS, 3, SXG, SYG, SZG)
    noise = 0.5 * jnp.clip(jax.random.normal(key_noise, shape, jnp.float32), -6.0, 6.0)
    return first_weight * modes[:COLS] + second_weight * modes[COLS:2 * COLS] + noise


def block_scale(own_key, shape, cuts, smallest, largest):
    def one(axis_at, parts):
        heights = jax.random.uniform(jax.random.fold_in(jax.random.fold_in(own_key, 6), axis_at), (parts,), jnp.float32, smallest / len(cuts), largest / len(cuts))
        return jnp.repeat(jnp.exp(heights), shape[axis_at] // parts).reshape((-1,) + (1,) * (len(shape) - axis_at - 1))

    factor_of = one(*cuts[0])
    for cut in cuts[1:]:
        factor_of = factor_of * one(*cut)
    return factor_of


def scatter_about(own_key, dims, deviation, reach, cuts=(), kind=jnp.bfloat16):
    drawn = jax.random.normal(own_key, dims, jnp.float32) * deviation
    if len(cuts) > 0:
        drawn = block_scale(own_key, dims, cuts, -0.22, 0.18) * drawn
    return jnp.clip(drawn, min=-reach, max=reach).astype(kind)


def setup_inputs(seed: int = 0) -> dict:
    splits = jax.random.split(jax.random.key(seed), 7)
    return {
        "fields": scatter_about(splits[0], (FIELDS, NX, NY, NZ), 1.0, 6.0, ((1, 16), (2, 2), (3, 8)), jnp.float32),
        "diffusivity": jnp.clip(jnp.exp(jax.random.uniform(splits[1], (FIELDS,), jnp.float32, math.log(0.05), math.log(0.5))), 0.05, 0.5),
        "subsample_offsets": jax.random.randint(splits[2], (3,), 0, STRIDE).astype(jnp.int32),
        "column_id": jax.random.randint(splits[3], (1,), 0, COLS).astype(jnp.int32),
        "pod_basis": draw_pod_basis(jax.random.fold_in(splits[6], 71), 0),
        "held_block": draw_held_block(jax.random.fold_in(splits[6], 71), 0),
    }


time_step = 0.1
smagorinsky = 0.02

def tendency(padded, diffusivity):
    centre = padded[:, 1:-1, 1:-1, 1:-1]
    x_plus = padded[:, 2:, 1:-1, 1:-1]
    x_minus = padded[:, :-2, 1:-1, 1:-1]
    y_plus = padded[:, 1:-1, 2:, 1:-1]
    y_minus = padded[:, 1:-1, :-2, 1:-1]
    z_plus = padded[:, 1:-1, 1:-1, 2:]
    z_minus = padded[:, 1:-1, 1:-1, :-2]
    slope_x = 0.5 * (x_plus - x_minus)
    slope_y = 0.5 * (y_plus - y_minus)
    slope_z = 0.5 * (z_plus - z_minus)
    strain = lax.optimization_barrier(jnp.sum(slope_x[:3] * slope_x[:3] + slope_y[:3] * slope_y[:3] + slope_z[:3] * slope_z[:3], axis=0))
    eddy = smagorinsky * jnp.sqrt(strain)
    advect = centre[0] * slope_x + centre[1] * slope_y + centre[2] * slope_z
    laplace = x_plus + x_minus + y_plus + y_minus + z_plus + z_minus - 6.0 * centre
    return (diffusivity[:, None, None, None] + eddy) * laplace - advect

def pad_global(state):
    wrapped = jnp.pad(state, ((0, 0), (1, 1), (0, 0), (1, 1)), mode='wrap')
    return jnp.pad(wrapped, ((0, 0), (0, 0), (1, 1), (0, 0)))

def rate(state, diffusivity):
    padded = pad_global(state)

    def slab(number):
        piece = lax.dynamic_slice_in_dim(padded, number * CX, CX + 2, 1)
        return tendency(piece, diffusivity)
    blocks = lax.map(slab, jnp.arange(N_GX, dtype=jnp.int32))
    return jnp.moveaxis(blocks, 0, 1).reshape(state.shape)

def inner(left, right):
    return jnp.dot(left.astype(jnp.float32), right.T.astype(jnp.float32), precision=lax.Precision.HIGHEST, preferred_element_type=jnp.float32)

def reference(fields, diffusivity, subsample_offsets, column_id, pod_basis, held_block):
    first = fields + time_step * rate(fields, diffusivity)
    fields_out = 0.5 * (fields + first + time_step * rate(first, diffusivity))
    velocity = fields_out[:3].reshape(3, SXG, STRIDE, SYG, STRIDE, SZG, STRIDE)
    picked = lax.dynamic_index_in_dim(velocity, subsample_offsets[0].astype(jnp.int32), 6, keepdims=False)
    picked = lax.dynamic_index_in_dim(picked, subsample_offsets[1].astype(jnp.int32), 4, keepdims=False)
    snapshot = lax.dynamic_index_in_dim(picked, subsample_offsets[2].astype(jnp.int32), 2, keepdims=False)
    chosen = (jnp.arange(COLS, dtype=jnp.int32) == column_id[0].astype(jnp.int32)).reshape(COLS, 1, 1, 1, 1)
    block = jnp.where(chosen, snapshot[None], held_block)
    matrix_b = block.reshape(COLS, ROWS)
    matrix_q = pod_basis.reshape(RANK, ROWS)
    first_coef = inner(matrix_q, matrix_b) / ROWS
    residual_one = matrix_b - inner(first_coef.T, matrix_q.T)
    second_coef = inner(matrix_q, residual_one) / ROWS
    residual_two = residual_one - inner(second_coef.T, matrix_q.T)
    coefficients = first_coef + second_coef
    gram = inner(residual_two, residual_two) / ROWS
    lower = jnp.linalg.cholesky(gram)
    columns = jax.scipy.linalg.solve_triangular(lower, residual_two, lower=True)
    return (fields_out, coefficients, lower.T, columns.reshape(held_block.shape))
```

```python
import jax
import jax.numpy as jnp
from jax import lax
from jax.experimental import pallas as pl
from jax.experimental.pallas import tpu as pltpu
from jax.sharding import PartitionSpec as P

STRIDE = 4
LANES = 128

time_step = 0.1
smagorinsky = 0.02

VMEM = pl.BlockSpec(memory_space=pltpu.VMEM)
SMEM = pl.BlockSpec(memory_space=pltpu.SMEM)
HIGH = lax.Precision.HIGHEST
AXES = ("gx", "gz", "ga")


def params(mib):
    return pltpu.CompilerParams(vmem_limit_bytes=mib * 1024 * 1024)


def struct(*shape):
    return jax.ShapeDtypeStruct(shape, jnp.float32)


def iota(shape, dim):
    return lax.broadcasted_iota(jnp.int32, shape, dim)


def dot(left, right, left_dim, right_dim):
    return lax.dot_general(
        left,
        right,
        (((left_dim,), (right_dim,)), ((), ())),
        precision=HIGH,
        preferred_element_type=jnp.float32,
    )


def put_row(x, upper, top, bottom, ref, field, half):
    row = jnp.where(upper, bottom[0:1, :], top[7:8, :])
    rows = pl.ds(pl.multiple_of(x // 8 * 8, 8), 8)
    lanes = slice(half * LANES, (half + 1) * LANES)
    here = iota((8, LANES), 0) == x % 8
    ref[field, rows, lanes] = jnp.where(here, row, ref[field, rows, lanes])


def put_columns(x, lane, value, ref, field, tile, from_end):
    shift = (x + 1) % LANES if from_end else x
    rows = slice(tile * 8, tile * 8 + 8)
    ref[field, rows, :] = jnp.where(lane == x, pltpu.roll(value, shift, 1), ref[field, rows, :])


def pack_kernel(fields, x_low, x_high, y_row, z_low, z_high):
    count, cells, height, _ = fields.shape
    upper = lax.axis_index("ga") > 0
    lane = iota((8, LANES), 1)
    y_row[...] = jnp.zeros_like(y_row)
    x_low[...] = fields[:, 0]
    x_high[...] = fields[:, cells - 1]
    z_low[...] = jnp.zeros_like(z_low)
    z_high[...] = jnp.zeros_like(z_high)

    def body(x, carry):
        for f in range(count):
            for half in range(2):
                lanes = slice(half * LANES, (half + 1) * LANES)
                bottom = fields[f, x, 0:8, lanes]
                top = fields[f, x, height - 8 : height, lanes]
                put_row(x, upper, top, bottom, y_row, f, half)
                for tile, value in ((0, bottom), (1, top)):
                    put_columns(
                        x, lane, value, (z_low, z_high)[half], f, tile, half == 1
                    )
        return carry

    lax.fori_loop(0, cells, body, 0)


def stage_plane(x, current, before, after, y_halo, z_before, z_after, diffusivity, upper):
    count = current.shape[0]
    lane = iota((8, LANES), 1)
    sub = iota((8, LANES), 0)
    first_lane, last_lane = lane == 0, lane == LANES - 1
    first_sub, last_sub = sub == 0, sub == 7
    below = jnp.where(upper, 1.0, 0.0)
    above = 1.0 - below
    row_shift = (jnp.where(upper, 8, 15) - x % 8) % 8
    centre, slope_x, slope_y, slope_z, laplace = {}, {}, {}, {}, {}
    for f in range(count):
        for tile in range(2):
            for half in range(2):
                centre[f, tile, half] = current[
                    f, x, tile * 8 : tile * 8 + 8, half * LANES : (half + 1) * LANES
                ]
        for half in range(2):
            lanes = slice(half * LANES, (half + 1) * LANES)
            row = y_halo[f, pl.ds(pl.multiple_of(x // 8 * 8, 8), 8), lanes]
            row = pltpu.roll(row, row_shift, 0)
            row_low, row_high = row * below, row * above
            down = [pltpu.roll(centre[f, tile, half], 1, 0) for tile in range(2)]
            up = [pltpu.roll(centre[f, tile, half], 7, 0) for tile in range(2)]
            y_minus = (
                jnp.where(first_sub, row_low, down[0]),
                jnp.where(first_sub, down[0], down[1]),
            )
            y_plus = (
                jnp.where(last_sub, up[1], up[0]),
                jnp.where(last_sub, row_high, up[1]),
            )
            for tile in range(2):
                slope_y[f, tile, half] = y_plus[tile] - y_minus[tile]
                laplace[f, tile, half] = y_plus[tile] + y_minus[tile]
        for tile in range(2):
            rows = slice(tile * 8, tile * 8 + 8)
            from_low = pltpu.roll(z_before[f, rows, :], (LANES - x) % LANES, 1)
            from_high = pltpu.roll(z_after[f, rows, :], LANES - 1 - x, 1)
            right = [pltpu.roll(centre[f, tile, half], 1, 1) for half in range(2)]
            left = [pltpu.roll(centre[f, tile, half], LANES - 1, 1) for half in range(2)]
            z_minus = (
                jnp.where(first_lane, from_low, right[0]),
                jnp.where(first_lane, right[0], right[1]),
            )
            z_plus = (
                jnp.where(last_lane, left[1], left[0]),
                jnp.where(last_lane, from_high, left[1]),
            )
            for half in range(2):
                lanes = slice(half * LANES, (half + 1) * LANES)
                slope_z[f, tile, half] = z_plus[half] - z_minus[half]
                x_minus, x_plus = before(f, rows, lanes), after(f, rows, lanes)
                slope_x[f, tile, half] = x_plus - x_minus
                laplace[f, tile, half] = (
                    laplace[f, tile, half]
                    + (z_plus[half] + z_minus[half])
                    + (x_plus + x_minus)
                    - 6.0 * centre[f, tile, half]
                )
    rates = {}
    for tile in range(2):
        for half in range(2):
            at = (tile, half)
            strain = 0.0
            for f in range(3):
                strain = strain + (
                    slope_x[f, *at] * slope_x[f, *at]
                    + slope_y[f, *at] * slope_y[f, *at]
                    + slope_z[f, *at] * slope_z[f, *at]
                )
            eddy = smagorinsky * jnp.sqrt(0.25 * strain)
            speeds = [0.5 * centre[f, *at] for f in range(3)]
            for f in range(count):
                advect = (
                    speeds[0] * slope_x[f, *at]
                    + speeds[1] * slope_y[f, *at]
                    + speeds[2] * slope_z[f, *at]
                )
                rates[f, *at] = (diffusivity[f] + eddy) * laplace[f, *at] - advect
    return centre, rates


def planes(current, halos, diffusivity, finish):
    x_before, x_after, y_halo, z_before, z_after = halos
    cells = current.shape[1]
    upper = lax.axis_index("ga") > 0

    def one(x, before, after):
        centre, rates = stage_plane(
            x, current, before, after, y_halo, z_before, z_after, diffusivity, upper
        )
        finish(x, centre, rates)

    def inside(offset, x):
        return lambda f, rows, lanes: current[f, x + offset, rows, lanes]

    def outside(ref):
        return lambda f, rows, lanes: ref[f, rows, lanes]

    one(0, outside(x_before), inside(1, 0))

    def body(x, carry):
        one(x, inside(-1, x), inside(1, x))
        return carry

    lax.fori_loop(1, cells - 1, body, 0)
    one(cells - 1, inside(-1, cells - 1), outside(x_after))


def first_kernel(
    diffusivity, current, x_before, x_after, y_halo, z_before, z_after,
    first, x_low, x_high, y_row, z_low, z_high,
):
    count, cells = current.shape[:2]
    upper = lax.axis_index("ga") > 0
    lane = iota((8, LANES), 1)
    y_row[...] = jnp.zeros_like(y_row)
    z_low[...] = jnp.zeros_like(z_low)
    z_high[...] = jnp.zeros_like(z_high)

    def finish(x, centre, rates):
        for f in range(count):
            new = {}
            for tile in range(2):
                for half in range(2):
                    rows = slice(tile * 8, tile * 8 + 8)
                    lanes = slice(half * LANES, (half + 1) * LANES)
                    value = centre[f, tile, half] + time_step * rates[f, tile, half]
                    new[tile, half] = value
                    first[f, x, rows, lanes] = value
                    if isinstance(x, int):
                        (x_low if x == 0 else x_high)[f, rows, lanes] = value
            for half in range(2):
                put_row(x, upper, new[1, half], new[0, half], y_row, f, half)
            for tile in range(2):
                put_columns(x, lane, new[tile, 0], z_low, f, tile, False)
                put_columns(x, lane, new[tile, 1], z_high, f, tile, True)

    planes(current, (x_before, x_after, y_halo, z_before, z_after), diffusivity, finish)


def second_kernel(
    diffusivity, offsets, start, current, x_before, x_after, y_halo, z_before, z_after,
    result, snapshot, picked,
):
    count, cells, height, width = current.shape

    def finish(x, centre, rates):
        for f in range(count):
            for tile in range(2):
                for half in range(2):
                    rows = slice(tile * 8, tile * 8 + 8)
                    lanes = slice(half * LANES, (half + 1) * LANES)
                    result[f, x, rows, lanes] = 0.5 * (
                        start[f, x, rows, lanes]
                        + centre[f, tile, half]
                        + time_step * rates[f, tile, half]
                    )

    planes(current, (x_before, x_after, y_halo, z_before, z_after), diffusivity, finish)
    levels = height // STRIDE
    picked[...] = jnp.zeros_like(picked)
    for column in range(cells // STRIDE):
        for f in range(3):
            for tile in range(2):
                plane = result[f, column * STRIDE + offsets[2], tile * 8 : tile * 8 + 8, :]
                plane = pltpu.roll(plane, (8 - offsets[1]) % 8, 0)
                for part in range(2):
                    row = column * 16 + f * levels + tile * 2 + part
                    picked[row : row + 1, :] = plane[part * STRIDE : part * STRIDE + 1, :]
    points = width // STRIDE
    choose = iota((width, LANES), 0) == STRIDE * (iota((width, LANES), 1) % points) + offsets[0]
    snapshot[...] = dot(picked[...], choose.astype(jnp.float32), 1, 0)


def gram_kernel(basis, held, joined, message):
    rank, _, _, levels, points = basis.shape
    columns = held.shape[0]
    total = rank + columns
    for c in range(3):
        for level in range(levels):
            lanes = slice((c * levels + level) * points, (c * levels + level + 1) * points)
            joined[0:rank, lanes] = basis[:, c, 0, level, :]
            joined[rank:total, lanes] = held[:, c, 0, level, :]

    def body(step, gram):
        part = joined[:, pl.ds(pl.multiple_of(step * points, LANES), points)]
        return gram + dot(part, part, 1, 1)

    gram = lax.fori_loop(0, 3 * levels, body, jnp.zeros((total, total), jnp.float32))
    gram = jnp.concatenate([gram, jnp.zeros((total, LANES - total), jnp.float32)], axis=1)
    for piece in range(3):
        message[piece * total : (piece + 1) * total, :] = pltpu.roll(
            gram, (LANES - 27 * piece) % LANES, 1
        )
    message[3 * total :, :] = jnp.zeros((message.shape[0] - 3 * total, LANES), jnp.float32)


def product_kernel(relayed, joined, pieces, message, column, partial):
    total = joined.shape[0]
    groups = total // 8
    lane = iota((8, LANES), 1)
    low = iota((1, LANES), 1) < LANES // 2
    sums = [jnp.zeros((8, LANES), jnp.float32) for _ in range(groups + 1)]
    for row in range(12):
        for pair in range(4):
            tile = row * 4 + pair
            lanes = slice(tile * LANES, (tile + 1) * LANES)
            values = jnp.where(
                low,
                relayed[2 * pair, row : row + 1, :],
                relayed[2 * pair + 1, row : row + 1, :],
            )
            values = jnp.broadcast_to(values, (8, LANES))
            column[:, lanes] = values
            for group in range(groups):
                sums[group] += joined[group * 8 : group * 8 + 8, lanes] * values
            sums[groups] += values * values
    partial[...] = jnp.zeros_like(partial)
    for group in range(groups + 1):
        partial[group * 8 : group * 8 + 8, :] = sums[group]
    products = dot(jnp.ones((8, LANES), jnp.float32), partial[...], 1, 1)
    own = jnp.sum(pieces[...].reshape(-1, 8, LANES), axis=0)
    own = jnp.broadcast_to(jnp.sum(own, axis=0, keepdims=True), (8, LANES))
    values = jnp.where(lane < 96, products, pltpu.roll(own, 96, 1))
    count = message.shape[0]
    message[...] = jnp.broadcast_to(values[None], (count // 8, 8, LANES)).reshape(count, LANES)


def final_kernel(column_id, gathered, joined, column, coefficients, r_factor, columns_out):
    total = joined.shape[0]
    rank, count = coefficients.shape
    _, _, _, levels, points = columns_out.shape
    rows_total = float(gathered.shape[0] * joined.shape[1])
    chosen = column_id[0]
    received = gathered[...]
    sums = jnp.sum(received.reshape(-1, 8, LANES), axis=0)
    sums = jnp.sum(sums, axis=0, keepdims=True) / rows_total
    lane = iota((total, LANES), 1)
    pieces = [
        pltpu.roll(received[piece * total : (piece + 1) * total, :], (27 * piece + 32) % LANES, 1)
        for piece in range(3)
    ]
    gram = jnp.where(lane < 27, pieces[0], jnp.where(lane < 54, pieces[1], pieces[2])) / rows_total
    down = jnp.broadcast_to(sums, (LANES, LANES)).T
    modes = gram[:rank, :rank]
    shifted = pltpu.roll(gram, LANES - rank, 1)
    first = jnp.where(lane[:rank] == chosen, down[:rank], shifted[:rank])[:, :count]
    block_lane, block_sub = iota((count, LANES), 1), iota((count, LANES), 0)
    square = jnp.broadcast_to(sums[:, total : total + 1], (1, LANES))
    across = jnp.where(
        block_lane[0:1] == chosen, square, pltpu.roll(sums, LANES - rank, 1)
    )
    block = jnp.where(block_lane == chosen, down[rank:total], shifted[rank:total])
    block = jnp.where(block_sub == chosen, jnp.broadcast_to(across, (count, LANES)), block)
    second = first - dot(modes, first, 1, 0)
    both = first + second
    third = first - dot(modes, both, 1, 0)
    coefficients[...] = both
    square = dot(
        jnp.concatenate([first, both], axis=0), jnp.concatenate([both, third], axis=0), 0, 0
    )
    square = jnp.concatenate([square, jnp.zeros((count, LANES - count), jnp.float32)], axis=1)
    state = jnp.where(block_lane < count, block - square, 0.0)
    state = jnp.where(block_lane == block_sub + count, 1.0, state)
    for step in range(count - 1):
        row = state[step : step + 1, :]
        scale = state[:, step : step + 1] / row[:, step : step + 1]
        scale = jnp.where(block_sub > step, jnp.broadcast_to(scale, (count, LANES)), 0.0)
        state = state - scale * row
    diagonal = jnp.sum(jnp.where(block_lane == block_sub, state, 0.0), axis=1, keepdims=True)
    state = state / jnp.sqrt(diagonal)
    r_factor[...] = jnp.where(block_lane >= block_sub, state, 0.0)[:, :count]
    inverse = pltpu.roll(state, LANES - count, 1)
    inverse = jnp.where(block_lane < count, inverse, 0.0)
    onto_modes = dot(inverse[:, :count], both, 1, 1)
    own = jnp.sum(jnp.where(block_lane == chosen, inverse, 0.0), axis=1, keepdims=True)
    onto_block = pltpu.roll(jnp.where(block_lane == chosen, 0.0, inverse), rank, 1)
    onto_modes = jnp.concatenate(
        [-onto_modes, jnp.zeros((count, LANES - rank), jnp.float32)], axis=1
    )
    weights = jnp.where(block_lane < rank, onto_modes, onto_block)[:, :total]
    for c in range(3):
        for level in range(levels):
            lanes = slice((c * levels + level) * points, (c * levels + level + 1) * points)
            columns_out[:, c, 0, level, :] = (
                dot(weights, joined[:, lanes], 1, 0) + own * column[0:1, lanes]
            )


def shifted(value, axis, step):
    count = lax.axis_size(axis)
    return lax.ppermute(value, axis, [(i, (i + step) % count) for i in range(count)])


def exchange(faces):
    x_low, x_high, y_row, z_low, z_high = faces
    return (
        shifted(x_high, "gx", 1),
        shifted(x_low, "gx", -1),
        shifted(y_row, "ga", 1),
        shifted(z_high, "gz", 1),
        shifted(z_low, "gz", -1),
    )


def on_device(fields, diffusivity, subsample_offsets, column_id, pod_basis, held_block):
    count, cells, height, width = fields.shape
    rank, columns = pod_basis.shape[0], held_block.shape[0]
    devices = 1
    for axis in AXES:
        devices *= lax.axis_size(axis)
    points = held_block.shape[-1]
    length = 3 * held_block.shape[3] * points
    faces = (
        struct(count, height, width),
        struct(count, height, width),
        struct(count, cells, width),
        struct(count, height, LANES),
        struct(count, height, LANES),
    )

    packed = pl.pallas_call(
        pack_kernel, in_specs=[VMEM], out_specs=[VMEM] * 5, out_shape=faces,
        compiler_params=params(16),
    )(fields)
    halos = exchange(packed)

    joined, gram_message = pl.pallas_call(
        gram_kernel, in_specs=[VMEM] * 2, out_specs=[VMEM] * 2,
        out_shape=(struct(rank + columns, length), struct(devices, LANES)),
        compiler_params=params(24),
    )(pod_basis, held_block)
    pieces = lax.all_to_all(gram_message, AXES, 0, 0, tiled=True)

    first, *packed = pl.pallas_call(
        first_kernel, in_specs=[SMEM] + [VMEM] * 6, out_specs=[VMEM] * 6,
        out_shape=(struct(*fields.shape),) + faces,
        compiler_params=params(24),
    )(diffusivity, fields, *halos)
    halos = exchange(packed)

    fields_out, snapshot = pl.pallas_call(
        second_kernel, in_specs=[SMEM] * 2 + [VMEM] * 7, out_specs=[VMEM] * 2,
        out_shape=(struct(*fields.shape), struct(LANES, LANES)),
        scratch_shapes=[pltpu.VMEM((LANES, width), jnp.float32)],
        compiler_params=params(24),
    )(diffusivity, subsample_offsets, fields, first, *halos)
    relayed = lax.all_to_all(snapshot.reshape(8, 16, LANES), "gz", 0, 0, tiled=True)

    message, column = pl.pallas_call(
        product_kernel, in_specs=[VMEM] * 3, out_specs=[VMEM] * 2,
        out_shape=(struct(devices, LANES), struct(8, length)),
        scratch_shapes=[pltpu.VMEM((LANES, LANES), jnp.float32)],
        compiler_params=params(16),
    )(relayed, joined, pieces)
    gathered = lax.all_to_all(message, AXES, 0, 0, tiled=True)

    coefficients, r_factor, new_columns = pl.pallas_call(
        final_kernel, in_specs=[SMEM] + [VMEM] * 3, out_specs=[VMEM] * 3,
        out_shape=(
            struct(rank, columns), struct(columns, columns), struct(*held_block.shape)
        ),
        compiler_params=params(24),
    )(column_id, gathered, joined, column)
    return fields_out, coefficients, r_factor, new_columns


def solution(mesh):
    placed = (
        P(None, "gx", "ga", "gz"),
        P(),
        P(),
        P(),
        P(None, None, ("gx", "gz"), "ga", None),
        P(None, None, ("gx", "gz"), "ga", None),
    )
    return jax.shard_map(
        on_device,
        mesh=mesh,
        in_specs=placed,
        out_specs=(P(None, "gx", "ga", "gz"), P(), P(), P(None, None, ("gx", "gz"), "ga", None)),
        check_vma=False,
    )
```

```python
import jax
import jax.numpy as jnp
from jax import lax
from jax.experimental import pallas as pl
from jax.experimental.pallas import tpu as pltpu
from jax.sharding import PartitionSpec as P

STRIDE = 4
LANES = 128
PACK_UNROLL = 4
PLANE_UNROLL = 3

time_step = 0.1
smagorinsky = 0.02

VMEM = pl.BlockSpec(memory_space=pltpu.VMEM)
SMEM = pl.BlockSpec(memory_space=pltpu.SMEM)
HIGH = lax.Precision.HIGHEST
AXES = ("gx", "gz", "ga")


def params(mib):
    return pltpu.CompilerParams(vmem_limit_bytes=mib * 1024 * 1024)


def struct(*shape):
    return jax.ShapeDtypeStruct(shape, jnp.float32)


def iota(shape, dim):
    return lax.broadcasted_iota(jnp.int32, shape, dim)


def dot(left, right, left_dim, right_dim):
    return lax.dot_general(
        left,
        right,
        (((left_dim,), (right_dim,)), ((), ())),
        precision=HIGH,
        preferred_element_type=jnp.float32,
    )


def put_row(x, upper, top, bottom, ref, field, half):
    row = jnp.where(upper, bottom[0:1, :], top[7:8, :])
    rows = pl.ds(pl.multiple_of(x // 8 * 8, 8), 8)
    lanes = slice(half * LANES, (half + 1) * LANES)
    here = iota((8, LANES), 0) == x % 8
    ref[field, rows, lanes] = jnp.where(here, row, ref[field, rows, lanes])


def put_columns(x, lane, value, ref, field, tile, from_end):
    shift = (x + 1) % LANES if from_end else x
    rows = slice(tile * 8, tile * 8 + 8)
    ref[field, rows, :] = jnp.where(lane == x, pltpu.roll(value, shift, 1), ref[field, rows, :])


def pack_kernel(fields, x_low, x_high, y_row, z_low, z_high):
    count, cells, height, _ = fields.shape
    upper = lax.axis_index("ga") > 0
    lane = iota((8, LANES), 1)
    y_row[...] = jnp.zeros_like(y_row)
    x_low[...] = fields[:, 0]
    x_high[...] = fields[:, cells - 1]
    z_low[...] = jnp.zeros_like(z_low)
    z_high[...] = jnp.zeros_like(z_high)

    def body(x, carry):
        for f in range(count):
            for half in range(2):
                lanes = slice(half * LANES, (half + 1) * LANES)
                bottom = fields[f, x, 0:8, lanes]
                top = fields[f, x, height - 8 : height, lanes]
                put_row(x, upper, top, bottom, y_row, f, half)
                for tile, value in ((0, bottom), (1, top)):
                    put_columns(
                        x, lane, value, (z_low, z_high)[half], f, tile, half == 1
                    )
        return carry

    lax.fori_loop(0, cells, body, 0, unroll=PACK_UNROLL)


def stage_plane(x, current, before, after, y_halo, z_before, z_after, diffusivity, upper):
    count = current.shape[0]
    lane = iota((8, LANES), 1)
    sub = iota((8, LANES), 0)
    first_lane, last_lane = lane == 0, lane == LANES - 1
    first_sub, last_sub = sub == 0, sub == 7
    below = jnp.where(upper, 1.0, 0.0)
    above = 1.0 - below
    row_shift = (jnp.where(upper, 8, 15) - x % 8) % 8
    centre, slope_x, slope_y, slope_z, laplace = {}, {}, {}, {}, {}
    for f in range(count):
        for tile in range(2):
            for half in range(2):
                centre[f, tile, half] = current[
                    f, x, tile * 8 : tile * 8 + 8, half * LANES : (half + 1) * LANES
                ]
        for half in range(2):
            lanes = slice(half * LANES, (half + 1) * LANES)
            row = y_halo[f, pl.ds(pl.multiple_of(x // 8 * 8, 8), 8), lanes]
            row = pltpu.roll(row, row_shift, 0)
            row_low, row_high = row * below, row * above
            down = [pltpu.roll(centre[f, tile, half], 1, 0) for tile in range(2)]
            up = [pltpu.roll(centre[f, tile, half], 7, 0) for tile in range(2)]
            y_minus = (
                jnp.where(first_sub, row_low, down[0]),
                jnp.where(first_sub, down[0], down[1]),
            )
            y_plus = (
                jnp.where(last_sub, up[1], up[0]),
                jnp.where(last_sub, row_high, up[1]),
            )
            for tile in range(2):
                slope_y[f, tile, half] = y_plus[tile] - y_minus[tile]
                laplace[f, tile, half] = y_plus[tile] + y_minus[tile]
        for tile in range(2):
            rows = slice(tile * 8, tile * 8 + 8)
            from_low = pltpu.roll(z_before[f, rows, :], (LANES - x) % LANES, 1)
            from_high = pltpu.roll(z_after[f, rows, :], LANES - 1 - x, 1)
            right = [pltpu.roll(centre[f, tile, half], 1, 1) for half in range(2)]
            left = [pltpu.roll(centre[f, tile, half], LANES - 1, 1) for half in range(2)]
            z_minus = (
                jnp.where(first_lane, from_low, right[0]),
                jnp.where(first_lane, right[0], right[1]),
            )
            z_plus = (
                jnp.where(last_lane, left[1], left[0]),
                jnp.where(last_lane, from_high, left[1]),
            )
            for half in range(2):
                lanes = slice(half * LANES, (half + 1) * LANES)
                slope_z[f, tile, half] = z_plus[half] - z_minus[half]
                x_minus, x_plus = before(f, rows, lanes), after(f, rows, lanes)
                slope_x[f, tile, half] = x_plus - x_minus
                laplace[f, tile, half] = (
                    laplace[f, tile, half]
                    + (z_plus[half] + z_minus[half])
                    + (x_plus + x_minus)
                    - 6.0 * centre[f, tile, half]
                )
    rates = {}
    for tile in range(2):
        for half in range(2):
            at = (tile, half)
            strain = 0.0
            for f in range(3):
                strain = strain + (
                    slope_x[f, *at] * slope_x[f, *at]
                    + slope_y[f, *at] * slope_y[f, *at]
                    + slope_z[f, *at] * slope_z[f, *at]
                )
            eddy = smagorinsky * jnp.sqrt(0.25 * strain)
            speeds = [0.5 * centre[f, *at] for f in range(3)]
            for f in range(count):
                advect = (
                    speeds[0] * slope_x[f, *at]
                    + speeds[1] * slope_y[f, *at]
                    + speeds[2] * slope_z[f, *at]
                )
                rates[f, *at] = (diffusivity[f] + eddy) * laplace[f, *at] - advect
    return centre, rates


def planes(current, halos, diffusivity, finish):
    x_before, x_after, y_halo, z_before, z_after = halos
    cells = current.shape[1]
    upper = lax.axis_index("ga") > 0

    def one(x, before, after):
        centre, rates = stage_plane(
            x, current, before, after, y_halo, z_before, z_after, diffusivity, upper
        )
        finish(x, centre, rates)

    def inside(offset, x):
        return lambda f, rows, lanes: current[f, x + offset, rows, lanes]

    def outside(ref):
        return lambda f, rows, lanes: ref[f, rows, lanes]

    one(0, outside(x_before), inside(1, 0))

    def body(x, carry):
        one(x, inside(-1, x), inside(1, x))
        return carry

    lax.fori_loop(1, cells - 1, body, 0, unroll=PLANE_UNROLL)
    one(cells - 1, inside(-1, cells - 1), outside(x_after))


def first_kernel(
    diffusivity, folded, current, x_before, x_after, y_halo, z_before, z_after,
    first, x_low, x_high, y_row, z_low, z_high,
):
    count, cells = current.shape[:2]
    upper = lax.axis_index("ga") > 0
    lane = iota((8, LANES), 1)
    y_row[...] = jnp.zeros_like(y_row)
    z_low[...] = jnp.zeros_like(z_low)
    z_high[...] = jnp.zeros_like(z_high)
    for group in range(3):
        lanes = slice(group % 2 * LANES, (group % 2 + 1) * LANES)
        given = jnp.where(upper, folded[group * 8 : group * 8 + 8], folded[group * 8 + 24 : group * 8 + 32])
        y_row[group // 2, cells:, lanes] = given

    def finish(x, centre, rates):
        for f in range(count):
            new = {}
            for tile in range(2):
                for half in range(2):
                    rows = slice(tile * 8, tile * 8 + 8)
                    lanes = slice(half * LANES, (half + 1) * LANES)
                    value = centre[f, tile, half] + time_step * rates[f, tile, half]
                    new[tile, half] = value
                    first[f, x, rows, lanes] = value
                    if isinstance(x, int):
                        (x_low if x == 0 else x_high)[f, rows, lanes] = value
            for half in range(2):
                put_row(x, upper, new[1, half], new[0, half], y_row, f, half)
            for tile in range(2):
                put_columns(x, lane, new[tile, 0], z_low, f, tile, False)
                put_columns(x, lane, new[tile, 1], z_high, f, tile, True)

    planes(current, (x_before, x_after, y_halo, z_before, z_after), diffusivity, finish)


def second_kernel(
    diffusivity, offsets, folded, start, current, x_before, x_after, y_halo, z_before, z_after,
    result, snapshot, picked,
):
    count, cells, height, width = current.shape

    def finish(x, centre, rates):
        for f in range(count):
            for tile in range(2):
                for half in range(2):
                    rows = slice(tile * 8, tile * 8 + 8)
                    lanes = slice(half * LANES, (half + 1) * LANES)
                    result[f, x, rows, lanes] = 0.5 * (
                        start[f, x, rows, lanes]
                        + centre[f, tile, half]
                        + time_step * rates[f, tile, half]
                    )

    planes(current, (x_before, x_after, y_halo, z_before, z_after), diffusivity, finish)
    levels = height // STRIDE
    picked[...] = jnp.zeros_like(picked)
    for column in range(cells // STRIDE):
        for f in range(3):
            for tile in range(2):
                plane = result[f, column * STRIDE + offsets[2], tile * 8 : tile * 8 + 8, :]
                plane = pltpu.roll(plane, (8 - offsets[1]) % 8, 0)
                for part in range(2):
                    row = column * 16 + f * levels + tile * 2 + part
                    picked[row : row + 1, :] = plane[part * STRIDE : part * STRIDE + 1, :]
    points = width // STRIDE
    choose = iota((width, LANES), 0) == STRIDE * (iota((width, LANES), 1) % points) + offsets[0]
    snapshot[...] = dot(picked[...], choose.astype(jnp.float32), 1, 0)
    upper = lax.axis_index("ga") > 0
    for group in range(3):
        lanes = slice(group % 2 * LANES, (group % 2 + 1) * LANES)
        kept = jnp.where(upper, folded[group * 8 + 24 : group * 8 + 32], folded[group * 8 : group * 8 + 8])
        kept = kept + y_halo[group // 2, cells:, lanes]
        for column in range(cells // STRIDE):
            row = column * 16 + 12 + group
            snapshot[row : row + 1, :] = kept[column : column + 1]


def gram_kernel(basis, held, joined, folded):
    rank, _, _, levels, points = basis.shape
    columns = held.shape[0]
    total = rank + columns
    half = total // 2
    for c in range(3):
        for level in range(levels):
            lanes = slice((c * levels + level) * points, (c * levels + level + 1) * points)
            joined[0:rank, lanes] = basis[:, c, 0, level, :]
            joined[rank:total, lanes] = held[:, c, 0, level, :]

    def body(step, gram):
        part = joined[:, pl.ds(pl.multiple_of(step * points, LANES), points)]
        return gram + dot(part, part, 1, 1)

    gram = lax.fori_loop(0, 3 * levels, body, jnp.zeros((total, total), jnp.float32))
    gram = jnp.concatenate([gram, jnp.zeros((total, LANES - total), jnp.float32)], axis=1)
    lane, sub = iota((half, LANES), 1), iota((half, LANES), 0)
    lower = pltpu.roll(gram[half:], LANES - half, 1)
    diagonal = jnp.sum(jnp.where(lane == sub, lower, 0.0), axis=1, keepdims=True)
    values = jnp.where((lane < sub), lower, gram[:half])
    values = jnp.where(lane == total, jnp.broadcast_to(diagonal, (half, LANES)), values)
    folded[0:half, :] = jnp.where(lane <= total, values, 0.0)
    folded[half:, :] = jnp.zeros((folded.shape[0] - half, LANES), jnp.float32)


def product_kernel(relayed, joined, message, column, partial):
    total = joined.shape[0]
    groups = total // 8
    low = iota((1, LANES), 1) < LANES // 2
    sums = [jnp.zeros((8, LANES), jnp.float32) for _ in range(groups + 1)]
    for row in range(12):
        for pair in range(4):
            tile = row * 4 + pair
            lanes = slice(tile * LANES, (tile + 1) * LANES)
            values = jnp.where(
                low,
                relayed[2 * pair, row : row + 1, :],
                relayed[2 * pair + 1, row : row + 1, :],
            )
            values = jnp.broadcast_to(values, (8, LANES))
            column[:, lanes] = values
            for group in range(groups):
                sums[group] += joined[group * 8 : group * 8 + 8, lanes] * values
            sums[groups] += values * values
    partial[...] = jnp.zeros_like(partial)
    for group in range(groups + 1):
        partial[group * 8 : group * 8 + 8, :] = sums[group]
    products = dot(jnp.ones((8, LANES), jnp.float32), partial[...], 1, 1)
    own = jnp.sum(relayed[:, 8:16, :], axis=0)
    count = message.shape[0]
    lane, which = iota((24, LANES), 1), iota((24, LANES), 0) % 3
    values = jnp.zeros((24, LANES), jnp.float32)
    for piece in range(3):
        moved = pltpu.roll(products, 88 - 40 * piece if piece < 2 else 8, 1)[0:1]
        row = jnp.where(lane[0:1] < 88, own[4 + piece : 5 + piece], moved)
        values = jnp.where(which == piece, row, values)
    message[...] = jnp.broadcast_to(values[None], (count // 24, 24, LANES)).reshape(count, LANES)


def final_kernel(
    column_id, gathered, joined, column, coefficients, r_factor, columns_out, stacked
):
    total = joined.shape[0]
    count, rank = coefficients.shape
    _, _, _, levels, points = columns_out.shape
    rows_total = float(gathered.shape[0] // 3 * joined.shape[1])
    chosen = column_id[0]
    half = total // 2
    stacked[...] = jnp.sum(gathered[...].reshape(-1, 48, LANES), axis=0)
    pieces = [
        [stacked[pl.ds(part * 3 + piece, 8, stride=6), :] for piece in range(3)]
        for part in range(2)
    ]
    sums = [jnp.sum(pieces[0][i] + pieces[1][i], axis=0, keepdims=True) for i in range(3)]
    sums = [pltpu.roll(row, shift, 1) for row, shift in zip(sums, (40, 80, 120))]
    lane = iota((1, LANES), 1)
    sums = jnp.where(lane < 40, sums[0], jnp.where(lane < 80, sums[1], sums[2])) / rows_total
    folded = jnp.concatenate(pieces[0] + pieces[1][:2], axis=0) / rows_total
    turned = jnp.concatenate([folded, jnp.zeros((LANES - half, LANES), jnp.float32)], axis=0).T
    lane, sub = iota((half, LANES), 1), iota((half, LANES), 0)
    diagonal = jnp.broadcast_to(folded[:, total : total + 1], (half, LANES))
    upper = jnp.where((lane >= sub), folded, turned[:half])
    lower = jnp.where(lane < sub, folded, jnp.where(lane > sub, turned[:half], diagonal))
    gram = jnp.concatenate(
        [
            upper,
            jnp.where(lane < half, turned[half:total], pltpu.roll(lower, half, 1)),
        ],
        axis=0,
    )
    lane = iota((total, LANES), 1)
    down = jnp.broadcast_to(sums, (LANES, LANES)).T
    modes = gram[:rank, :rank]
    shifted = pltpu.roll(gram, LANES - rank, 1)
    first = jnp.where(lane[:rank] == chosen, down[:rank], shifted[:rank])[:, :count]
    block_lane, block_sub = iota((count, LANES), 1), iota((count, LANES), 0)
    square = jnp.broadcast_to(sums[:, total : total + 1], (1, LANES))
    across = jnp.where(
        block_lane[0:1] == chosen, square, pltpu.roll(sums, LANES - rank, 1)
    )
    block = jnp.where(block_lane == chosen, down[rank:total], shifted[rank:total])
    block = jnp.where(block_sub == chosen, jnp.broadcast_to(across, (count, LANES)), block)
    second = first - dot(modes, first, 1, 0)
    both = first + second
    third = first - dot(modes, both, 1, 0)
    square = dot(
        jnp.concatenate([first, both], axis=0), jnp.concatenate([both, third], axis=0), 0, 0
    )
    square = jnp.concatenate([square, jnp.zeros((count, LANES - count), jnp.float32)], axis=1)
    state = jnp.where(block_lane < count, block - square, 0.0)
    state = jnp.where(block_lane == block_sub + count, 1.0, state)
    for step in range(count - 1):
        row = state[step : step + 1, :]
        scale = state[:, step : step + 1] / row[:, step : step + 1]
        scale = jnp.where(block_sub > step, jnp.broadcast_to(scale, (count, LANES)), 0.0)
        state = state - scale * row
    diagonal = jnp.sum(jnp.where(block_lane == block_sub, state, 0.0), axis=1, keepdims=True)
    state = state / jnp.sqrt(diagonal)
    r_factor[...] = jnp.where(block_lane >= block_sub, state, 0.0)[:, :count]
    padded = jnp.concatenate([both, jnp.zeros((rank, LANES - count), jnp.float32)], axis=1)
    padded = jnp.concatenate([padded, jnp.zeros((LANES - rank, LANES), jnp.float32)], axis=0)
    coefficients[...] = padded.T[:count, :rank]
    inverse = pltpu.roll(state, LANES - count, 1)
    inverse = jnp.where(block_lane < count, inverse, 0.0)
    onto_modes = dot(inverse[:, :count], both, 1, 1)
    own = jnp.sum(jnp.where(block_lane == chosen, inverse, 0.0), axis=1, keepdims=True)
    onto_block = pltpu.roll(jnp.where(block_lane == chosen, 0.0, inverse), rank, 1)
    onto_modes = jnp.concatenate(
        [-onto_modes, jnp.zeros((count, LANES - rank), jnp.float32)], axis=1
    )
    weights = jnp.where(block_lane < rank, onto_modes, onto_block)[:, :total]
    for c in range(3):
        for level in range(levels):
            lanes = slice((c * levels + level) * points, (c * levels + level + 1) * points)
            columns_out[:, c, 0, level, :] = (
                dot(weights, joined[:, lanes], 1, 0) + own * column[0:1, lanes]
            )


def shifted(value, axis, step):
    count = lax.axis_size(axis)
    return lax.ppermute(value, axis, [(i, (i + step) % count) for i in range(count)])


def exchange(faces):
    x_low, x_high, y_row, z_low, z_high = faces
    return (
        shifted(x_high, "gx", 1),
        shifted(x_low, "gx", -1),
        shifted(y_row, "ga", 1),
        shifted(z_high, "gz", 1),
        shifted(z_low, "gz", -1),
    )


def on_device(fields, diffusivity, subsample_offsets, column_id, pod_basis, held_block):
    count, cells, height, width = fields.shape
    rank, columns = pod_basis.shape[0], held_block.shape[0]
    devices = 1
    for axis in AXES:
        devices *= lax.axis_size(axis)
    points = held_block.shape[-1]
    length = 3 * held_block.shape[3] * points
    faces = (
        struct(count, height, width),
        struct(count, height, width),
        struct(count, cells, width),
        struct(count, height, LANES),
        struct(count, height, LANES),
    )

    packed = pl.pallas_call(
        pack_kernel, in_specs=[VMEM], out_specs=[VMEM] * 5, out_shape=faces,
        compiler_params=params(16),
    )(fields)
    halos = exchange(packed)

    joined, folded = pl.pallas_call(
        gram_kernel, in_specs=[VMEM] * 2, out_specs=[VMEM] * 2,
        out_shape=(struct(rank + columns, length), struct(48, LANES)),
        compiler_params=params(24),
    )(pod_basis, held_block)
    first, *packed = pl.pallas_call(
        first_kernel, in_specs=[SMEM] + [VMEM] * 7, out_specs=[VMEM] * 6,
        out_shape=(struct(*fields.shape),) + faces[:2] + (struct(count, cells + 8, width),) + faces[3:],
        compiler_params=params(24),
    )(diffusivity, folded, fields, *halos)
    halos = exchange(packed)

    fields_out, snapshot = pl.pallas_call(
        second_kernel, in_specs=[SMEM] * 2 + [VMEM] * 8, out_specs=[VMEM] * 2,
        out_shape=(struct(*fields.shape), struct(LANES, LANES)),
        scratch_shapes=[pltpu.VMEM((LANES, width), jnp.float32)],
        compiler_params=params(24),
    )(diffusivity, subsample_offsets, folded, fields, first, *halos)
    relayed = lax.all_to_all(snapshot.reshape(8, 16, LANES), "gz", 0, 0, tiled=True)

    message, column = pl.pallas_call(
        product_kernel, in_specs=[VMEM] * 2, out_specs=[VMEM] * 2,
        out_shape=(struct(devices * 3, LANES), struct(8, length)),
        scratch_shapes=[pltpu.VMEM((LANES, LANES), jnp.float32)],
        compiler_params=params(16),
    )(relayed, joined)
    message = message.reshape(devices * 3, 1, LANES)
    gathered = lax.all_to_all(message, AXES, 0, 0, tiled=True).reshape(devices * 3, LANES)

    coefficients, r_factor, new_columns = pl.pallas_call(
        final_kernel, in_specs=[SMEM] + [VMEM] * 3, out_specs=[VMEM] * 3,
        out_shape=(
            struct(columns, rank), struct(columns, columns), struct(*held_block.shape)
        ),
        scratch_shapes=[pltpu.VMEM((48, LANES), jnp.float32)],
        compiler_params=params(24),
    )(column_id, gathered, joined, column)
    return fields_out, coefficients.T, r_factor, new_columns


def solution(mesh):
    placed = (
        P(None, "gx", "ga", "gz"),
        P(),
        P(),
        P(),
        P(None, None, ("gx", "gz"), "ga", None),
        P(None, None, ("gx", "gz"), "ga", None),
    )
    return jax.shard_map(
        on_device,
        mesh=mesh,
        in_specs=placed,
        out_specs=(P(None, "gx", "ga", "gz"), P(), P(), P(None, None, ("gx", "gz"), "ga", None)),
        check_vma=False,
    )
```

```python
import functools

import jax
import jax.numpy as jnp
from jax import lax
from jax.experimental import pallas as pl
from jax.experimental.pallas import tpu as pltpu
from jax.sharding import PartitionSpec as P

STRIDE = 4
LANES = 128
PACK_UNROLL = 4
BLOCK = 3

time_step = 0.1
smagorinsky = 0.02

VMEM = pl.BlockSpec(memory_space=pltpu.VMEM)
ANY = pl.BlockSpec(memory_space=pl.ANY)
SMEM = pl.BlockSpec(memory_space=pltpu.SMEM)
HIGH = lax.Precision.HIGHEST
AXES = ("zh", "x", "y", "core", "zl")


def params(mib):
    return pltpu.CompilerParams(vmem_limit_bytes=mib * 1024 * 1024)


def struct(*shape):
    return jax.ShapeDtypeStruct(shape, jnp.float32)


def iota(shape, dim):
    return lax.broadcasted_iota(jnp.int32, shape, dim)


def dot(left, right, left_dim, right_dim):
    return lax.dot_general(
        left,
        right,
        (((left_dim,), (right_dim,)), ((), ())),
        precision=HIGH,
        preferred_element_type=jnp.float32,
    )


def put_row(x, upper, top, bottom, ref, field, half):
    row = jnp.where(upper, bottom[0:1, :], top[7:8, :])
    rows = pl.ds(pl.multiple_of(x // 8 * 8, 8), 8)
    lanes = slice(half * LANES, (half + 1) * LANES)
    here = iota((8, LANES), 0) == x % 8
    ref[field, rows, lanes] = jnp.where(here, row, ref[field, rows, lanes])


def put_columns(x, lane, value, ref, field, tile, from_end):
    shift = (x + 1) % LANES if from_end else x
    rows = slice(tile * 8, tile * 8 + 8)
    ref[field, rows, :] = jnp.where(lane == x, pltpu.roll(value, shift, 1), ref[field, rows, :])


def split(value):
    high = value.astype(jnp.bfloat16)
    value = value - high.astype(jnp.float32)
    middle = value.astype(jnp.bfloat16)
    return high, middle, (value - middle.astype(jnp.float32)).astype(jnp.bfloat16)


def matmul(left, right, right_dim):
    return lax.dot_general(
        left, right, (((1,), (right_dim,)), ((), ())), preferred_element_type=jnp.float32
    )


def pack_kernel(source, x_low, x_high, y_row, z_low, z_high, fields, semaphores):
    count, cells, height, _ = fields.shape
    upper = lax.axis_index("zl") > 0
    lane = iota((8, LANES), 1)
    parts = semaphores.shape[0]
    each = cells // parts
    copies = [
        pltpu.make_async_copy(
            source.at[:, part * each : (part + 1) * each],
            fields.at[:, part * each : (part + 1) * each],
            semaphores.at[part],
        )
        for part in range(parts)
    ]
    for copy in copies:
        copy.start()
    y_row[...] = jnp.zeros_like(y_row)
    z_low[...] = jnp.zeros_like(z_low)
    z_high[...] = jnp.zeros_like(z_high)

    def body(x, carry):
        for f in range(count):
            for half in range(2):
                lanes = slice(half * LANES, (half + 1) * LANES)
                bottom = fields[f, x, 0:8, lanes]
                top = fields[f, x, height - 8 : height, lanes]
                put_row(x, upper, top, bottom, y_row, f, half)
                for tile, value in ((0, bottom), (1, top)):
                    put_columns(x, lane, value, (z_low, z_high)[half], f, tile, half == 1)
        return carry

    for part in range(parts):
        copies[part].wait()
        lax.fori_loop(part * each, (part + 1) * each, body, 0, unroll=PACK_UNROLL)
    x_low[...] = fields[:, 0]
    x_high[...] = fields[:, cells - 1]


def half_plane(x, half, current, before, after, y_halo, z_before, z_after, diffusivity, upper):
    count = current.shape[0]
    lane = iota((8, LANES), 1)
    sub = iota((8, LANES), 0)
    first_lane, last_lane = lane == 0, lane == LANES - 1
    first_sub, last_sub = sub == 0, sub == 7
    below = jnp.where(upper, 1.0, 0.0)
    above = 1.0 - below
    row_shift = (jnp.where(upper, 8, 15) - x % 8) % 8
    tile_rows = (slice(0, 8), slice(8, 16))
    lanes = slice(half * LANES, (half + 1) * LANES)
    other_lanes = slice((1 - half) * LANES, (2 - half) * LANES)
    centre = {
        (f, tile): current[f, x, tile_rows[tile], lanes] for f in range(count) for tile in range(2)
    }
    speeds = [[0.5 * centre[f, tile] for f in range(3)] for tile in range(2)]
    strain = [0.0, 0.0]
    laplace, rest = {}, {}
    for f in range(count):
        row = y_halo[f, pl.ds(pl.multiple_of(x // 8 * 8, 8), 8), lanes]
        row = pltpu.roll(row, row_shift, 0)
        down = [pltpu.roll(centre[f, tile], 1, 0) for tile in range(2)]
        up = [pltpu.roll(centre[f, tile], 7, 0) for tile in range(2)]
        y_minus = (
            jnp.where(first_sub, row * below, down[0]),
            jnp.where(first_sub, down[0], down[1]),
        )
        y_plus = (
            jnp.where(last_sub, up[1], up[0]),
            jnp.where(last_sub, row * above, up[1]),
        )
        for tile in range(2):
            rows = tile_rows[tile]
            value = centre[f, tile]
            other = current[f, x, rows, other_lanes]
            if half == 0:
                edge_low = pltpu.roll(z_before[f, rows, :], (LANES - x) % LANES, 1)
                edge_high = pltpu.roll(other, LANES - 1, 1)
            else:
                edge_low = pltpu.roll(other, 1, 1)
                edge_high = pltpu.roll(z_after[f, rows, :], LANES - 1 - x, 1)
            z_minus = jnp.where(first_lane, edge_low, pltpu.roll(value, 1, 1))
            z_plus = jnp.where(last_lane, edge_high, pltpu.roll(value, LANES - 1, 1))
            x_minus, x_plus = before(f, rows, lanes), after(f, rows, lanes)
            slope_x = x_plus - x_minus
            slope_y = y_plus[tile] - y_minus[tile]
            slope_z = z_plus - z_minus
            laplace[f, tile] = (
                (x_plus + x_minus)
                + (y_plus[tile] + y_minus[tile])
                + (z_plus + z_minus)
                - 6.0 * value
            )
            if f < 3:
                strain[tile] = strain[tile] + (
                    slope_x * slope_x + slope_y * slope_y + slope_z * slope_z
                )
            advect = (
                speeds[tile][0] * slope_x + speeds[tile][1] * slope_y + speeds[tile][2] * slope_z
            )
            rest[f, tile] = diffusivity[f] * laplace[f, tile] - advect
    rates = {}
    for tile in range(2):
        eddy = smagorinsky * jnp.sqrt(0.25 * strain[tile])
        for f in range(count):
            rates[f, tile] = eddy * laplace[f, tile] + rest[f, tile]
    return centre, rates


def planes(current, halos, diffusivity, finish, after_three, after_first=lambda: None):
    x_before, x_after, y_halo, z_before, z_after = halos
    cells = current.shape[1]
    upper = lax.axis_index("zl") > 0

    def one(x, before, after):
        for half in range(2):
            finish(
                x,
                half,
                *half_plane(
                    x, half, current, before, after, y_halo, z_before, z_after, diffusivity, upper
                ),
            )

    def inside(offset, x):
        return lambda f, rows, lanes: current[f, x + offset, rows, lanes]

    def outside(ref):
        return lambda f, rows, lanes: ref[f, rows, lanes]

    one(0, outside(x_before), inside(1, 0))
    after_first()
    blocks = (cells - 2) // BLOCK

    def body(step, carry):
        for i in range(BLOCK):
            x = step * BLOCK + 1 + i
            one(x, inside(-1, x), inside(1, x))
        after_three(step)
        return carry

    lax.fori_loop(0, blocks, body, 0)
    one(cells - 1, inside(-1, cells - 1), outside(x_after))


def first_kernel(
    diffusivity, basis, held, current, x_before, x_after, y_halo, z_before, z_after,
    first, x_low, x_high, y_row, z_low, z_high, joined, folded, sums, squares, semaphores,
):
    count, cells = current.shape[:2]
    rank, _, _, levels, points = basis.shape
    total = rank + held.shape[0]
    upper = lax.axis_index("zl") > 0
    lane = iota((8, LANES), 1)
    copies = []
    for chunk in range(3 * levels):
        lanes = slice(chunk * points, (chunk + 1) * points)
        for i, (source, rows) in enumerate(
            ((basis, slice(0, rank)), (held, slice(rank, total)))
        ):
            copies.append(
                pltpu.make_async_copy(
                    source.at[:, chunk // levels, 0, chunk % levels, :],
                    joined.at[rows, lanes],
                    semaphores.at[2 * chunk + i],
                )
            )
    for copy in copies:
        copy.start()
    y_row[...] = jnp.zeros_like(y_row)
    z_low[...] = jnp.zeros_like(z_low)
    z_high[...] = jnp.zeros_like(z_high)
    sums[...] = jnp.zeros_like(sums)
    squares[...] = jnp.zeros_like(squares)

    def finish(x, half, centre, rates):
        lanes = slice(half * LANES, (half + 1) * LANES)
        for f in range(count):
            new = []
            for tile in range(2):
                rows = slice(tile * 8, tile * 8 + 8)
                value = centre[f, tile] + time_step * rates[f, tile]
                new.append(value)
                first[f, x, rows, lanes] = value
                if isinstance(x, int):
                    (x_low if x == 0 else x_high)[f, rows, lanes] = value
                put_columns(x, lane, value, (z_low, z_high)[half], f, tile, half == 1)
            put_row(x, upper, new[1], new[0], y_row, f, half)

    def gram(chunk):
        part = joined[:, pl.ds(pl.multiple_of(chunk * points, LANES), points)]
        high, middle, low = split(part)
        sums[...] += matmul(jnp.concatenate([high, middle, low], axis=0), high, 1)
        squares[...] += matmul(middle, middle, 1)

    def arrived():
        for copy in copies:
            copy.wait()

    halos = (x_before, x_after, y_halo, z_before, z_after)
    planes(current, halos, diffusivity, finish, gram, arrived)
    for chunk in range((cells - 2) // BLOCK, 3 * levels):
        gram(chunk)
    half = total // 2
    wide = jnp.zeros((total, LANES - total), jnp.float32)
    cross = jnp.concatenate([sums[total : 2 * total] + sums[2 * total :], wide], axis=1)
    tall = jnp.concatenate([cross, jnp.zeros((LANES - total, LANES), jnp.float32)], axis=0)
    values = jnp.concatenate([sums[:total] + squares[...], wide], axis=1)
    values = values + (cross + tall.T[:total])
    lane, sub = iota((half, LANES), 1), iota((half, LANES), 0)
    lower = pltpu.roll(values[half:], LANES - half, 1)
    diagonal = jnp.sum(jnp.where(lane == sub, lower, 0.0), axis=1, keepdims=True)
    values = jnp.where(lane < sub, lower, values[:half])
    values = jnp.where(lane == total, jnp.broadcast_to(diagonal, (half, LANES)), values)
    folded[0:half, :] = jnp.where(lane <= total, values, 0.0)
    folded[half:, :] = jnp.zeros((folded.shape[0] - half, LANES), jnp.float32)
    for group in range(3):
        lanes = slice(group % 2 * LANES, (group % 2 + 1) * LANES)
        y_row[group // 2, cells:, lanes] = jnp.where(
            upper, folded[group * 8 : group * 8 + 8], folded[group * 8 + 24 : group * 8 + 32]
        )


def second_kernel(
    diffusivity, offsets, folded, start, current, x_before, x_after, y_halo, z_before, z_after,
    target, snapshot, picked, result, semaphores,
):
    count, cells, height, width = current.shape
    blocks = (cells - 2) // BLOCK

    def finish(x, half, centre, rates):
        lanes = slice(half * LANES, (half + 1) * LANES)
        for f in range(count):
            for tile in range(2):
                rows = slice(tile * 8, tile * 8 + 8)
                result[f, x, rows, lanes] = 0.5 * (
                    start[f, x, rows, lanes] + centre[f, tile] + time_step * rates[f, tile]
                )

    def copied(first, planes_count, index):
        part = pl.ds(first, planes_count)
        return pltpu.make_async_copy(result.at[:, part], target.at[:, part], semaphores.at[index])

    def send(step):
        copied(step * BLOCK + 1, BLOCK, step).start()

    planes(current, (x_before, x_after, y_halo, z_before, z_after), diffusivity, finish, send)
    copied(0, 1, blocks).start()
    copied(cells - 1, 1, blocks + 1).start()
    levels = height // STRIDE
    picked[...] = jnp.zeros_like(picked)
    for column in range(cells // STRIDE):
        for f in range(3):
            for tile in range(2):
                plane = result[f, column * STRIDE + offsets[2], tile * 8 : tile * 8 + 8, :]
                plane = pltpu.roll(plane, (8 - offsets[1]) % 8, 0)
                for part in range(2):
                    row = column * 16 + f * levels + tile * 2 + part
                    picked[row : row + 1, :] = plane[part * STRIDE : part * STRIDE + 1, :]
    points = width // STRIDE
    choose = iota((width, LANES), 0) == STRIDE * (iota((width, LANES), 1) % points) + offsets[0]
    snapshot[...] = dot(picked[...], choose.astype(jnp.float32), 1, 0)
    upper = lax.axis_index("zl") > 0
    for group in range(3):
        lanes = slice(group % 2 * LANES, (group % 2 + 1) * LANES)
        kept = jnp.where(
            upper, folded[group * 8 + 24 : group * 8 + 32], folded[group * 8 : group * 8 + 8]
        )
        kept = kept + y_halo[group // 2, cells:, lanes]
        for column in range(cells // STRIDE):
            row = column * 16 + 12 + group
            snapshot[row : row + 1, :] = kept[column : column + 1]

    def settle(step, carry):
        copied(step * BLOCK + 1, BLOCK, step).wait()
        return carry

    lax.fori_loop(0, blocks, settle, 0)
    copied(0, 1, blocks).wait()
    copied(cells - 1, 1, blocks + 1).wait()


def product_kernel(relayed, joined, message, column, partial):
    total = joined.shape[0]
    groups = total // 8
    low = iota((1, LANES), 1) < LANES // 2
    sums = [jnp.zeros((8, LANES), jnp.float32) for _ in range(groups + 1)]
    for row in range(12):
        for pair in range(4):
            tile = row * 4 + pair
            lanes = slice(tile * LANES, (tile + 1) * LANES)
            values = jnp.where(
                low,
                relayed[2 * pair, row : row + 1, :],
                relayed[2 * pair + 1, row : row + 1, :],
            )
            values = jnp.broadcast_to(values, (8, LANES))
            column[:, lanes] = values
            for group in range(groups):
                sums[group] += joined[group * 8 : group * 8 + 8, lanes] * values
            sums[groups] += values * values
    partial[...] = jnp.zeros_like(partial)
    for group in range(groups + 1):
        partial[group * 8 : group * 8 + 8, :] = sums[group]
    products = dot(jnp.ones((8, LANES), jnp.float32), partial[...], 1, 1)
    own = jnp.sum(relayed[:, 8:16, :], axis=0)
    lane, which = iota((24, LANES), 1), iota((24, LANES), 0) % 3
    values = jnp.zeros((24, LANES), jnp.float32)
    for piece in range(3):
        moved = pltpu.roll(products, 88 - 40 * piece if piece < 2 else 8, 1)[0:1]
        row = jnp.where(lane[0:1] < 88, own[4 + piece : 5 + piece], moved)
        values = jnp.where(which == piece, row, values)
    message[...] = values


def middle_kernel(received, message):
    rows = sum(received[6 * part : 6 * part + 6, :] for part in range(4))
    tile = jnp.concatenate([rows] * 4, axis=0)
    count = message.shape[0]
    message[...] = jnp.broadcast_to(tile[None], (count // 24, 24, LANES)).reshape(count, LANES)


def final_kernel(
    rows_total, column_id, gathered, joined, column,
    coefficients, r_factor, columns_out, stacked, results, semaphores,
):
    total = joined.shape[0]
    count, rank = coefficients.shape
    _, _, _, levels, points = columns_out.shape
    chosen = column_id[0]
    half = total // 2
    stacked[...] = jnp.sum(gathered[...].reshape(-1, 48, LANES), axis=0)
    pieces = [
        [stacked[pl.ds(part * 3 + piece, 8, stride=6), :] for piece in range(3)]
        for part in range(2)
    ]
    sums = [jnp.sum(pieces[0][i] + pieces[1][i], axis=0, keepdims=True) for i in range(3)]
    sums = [pltpu.roll(row, shift, 1) for row, shift in zip(sums, (40, 80, 120))]
    lane = iota((1, LANES), 1)
    sums = jnp.where(lane < 40, sums[0], jnp.where(lane < 80, sums[1], sums[2])) / rows_total
    folded = jnp.concatenate(pieces[0] + pieces[1][:2], axis=0) / rows_total
    turned = jnp.concatenate([folded, jnp.zeros((LANES - half, LANES), jnp.float32)], axis=0).T
    lane, sub = iota((half, LANES), 1), iota((half, LANES), 0)
    diagonal = jnp.broadcast_to(folded[:, total : total + 1], (half, LANES))
    upper = jnp.where((lane >= sub), folded, turned[:half])
    lower = jnp.where(lane < sub, folded, jnp.where(lane > sub, turned[:half], diagonal))
    gram = jnp.concatenate(
        [
            upper,
            jnp.where(lane < half, turned[half:total], pltpu.roll(lower, half, 1)),
        ],
        axis=0,
    )
    lane = iota((total, LANES), 1)
    down = jnp.broadcast_to(sums, (LANES, LANES)).T
    modes = gram[:rank, :rank]
    shifted = pltpu.roll(gram, LANES - rank, 1)
    first = jnp.where(lane[:rank] == chosen, down[:rank], shifted[:rank])[:, :count]
    block_lane, block_sub = iota((count, LANES), 1), iota((count, LANES), 0)
    square = jnp.broadcast_to(sums[:, total : total + 1], (1, LANES))
    across = jnp.where(
        block_lane[0:1] == chosen, square, pltpu.roll(sums, LANES - rank, 1)
    )
    block = jnp.where(block_lane == chosen, down[rank:total], shifted[rank:total])
    block = jnp.where(block_sub == chosen, jnp.broadcast_to(across, (count, LANES)), block)
    second = first - dot(modes, first, 1, 0)
    both = first + second
    third = first - dot(modes, both, 1, 0)
    square = dot(
        jnp.concatenate([first, both], axis=0), jnp.concatenate([both, third], axis=0), 0, 0
    )
    square = jnp.concatenate([square, jnp.zeros((count, LANES - count), jnp.float32)], axis=1)
    state = jnp.where(block_lane < count, block - square, 0.0)
    state = jnp.where(block_lane == block_sub + count, 1.0, state)
    for step in range(count - 1):
        row = state[step : step + 1, :]
        scale = state[:, step : step + 1] / row[:, step : step + 1]
        scale = jnp.where(block_sub > step, jnp.broadcast_to(scale, (count, LANES)), 0.0)
        state = state - scale * row
    diagonal = jnp.sum(jnp.where(block_lane == block_sub, state, 0.0), axis=1, keepdims=True)
    state = state / jnp.sqrt(diagonal)
    r_factor[...] = jnp.where(block_lane >= block_sub, state, 0.0)[:, :count]
    padded = jnp.concatenate([both, jnp.zeros((rank, LANES - count), jnp.float32)], axis=1)
    padded = jnp.concatenate([padded, jnp.zeros((LANES - rank, LANES), jnp.float32)], axis=0)
    coefficients[...] = padded.T[:count, :rank]
    inverse = pltpu.roll(state, LANES - count, 1)
    inverse = jnp.where(block_lane < count, inverse, 0.0)
    onto_modes = dot(inverse[:, :count], both, 1, 1)
    own = jnp.sum(jnp.where(block_lane == chosen, inverse, 0.0), axis=1, keepdims=True)
    onto_block = pltpu.roll(jnp.where(block_lane == chosen, 0.0, inverse), rank, 1)
    onto_modes = jnp.concatenate(
        [-onto_modes, jnp.zeros((count, LANES - rank), jnp.float32)], axis=1
    )
    weights = jnp.where(block_lane < rank, onto_modes, onto_block)[:, :total]
    weights = jnp.concatenate(split(weights), axis=0)
    copies = []
    for chunk in range(3 * levels):
        lanes = slice(chunk * points, (chunk + 1) * points)
        high, middle, low = split(joined[:, lanes])
        first = matmul(weights, high, 0)
        second = matmul(weights[: 2 * count], middle, 0)
        third = matmul(weights[:count], low, 0)
        results[chunk] = (
            (first[:count] + own * column[0:1, lanes])
            + (first[count : 2 * count] + second[:count])
            + (first[2 * count :] + second[count:] + third)
        )
        copies.append(
            pltpu.make_async_copy(
                results.at[chunk],
                columns_out.at[:, chunk // levels, 0, chunk % levels, :],
                semaphores.at[chunk],
            )
        )
        copies[-1].start()
    for copy in copies:
        copy.wait()


def shifted(value, axes, step):
    axes = axes if isinstance(axes, tuple) else (axes,)
    count = 1
    for axis in axes:
        count *= lax.axis_size(axis)
    return lax.ppermute(value, axes, [(i, (i + step) % count) for i in range(count)])


def exchange(faces):
    x_low, x_high, y_row, z_low, z_high = faces
    return (
        shifted(x_high, ("zh", "x"), 1),
        shifted(x_low, ("zh", "x"), -1),
        shifted(y_row, "zl", 1),
        shifted(z_high, ("y", "core"), 1),
        shifted(z_low, ("y", "core"), -1),
    )


def everyone(message, axes):
    rows = message.shape[0]
    message = lax.all_to_all(message.reshape(rows, 1, LANES), axes, 0, 0, tiled=True)
    return message.reshape(rows, LANES)


def on_device(fields, diffusivity, subsample_offsets, column_id, pod_basis, held_block):
    count, cells, height, width = fields.shape
    rank, columns = pod_basis.shape[0], held_block.shape[0]
    devices = 1
    for axis in AXES:
        devices *= lax.axis_size(axis)
    points = held_block.shape[-1]
    chunks = 3 * held_block.shape[3]
    length = chunks * points
    total = rank + columns
    faces = (
        struct(count, height, width),
        struct(count, height, width),
        struct(count, cells, width),
        struct(count, height, LANES),
        struct(count, height, LANES),
    )
    block_space = pltpu.VMEM(fields.shape, jnp.float32)

    packed = pl.pallas_call(
        pack_kernel, in_specs=[ANY], out_specs=[VMEM] * 5, out_shape=faces,
        scratch_shapes=[block_space, pltpu.SemaphoreType.DMA((4,))],
        compiler_params=params(16),
    )(fields)
    halos = exchange(packed)

    first, *packed, joined, folded = pl.pallas_call(
        first_kernel, in_specs=[SMEM] + [ANY] * 2 + [VMEM] * 6, out_specs=[VMEM] * 8,
        out_shape=(struct(*fields.shape),) + faces[:2] + (struct(count, cells + 8, width),)
        + faces[3:] + (struct(total, length), struct(48, LANES)),
        scratch_shapes=[
            pltpu.VMEM((3 * total, total), jnp.float32),
            pltpu.VMEM((total, total), jnp.float32),
            pltpu.SemaphoreType.DMA((2 * chunks,)),
        ],
        compiler_params=params(24),
    )(diffusivity, pod_basis, held_block, fields, *halos)
    halos = exchange(packed)

    fields_out, snapshot = pl.pallas_call(
        second_kernel, in_specs=[SMEM] * 2 + [VMEM] * 8, out_specs=[ANY, VMEM],
        out_shape=(struct(*fields.shape), struct(LANES, LANES)),
        scratch_shapes=[
            pltpu.VMEM((LANES, width), jnp.float32), block_space, pltpu.SemaphoreType.DMA((12,)),
        ],
        compiler_params=params(24),
    )(diffusivity, subsample_offsets, folded, fields, first, *halos)
    relayed = lax.all_to_all(snapshot.reshape(8, 16, LANES), ("y", "core"), 0, 0, tiled=True)

    message, column = pl.pallas_call(
        product_kernel, in_specs=[VMEM] * 2, out_specs=[VMEM] * 2,
        out_shape=(struct(24, LANES), struct(8, length)),
        scratch_shapes=[pltpu.VMEM((LANES, LANES), jnp.float32)],
        compiler_params=params(16),
    )(relayed, joined)
    message = pl.pallas_call(
        middle_kernel, in_specs=[VMEM], out_specs=VMEM, out_shape=struct(192, LANES),
        compiler_params=params(4),
    )(everyone(message, ("zh", "zl")))
    gathered = everyone(message, ("x", "y", "core"))

    coefficients, r_factor, new_columns = pl.pallas_call(
        functools.partial(final_kernel, float(devices * length)),
        in_specs=[SMEM] + [VMEM] * 3, out_specs=[VMEM] * 2 + [ANY],
        out_shape=(
            struct(columns, rank), struct(columns, columns), struct(*held_block.shape)
        ),
        scratch_shapes=[
            pltpu.VMEM((48, LANES), jnp.float32),
            pltpu.VMEM((chunks, columns, points), jnp.float32),
            pltpu.SemaphoreType.DMA((chunks,)),
        ],
        compiler_params=params(24),
    )(column_id, gathered, joined, column)
    return fields_out, coefficients.T, r_factor, new_columns


def solution(mesh):
    mesh = jax.sharding.Mesh(mesh.devices.reshape(4, 4, 4, 2, 2), AXES)
    block = P(None, ("zh", "x"), "zl", ("y", "core"))
    rows = P(None, None, ("zh", "x", "y", "core"), "zl", None)
    return jax.shard_map(
        on_device,
        mesh=mesh,
        in_specs=(block, P(), P(), P(), rows, rows),
        out_specs=(block, P(), P(), rows),
        check_vma=False,
    )
```

```python
import functools
import itertools

import jax
import jax.numpy as jnp
from jax import lax
from jax.experimental import pallas as pl
from jax.experimental.pallas import tpu as pltpu
from jax.sharding import PartitionSpec as P

STRIDE = 4
LANES = 128
PACK_UNROLL = 4
BLOCK = 3

time_step = 0.1
smagorinsky = 0.02

VMEM = pl.BlockSpec(memory_space=pltpu.VMEM)
ANY = pl.BlockSpec(memory_space=pl.ANY)
SMEM = pl.BlockSpec(memory_space=pltpu.SMEM)
HIGH = lax.Precision.HIGHEST
AXES = ("zh", "x", "y", "core", "zl")


def params(mib):
    return pltpu.CompilerParams(vmem_limit_bytes=mib * 1024 * 1024)


def struct(*shape):
    return jax.ShapeDtypeStruct(shape, jnp.float32)


def iota(shape, dim):
    return lax.broadcasted_iota(jnp.int32, shape, dim)


def dot(left, right, left_dim, right_dim):
    return lax.dot_general(
        left,
        right,
        (((left_dim,), (right_dim,)), ((), ())),
        precision=HIGH,
        preferred_element_type=jnp.float32,
    )


def put_row(x, upper, top, bottom, ref, field, half):
    row = jnp.where(upper, bottom[0:1, :], top[7:8, :])
    rows = pl.ds(pl.multiple_of(x // 8 * 8, 8), 8)
    lanes = slice(half * LANES, (half + 1) * LANES)
    here = iota((8, LANES), 0) == x % 8
    ref[field, rows, lanes] = jnp.where(here, row, ref[field, rows, lanes])


def put_columns(x, lane, value, ref, field, tile, from_end):
    shift = (x + 1) % LANES if from_end else x
    rows = slice(tile * 8, tile * 8 + 8)
    ref[field, rows, :] = jnp.where(lane == x, pltpu.roll(value, shift, 1), ref[field, rows, :])


def split(value):
    high = value.astype(jnp.bfloat16)
    value = value - high.astype(jnp.float32)
    middle = value.astype(jnp.bfloat16)
    return high, middle, (value - middle.astype(jnp.float32)).astype(jnp.bfloat16)


def matmul(left, right, right_dim):
    return lax.dot_general(
        left, right, (((1,), (right_dim,)), ((), ())), preferred_element_type=jnp.float32
    )


def odd(axis):
    return lax.rem(lax.axis_index(axis), 2) > 0


def arrange(x_low, x_high, z_low, z_high, x_pair, x_next, z_pair, z_next):
    x_odd, second = odd("x"), odd("core")
    x_pair[...] = jnp.where(x_odd, x_low, x_high)
    x_next[...] = jnp.where(x_odd, x_high, x_low)
    z_pair[...] = jnp.where(second, z_low, z_high)
    z_next[...] = jnp.where(second, z_high, z_low)


def pack_kernel(fields, x_pair, x_next, y_row, z_pair, z_next, z_low, z_high):
    count, cells, height, _ = fields.shape
    upper = lax.axis_index("zl") > 0
    lane = iota((8, LANES), 1)
    y_row[...] = jnp.zeros_like(y_row)
    z_low[...] = jnp.zeros_like(z_low)
    z_high[...] = jnp.zeros_like(z_high)

    def body(x, carry):
        for f in range(count):
            for half in range(2):
                lanes = slice(half * LANES, (half + 1) * LANES)
                bottom = fields[f, x, 0:8, lanes]
                top = fields[f, x, height - 8 : height, lanes]
                put_row(x, upper, top, bottom, y_row, f, half)
                for tile, value in ((0, bottom), (1, top)):
                    put_columns(x, lane, value, (z_low, z_high)[half], f, tile, half == 1)
        return carry

    lax.fori_loop(0, cells, body, 0, unroll=PACK_UNROLL)
    arrange(
        fields[:, 0], fields[:, cells - 1], z_low[...], z_high[...],
        x_pair, x_next, z_pair, z_next,
    )


def half_plane(x, half, current, before, after, y_halo, z_before, z_after, diffusivity, upper):
    count = current.shape[0]
    lane = iota((8, LANES), 1)
    sub = iota((8, LANES), 0)
    first_lane, last_lane = lane == 0, lane == LANES - 1
    first_sub, last_sub = sub == 0, sub == 7
    below = jnp.where(upper, 1.0, 0.0)
    above = 1.0 - below
    row_shift = (jnp.where(upper, 8, 15) - x % 8) % 8
    tile_rows = (slice(0, 8), slice(8, 16))
    lanes = slice(half * LANES, (half + 1) * LANES)
    other_lanes = slice((1 - half) * LANES, (2 - half) * LANES)
    centre = {
        (f, tile): current[f, x, tile_rows[tile], lanes] for f in range(count) for tile in range(2)
    }
    speeds = [[0.5 * centre[f, tile] for f in range(3)] for tile in range(2)]
    strain = [0.0, 0.0]
    laplace, rest = {}, {}
    for f in range(count):
        row = y_halo[f, pl.ds(pl.multiple_of(x // 8 * 8, 8), 8), lanes]
        row = pltpu.roll(row, row_shift, 0)
        down = [pltpu.roll(centre[f, tile], 1, 0) for tile in range(2)]
        up = [pltpu.roll(centre[f, tile], 7, 0) for tile in range(2)]
        y_minus = (
            jnp.where(first_sub, row * below, down[0]),
            jnp.where(first_sub, down[0], down[1]),
        )
        y_plus = (
            jnp.where(last_sub, up[1], up[0]),
            jnp.where(last_sub, row * above, up[1]),
        )
        for tile in range(2):
            rows = tile_rows[tile]
            value = centre[f, tile]
            other = current[f, x, rows, other_lanes]
            if half == 0:
                edge_low = pltpu.roll(z_before[f, rows, :], (LANES - x) % LANES, 1)
                edge_high = pltpu.roll(other, LANES - 1, 1)
            else:
                edge_low = pltpu.roll(other, 1, 1)
                edge_high = pltpu.roll(z_after[f, rows, :], LANES - 1 - x, 1)
            z_minus = jnp.where(first_lane, edge_low, pltpu.roll(value, 1, 1))
            z_plus = jnp.where(last_lane, edge_high, pltpu.roll(value, LANES - 1, 1))
            x_minus, x_plus = before(f, rows, lanes), after(f, rows, lanes)
            slope_x = x_plus - x_minus
            slope_y = y_plus[tile] - y_minus[tile]
            slope_z = z_plus - z_minus
            laplace[f, tile] = (
                (x_plus + x_minus)
                + (y_plus[tile] + y_minus[tile])
                + (z_plus + z_minus)
                - 6.0 * value
            )
            if f < 3:
                strain[tile] = strain[tile] + (
                    slope_x * slope_x + slope_y * slope_y + slope_z * slope_z
                )
            advect = (
                speeds[tile][0] * slope_x + speeds[tile][1] * slope_y + speeds[tile][2] * slope_z
            )
            rest[f, tile] = diffusivity[f] * laplace[f, tile] - advect
    rates = {}
    for tile in range(2):
        eddy = smagorinsky * jnp.sqrt(0.25 * strain[tile])
        for f in range(count):
            rates[f, tile] = eddy * laplace[f, tile] + rest[f, tile]
    return centre, rates


def planes(current, halos, diffusivity, finish, after_three=lambda step: None):
    x_pair, x_next, y_halo, z_pair, z_next, z_before, z_after = halos
    cells = current.shape[1]
    upper = lax.axis_index("zl") > 0
    x_odd, second = odd("x"), odd("core")
    z_before[...] = jnp.where(second, z_pair[...], z_next[...])
    z_after[...] = jnp.where(second, z_next[...], z_pair[...])

    def one(x, before, after):
        for half in range(2):
            finish(
                x,
                half,
                *half_plane(
                    x, half, current, before, after, y_halo, z_before, z_after, diffusivity, upper
                ),
            )

    def inside(offset, x):
        return lambda f, rows, lanes: current[f, x + offset, rows, lanes]

    def outside(here, there):
        return lambda f, rows, lanes: jnp.where(x_odd, here[f, rows, lanes], there[f, rows, lanes])

    one(0, outside(x_pair, x_next), inside(1, 0))
    blocks = (cells - 2) // BLOCK

    def body(step, carry):
        for i in range(BLOCK):
            x = step * BLOCK + 1 + i
            one(x, inside(-1, x), inside(1, x))
        after_three(step)
        return carry

    lax.fori_loop(0, blocks, body, 0)
    one(cells - 1, inside(-1, cells - 1), outside(x_next, x_pair))


def gram_kernel(basis, held, joined, folded, semaphores):
    rank, _, _, levels, points = basis.shape
    total = rank + held.shape[0]
    copies = []
    for chunk in range(3 * levels):
        lanes = slice(chunk * points, (chunk + 1) * points)
        for i, (source, rows) in enumerate(
            ((basis, slice(0, rank)), (held, slice(rank, total)))
        ):
            copies.append(
                pltpu.make_async_copy(
                    source.at[:, chunk // levels, 0, chunk % levels, :],
                    joined.at[rows, lanes],
                    semaphores.at[2 * chunk + i],
                )
            )
    for copy in copies:
        copy.start()
    sums = jnp.zeros((3 * total, total), jnp.float32)
    squares = jnp.zeros((total, total), jnp.float32)
    for chunk in range(3 * levels):
        copies[2 * chunk].wait()
        copies[2 * chunk + 1].wait()
        high, middle, low = split(joined[:, chunk * points : (chunk + 1) * points])
        sums += matmul(jnp.concatenate([high, middle, low], axis=0), high, 1)
        squares += matmul(middle, middle, 1)
    half = total // 2
    wide = jnp.zeros((total, LANES - total), jnp.float32)
    cross = jnp.concatenate([sums[total : 2 * total] + sums[2 * total :], wide], axis=1)
    tall = jnp.concatenate([cross, jnp.zeros((LANES - total, LANES), jnp.float32)], axis=0)
    values = jnp.concatenate([sums[:total] + squares, wide], axis=1)
    values = values + (cross + tall.T[:total])
    lane, sub = iota((half, LANES), 1), iota((half, LANES), 0)
    lower = pltpu.roll(values[half:], LANES - half, 1)
    diagonal = jnp.sum(jnp.where(lane == sub, lower, 0.0), axis=1, keepdims=True)
    values = jnp.where(lane < sub, lower, values[:half])
    values = jnp.where(lane == total, jnp.broadcast_to(diagonal, (half, LANES)), values)
    folded[0:half, :] = jnp.where(lane <= total, values, 0.0)
    folded[half:, :] = jnp.zeros((folded.shape[0] - half, LANES), jnp.float32)


def first_kernel(
    diffusivity, folded, current, x_pair_in, x_next_in, y_halo, z_pair_in, z_next_in,
    first, x_pair, x_next, y_row, z_pair, z_next, z_before, z_after, z_low, z_high,
):
    count, cells = current.shape[:2]
    upper = lax.axis_index("zl") > 0
    lane = iota((8, LANES), 1)
    y_row[...] = jnp.zeros_like(y_row)
    z_low[...] = jnp.zeros_like(z_low)
    z_high[...] = jnp.zeros_like(z_high)
    for group in range(3):
        lanes = slice(group % 2 * LANES, (group % 2 + 1) * LANES)
        y_row[group // 2, cells:, lanes] = jnp.where(
            upper, folded[group * 8 : group * 8 + 8], folded[group * 8 + 24 : group * 8 + 32]
        )

    def finish(x, half, centre, rates):
        lanes = slice(half * LANES, (half + 1) * LANES)
        for f in range(count):
            new = []
            for tile in range(2):
                value = centre[f, tile] + time_step * rates[f, tile]
                new.append(value)
                first[f, x, tile * 8 : tile * 8 + 8, lanes] = value
                put_columns(x, lane, value, (z_low, z_high)[half], f, tile, half == 1)
            put_row(x, upper, new[1], new[0], y_row, f, half)

    halos = (x_pair_in, x_next_in, y_halo, z_pair_in, z_next_in, z_before, z_after)
    planes(current, halos, diffusivity, finish)
    arrange(
        first[:, 0], first[:, cells - 1], z_low[...], z_high[...],
        x_pair, x_next, z_pair, z_next,
    )


def second_kernel(
    diffusivity, offsets, folded, start, current, x_pair, x_next, y_halo, z_pair, z_next,
    target, snapshot, z_before, z_after, picked, result, semaphores,
):
    count, cells, height, width = current.shape
    blocks = (cells - 2) // BLOCK

    def finish(x, half, centre, rates):
        lanes = slice(half * LANES, (half + 1) * LANES)
        for f in range(count):
            for tile in range(2):
                rows = slice(tile * 8, tile * 8 + 8)
                result[f, x, rows, lanes] = 0.5 * (
                    start[f, x, rows, lanes] + centre[f, tile] + time_step * rates[f, tile]
                )

    def copied(first, planes_count, index):
        part = pl.ds(first, planes_count)
        return pltpu.make_async_copy(result.at[:, part], target.at[:, part], semaphores.at[index])

    def send(step):
        copied(step * BLOCK + 1, BLOCK, step).start()

    halos = (x_pair, x_next, y_halo, z_pair, z_next, z_before, z_after)
    planes(current, halos, diffusivity, finish, send)
    copied(0, 1, blocks).start()
    copied(cells - 1, 1, blocks + 1).start()
    levels = height // STRIDE
    picked[...] = jnp.zeros_like(picked)
    for column in range(cells // STRIDE):
        for f in range(3):
            for tile in range(2):
                plane = result[f, column * STRIDE + offsets[2], tile * 8 : tile * 8 + 8, :]
                plane = pltpu.roll(plane, (8 - offsets[1]) % 8, 0)
                for part in range(2):
                    row = column * 16 + f * levels + tile * 2 + part
                    picked[row : row + 1, :] = plane[part * STRIDE : part * STRIDE + 1, :]
    points = width // STRIDE
    choose = iota((width, LANES), 0) == STRIDE * (iota((width, LANES), 1) % points) + offsets[0]
    snapshot[...] = dot(picked[...], choose.astype(jnp.float32), 1, 0)
    upper = lax.axis_index("zl") > 0
    for group in range(3):
        lanes = slice(group % 2 * LANES, (group % 2 + 1) * LANES)
        kept = jnp.where(
            upper, folded[group * 8 + 24 : group * 8 + 32], folded[group * 8 : group * 8 + 8]
        )
        kept = kept + y_halo[group // 2, cells:, lanes]
        for column in range(cells // STRIDE):
            row = column * 16 + 12 + group
            snapshot[row : row + 1, :] = kept[column : column + 1]

    def settle(step, carry):
        copied(step * BLOCK + 1, BLOCK, step).wait()
        return carry

    lax.fori_loop(0, blocks, settle, 0)
    copied(0, 1, blocks).wait()
    copied(cells - 1, 1, blocks + 1).wait()


def product_kernel(relayed, joined, message, column, partial):
    total = joined.shape[0]
    groups = total // 8
    low = iota((1, LANES), 1) < LANES // 2
    sums = [jnp.zeros((8, LANES), jnp.float32) for _ in range(groups + 1)]
    for row in range(12):
        for pair in range(4):
            tile = row * 4 + pair
            lanes = slice(tile * LANES, (tile + 1) * LANES)
            values = jnp.where(
                low,
                relayed[2 * pair, row : row + 1, :],
                relayed[2 * pair + 1, row : row + 1, :],
            )
            values = jnp.broadcast_to(values, (8, LANES))
            column[:, lanes] = values
            for group in range(groups):
                sums[group] += joined[group * 8 : group * 8 + 8, lanes] * values
            sums[groups] += values * values
    partial[...] = jnp.zeros_like(partial)
    for group in range(groups + 1):
        partial[group * 8 : group * 8 + 8, :] = sums[group]
    products = dot(jnp.ones((8, LANES), jnp.float32), partial[...], 1, 1)
    own = jnp.sum(relayed[:, 8:16, :], axis=0)
    lane, which = iota((24, LANES), 1), iota((24, LANES), 0) % 3
    values = jnp.zeros((24, LANES), jnp.float32)
    for piece in range(3):
        moved = pltpu.roll(products, 88 - 40 * piece if piece < 2 else 8, 1)[0:1]
        row = jnp.where(lane[0:1] < 88, own[4 + piece : 5 + piece], moved)
        values = jnp.where(which == piece, row, values)
    count = message.shape[0]
    message[...] = jnp.broadcast_to(values[None], (count // 24, 24, LANES)).reshape(count, LANES)


def middle_kernel(received, message):
    rows = jnp.sum(received[...].reshape(-1, 24, LANES), axis=0)
    count = message.shape[0]
    message[...] = jnp.broadcast_to(rows[None], (count // 24, 24, LANES)).reshape(count, LANES)


def final_kernel(
    rows_total, column_id, gathered, joined, column,
    coefficients, r_factor, columns_out, stacked,
):
    total = joined.shape[0]
    count, rank = coefficients.shape
    _, _, _, levels, points = columns_out.shape
    chosen = column_id[0]
    half = total // 2
    stacked[...] = jnp.sum(gathered[...].reshape(-1, 48, LANES), axis=0)
    pieces = [
        [stacked[pl.ds(part * 24 + piece, 8, stride=3), :] for piece in range(3)]
        for part in range(2)
    ]
    sums = [jnp.sum(pieces[0][i] + pieces[1][i], axis=0, keepdims=True) for i in range(3)]
    sums = [pltpu.roll(row, shift, 1) for row, shift in zip(sums, (40, 80, 120))]
    lane = iota((1, LANES), 1)
    sums = jnp.where(lane < 40, sums[0], jnp.where(lane < 80, sums[1], sums[2])) / rows_total
    folded = jnp.concatenate(pieces[0] + pieces[1][:2], axis=0) / rows_total
    turned = jnp.concatenate([folded, jnp.zeros((LANES - half, LANES), jnp.float32)], axis=0).T
    lane, sub = iota((half, LANES), 1), iota((half, LANES), 0)
    diagonal = jnp.broadcast_to(folded[:, total : total + 1], (half, LANES))
    upper = jnp.where((lane >= sub), folded, turned[:half])
    lower = jnp.where(lane < sub, folded, jnp.where(lane > sub, turned[:half], diagonal))
    gram = jnp.concatenate(
        [
            upper,
            jnp.where(lane < half, turned[half:total], pltpu.roll(lower, half, 1)),
        ],
        axis=0,
    )
    lane = iota((total, LANES), 1)
    down = jnp.broadcast_to(sums, (LANES, LANES)).T
    modes = gram[:rank, :rank]
    shifted = pltpu.roll(gram, LANES - rank, 1)
    first = jnp.where(lane[:rank] == chosen, down[:rank], shifted[:rank])[:, :count]
    block_lane, block_sub = iota((count, LANES), 1), iota((count, LANES), 0)
    square = jnp.broadcast_to(sums[:, total : total + 1], (1, LANES))
    across = jnp.where(
        block_lane[0:1] == chosen, square, pltpu.roll(sums, LANES - rank, 1)
    )
    block = jnp.where(block_lane == chosen, down[rank:total], shifted[rank:total])
    block = jnp.where(block_sub == chosen, jnp.broadcast_to(across, (count, LANES)), block)
    second = first - dot(modes, first, 1, 0)
    both = first + second
    third = first - dot(modes, both, 1, 0)
    square = dot(
        jnp.concatenate([first, both], axis=0), jnp.concatenate([both, third], axis=0), 0, 0
    )
    square = jnp.concatenate([square, jnp.zeros((count, LANES - count), jnp.float32)], axis=1)
    state = jnp.where(block_lane < count, block - square, 0.0)
    state = jnp.where(block_lane == block_sub + count, 1.0, state)
    for step in range(count - 1):
        row = state[step : step + 1, :]
        scale = state[:, step : step + 1] / row[:, step : step + 1]
        scale = jnp.where(block_sub > step, jnp.broadcast_to(scale, (count, LANES)), 0.0)
        state = state - scale * row
    diagonal = jnp.sum(jnp.where(block_lane == block_sub, state, 0.0), axis=1, keepdims=True)
    state = state / jnp.sqrt(diagonal)
    r_factor[...] = jnp.where(block_lane >= block_sub, state, 0.0)[:, :count]
    padded = jnp.concatenate([both, jnp.zeros((rank, LANES - count), jnp.float32)], axis=1)
    padded = jnp.concatenate([padded, jnp.zeros((LANES - rank, LANES), jnp.float32)], axis=0)
    coefficients[...] = padded.T[:count, :rank]
    inverse = pltpu.roll(state, LANES - count, 1)
    inverse = jnp.where(block_lane < count, inverse, 0.0)
    onto_modes = dot(inverse[:, :count], both, 1, 1)
    own = jnp.sum(jnp.where(block_lane == chosen, inverse, 0.0), axis=1, keepdims=True)
    onto_block = pltpu.roll(jnp.where(block_lane == chosen, 0.0, inverse), rank, 1)
    onto_modes = jnp.concatenate(
        [-onto_modes, jnp.zeros((count, LANES - rank), jnp.float32)], axis=1
    )
    weights = jnp.where(block_lane < rank, onto_modes, onto_block)[:, :total]
    weights = jnp.concatenate(split(weights), axis=0)
    for chunk in range(3 * levels):
        lanes = slice(chunk * points, (chunk + 1) * points)
        high, middle, low = split(joined[:, lanes])
        first = matmul(weights, high, 0)
        second = matmul(weights[: 2 * count], middle, 0)
        third = matmul(weights[:count], low, 0)
        columns_out[:, chunk // levels, 0, chunk % levels, :] = (
            (first[:count] + own * column[0:1, lanes])
            + (first[count : 2 * count] + second[:count])
            + (first[2 * count :] + second[count:] + third)
        )


def moved(value, axes, target):
    sizes = [lax.axis_size(axis) for axis in axes]
    places = list(itertools.product(*(range(size) for size in sizes)))
    flat = {place: i for i, place in enumerate(places)}
    pairs = [
        (flat[place], flat[tuple(i % size for i, size in zip(target(*place), sizes))])
        for place in places
    ]
    return lax.ppermute(value, axes, pairs)


def exchange(faces):
    x_pair, x_next, y_row, z_pair, z_next = faces

    def along(zh, x):
        step = x + 1 if x % 2 else x - 1
        return zh + step // 4, step

    def swap(core):
        return (core ^ 1,)

    z_next = moved(z_next, ("y", "core"), lambda y, core: (y + 2 * core - 1, core))
    return (
        moved(x_pair, ("x",), lambda x: (x ^ 1,)),
        moved(x_next, ("zh", "x"), along),
        moved(y_row, ("zl",), lambda zl: (zl + 1,)),
        moved(z_pair, ("core",), swap),
        moved(z_next, ("core",), swap),
    )


def everyone(message, axes):
    rows = message.shape[0]
    message = lax.all_to_all(message.reshape(rows, 1, LANES), axes, 0, 0, tiled=True)
    return message.reshape(rows, LANES)


def on_device(fields, diffusivity, subsample_offsets, column_id, pod_basis, held_block):
    count, cells, height, width = fields.shape
    rank, columns = pod_basis.shape[0], held_block.shape[0]
    devices = 1
    for axis in AXES:
        devices *= lax.axis_size(axis)
    points = held_block.shape[-1]
    chunks = 3 * held_block.shape[3]
    length = chunks * points
    total = rank + columns
    faces = (
        struct(count, height, width),
        struct(count, height, width),
        struct(count, cells, width),
        struct(count, height, LANES),
        struct(count, height, LANES),
    )
    edge = pltpu.VMEM((count, height, LANES), jnp.float32)

    packed = pl.pallas_call(
        pack_kernel, in_specs=[VMEM], out_specs=[VMEM] * 5, out_shape=faces,
        scratch_shapes=[edge] * 2, compiler_params=params(16),
    )(fields)
    halos = exchange(packed)

    joined, folded = pl.pallas_call(
        gram_kernel, in_specs=[ANY] * 2, out_specs=[VMEM] * 2,
        out_shape=(struct(total, length), struct(48, LANES)),
        scratch_shapes=[pltpu.SemaphoreType.DMA((2 * chunks,))],
        compiler_params=params(16),
    )(pod_basis, held_block)

    first, *packed = pl.pallas_call(
        first_kernel, in_specs=[SMEM] + [VMEM] * 7, out_specs=[VMEM] * 6,
        out_shape=(struct(*fields.shape),) + faces[:2] + (struct(count, cells + 8, width),)
        + faces[3:],
        scratch_shapes=[edge] * 4, compiler_params=params(24),
    )(diffusivity, folded, fields, *halos)
    halos = exchange(packed)

    fields_out, snapshot = pl.pallas_call(
        second_kernel, in_specs=[SMEM] * 2 + [VMEM] * 8, out_specs=[ANY, VMEM],
        out_shape=(struct(*fields.shape), struct(LANES, LANES)),
        scratch_shapes=[
            edge, edge, pltpu.VMEM((LANES, width), jnp.float32),
            pltpu.VMEM(fields.shape, jnp.float32), pltpu.SemaphoreType.DMA((12,)),
        ],
        compiler_params=params(24),
    )(diffusivity, subsample_offsets, folded, fields, first, *halos)
    relayed = lax.all_to_all(snapshot.reshape(8, 16, LANES), ("y", "core"), 0, 0, tiled=True)

    message, column = pl.pallas_call(
        product_kernel, in_specs=[VMEM] * 2, out_specs=[VMEM] * 2,
        out_shape=(struct(96, LANES), struct(8, length)),
        scratch_shapes=[pltpu.VMEM((LANES, LANES), jnp.float32)],
        compiler_params=params(16),
    )(relayed, joined)
    message = pl.pallas_call(
        middle_kernel, in_specs=[VMEM], out_specs=VMEM, out_shape=struct(192, LANES),
        compiler_params=params(4),
    )(everyone(message, ("x", "y", "core")))
    gathered = everyone(message, ("zh", "zl"))

    coefficients, r_factor, new_columns = pl.pallas_call(
        functools.partial(final_kernel, float(devices * length)),
        in_specs=[SMEM] + [VMEM] * 3, out_specs=[VMEM] * 3,
        out_shape=(
            struct(columns, rank), struct(columns, columns), struct(*held_block.shape)
        ),
        scratch_shapes=[
            pltpu.VMEM((48, LANES), jnp.float32),
        ],
        compiler_params=params(24),
    )(column_id, gathered, joined, column)
    return fields_out, coefficients.T, r_factor, new_columns


def solution(mesh):
    mesh = jax.sharding.Mesh(mesh.devices.reshape(4, 4, 4, 2, 2), AXES)
    block = P(None, ("zh", "x"), "zl", ("y", "core"))
    rows = P(None, None, ("zh", "x", "y", "core"), "zl", None)
    return jax.shard_map(
        on_device,
        mesh=mesh,
        in_specs=(block, P(), P(), P(), rows, rows),
        out_specs=(block, P(), P(), rows),
        check_vma=False,
    )
```

```python
import functools
import itertools

import jax
import jax.numpy as jnp
from jax import lax
from jax.experimental import pallas as pl
from jax.experimental.pallas import tpu as pltpu
from jax.sharding import PartitionSpec as P

STRIDE = 4
LANES = 128
BLOCK = 3

time_step = 0.1
smagorinsky = 0.02

VMEM = pl.BlockSpec(memory_space=pltpu.VMEM)
ANY = pl.BlockSpec(memory_space=pl.ANY)
SMEM = pl.BlockSpec(memory_space=pltpu.SMEM)
HIGH = lax.Precision.HIGHEST
AXES = ("zh", "x", "y", "core", "zl")


def params(mib):
    return pltpu.CompilerParams(vmem_limit_bytes=mib * 1024 * 1024)


def struct(*shape):
    return jax.ShapeDtypeStruct(shape, jnp.float32)


def iota(shape, dim):
    return lax.broadcasted_iota(jnp.int32, shape, dim)


def dot(left, right, left_dim, right_dim):
    return lax.dot_general(
        left,
        right,
        (((left_dim,), (right_dim,)), ((), ())),
        precision=HIGH,
        preferred_element_type=jnp.float32,
    )


def split(value):
    high = value.astype(jnp.bfloat16)
    value = value - high.astype(jnp.float32)
    middle = value.astype(jnp.bfloat16)
    return high, middle, (value - middle.astype(jnp.float32)).astype(jnp.bfloat16)


def matmul(left, right, right_dim):
    return lax.dot_general(
        left, right, (((1,), (right_dim,)), ((), ())), preferred_element_type=jnp.float32
    )


def odd(axis):
    return lax.rem(lax.axis_index(axis), 2) > 0


def pack(fields, rows, x_pair, x_next, y_row, z_pair, z_next):
    count, cells, height, _ = fields.shape
    upper = lax.axis_index("zl") > 0
    lane, sub = iota((8, LANES), 1), iota((8, LANES), 0)
    keys = [(f, half, tile) for f in range(count) for half in range(2) for tile in range(2)]

    def body(group, faces):
        faces = dict(zip(keys, faces))
        y_rows = {}
        for i in range(8):
            x = group * 8 + i
            for f in range(count):
                for half in range(2):
                    lanes = slice(half * LANES, (half + 1) * LANES)
                    values = (fields[f, x, 0:8, lanes], fields[f, x, height - 8 : height, lanes])
                    row = pltpu.roll(jnp.where(upper, values[0], values[1]), rows[i], 0)
                    y_rows[f, half] = row if i == 0 else jnp.where(sub == i, row, y_rows[f, half])
                    shift = (x + half) % LANES
                    for tile in range(2):
                        face = pltpu.roll(values[tile], shift, 1)
                        faces[f, half, tile] = jnp.where(lane == x, face, faces[f, half, tile])
        for f in range(count):
            for half in range(2):
                place = pl.ds(pl.multiple_of(group * 8, 8), 8)
                y_row[f, place, half * LANES : (half + 1) * LANES] = y_rows[f, half]
        return tuple(faces[key] for key in keys)

    zero = jnp.zeros((8, LANES), jnp.float32)
    faces = lax.fori_loop(0, cells // 8, body, tuple(zero for _ in keys))
    x_odd, second = odd("x"), odd("core")
    for (f, half, tile), face in zip(keys, faces):
        if half == 0:
            other = faces[keys.index((f, 1, tile))]
            place = slice(tile * 8, tile * 8 + 8)
            z_pair[f, place, :] = jnp.where(second, face, other)
            z_next[f, place, :] = jnp.where(second, other, face)
    low, high = fields[:, 0], fields[:, cells - 1]
    x_pair[...] = jnp.where(x_odd, low, high)
    x_next[...] = jnp.where(x_odd, high, low)


def row_shifts(upper):
    return [(i + jnp.where(upper, 0, 1)) % 8 for i in range(8)]


def pack_kernel(fields, x_pair, x_next, y_row, z_pair, z_next):
    rows = row_shifts(lax.axis_index("zl") > 0)
    pack(fields, rows, x_pair, x_next, y_row, z_pair, z_next)


def plane(x, current, before, after, y_low, y_high, z_before, z_after, diffusivity):
    count = current.shape[0]
    lane, sub = iota((8, LANES), 1), iota((8, LANES), 0)
    first_lane, last_lane = lane == 0, lane == LANES - 1
    first_sub, last_sub = sub == 0, sub == 7
    tile_rows = (slice(0, 8), slice(8, 16))
    half_lanes = (slice(0, LANES), slice(LANES, 2 * LANES))
    quarters = [(tile, half) for tile in range(2) for half in range(2)]
    group = pl.ds(pl.multiple_of(x // 8 * 8, 8), 8)
    to_first, to_last = (8 - x % 8) % 8, 7 - x % 8
    centre = {
        (f, tile, half): current[f, x, tile_rows[tile], half_lanes[half]]
        for f in range(count)
        for tile, half in quarters
    }
    speeds = {
        (f, *at): (0.5 * time_step) * centre[f, *at] for f in range(3) for at in quarters
    }
    strain = dict.fromkeys(quarters, 0.0)
    laplace, advect = {}, {}
    for f in range(count):
        y_minus, y_plus, z_minus, z_plus = {}, {}, {}, {}
        for half in range(2):
            lanes = half_lanes[half]
            low = pltpu.roll(y_low[f, group, lanes], to_first, 0)
            high = pltpu.roll(y_high[f, group, lanes], to_last, 0)
            down = [pltpu.roll(centre[f, tile, half], 1, 0) for tile in range(2)]
            up = [pltpu.roll(centre[f, tile, half], 7, 0) for tile in range(2)]
            y_minus[0, half] = jnp.where(first_sub, low, down[0])
            y_minus[1, half] = jnp.where(first_sub, down[0], down[1])
            y_plus[0, half] = jnp.where(last_sub, up[1], up[0])
            y_plus[1, half] = jnp.where(last_sub, high, up[1])
        for tile in range(2):
            low = pltpu.roll(z_before[f, tile_rows[tile], :], (LANES - x) % LANES, 1)
            high = pltpu.roll(z_after[f, tile_rows[tile], :], LANES - 1 - x, 1)
            right = [pltpu.roll(centre[f, tile, half], 1, 1) for half in range(2)]
            left = [pltpu.roll(centre[f, tile, half], LANES - 1, 1) for half in range(2)]
            z_minus[tile, 0] = jnp.where(first_lane, low, right[0])
            z_minus[tile, 1] = jnp.where(first_lane, right[0], right[1])
            z_plus[tile, 0] = jnp.where(last_lane, left[1], left[0])
            z_plus[tile, 1] = jnp.where(last_lane, high, left[1])
        for at in quarters:
            rows, lanes = tile_rows[at[0]], half_lanes[at[1]]
            x_minus, x_plus = before(f, rows, lanes), after(f, rows, lanes)
            slope_x = x_plus - x_minus
            slope_y = y_plus[at] - y_minus[at]
            slope_z = z_plus[at] - z_minus[at]
            laplace[f, *at] = (
                (x_plus + x_minus)
                + (y_plus[at] + y_minus[at])
                + (z_plus[at] + z_minus[at])
                - 6.0 * centre[f, *at]
            )
            if f < 3:
                strain[at] = strain[at] + (
                    slope_x * slope_x + slope_y * slope_y + slope_z * slope_z
                )
            advect[f, *at] = (
                speeds[0, *at] * slope_x + speeds[1, *at] * slope_y + speeds[2, *at] * slope_z
            )
    steps = {}
    for at in quarters:
        eddy = (0.5 * time_step * smagorinsky) * jnp.sqrt(strain[at])
        for f in range(count):
            mixing = time_step * diffusivity[f] + eddy
            steps[f, *at] = mixing * laplace[f, *at] - advect[f, *at]
    return centre, steps


class Planes:
    def __init__(self, current, halos, diffusivity, finish):
        self.x_pair, self.x_next, y_halo, z_pair, z_next, y_low, y_high, z_before, z_after = halos
        self.current, self.finish = current, finish
        self.rest = (y_low, y_high, z_before, z_after, diffusivity)
        cells = current.shape[1]
        upper, second = lax.axis_index("zl") > 0, odd("core")
        z_before[...] = jnp.where(second, z_pair[...], z_next[...])
        z_after[...] = jnp.where(second, z_next[...], z_pair[...])
        y_low[...] = jnp.where(upper, y_halo[:, :cells], 0.0)
        y_high[...] = jnp.where(upper, 0.0, y_halo[:, :cells])

    def one(self, x, before, after):
        self.finish(x, *plane(x, self.current, before, after, *self.rest))

    def inside(self, x):
        return lambda f, rows, lanes: self.current[f, x, rows, lanes]

    def outside(self, here, there):
        x_odd = odd("x")
        return lambda f, rows, lanes: jnp.where(x_odd, here[f, rows, lanes], there[f, rows, lanes])

    def ends(self):
        last = self.current.shape[1] - 1
        self.one(0, self.outside(self.x_pair, self.x_next), self.inside(1))
        self.one(last, self.inside(last - 1), self.outside(self.x_next, self.x_pair))

    def interior(self, after_block=lambda step: None):
        def body(step, carry):
            for i in range(BLOCK):
                x = step * BLOCK + 1 + i
                self.one(x, self.inside(x - 1), self.inside(x + 1))
            after_block(step)
            return carry

        lax.fori_loop(0, (self.current.shape[1] - 2) // BLOCK, body, 0)


def gram_kernel(basis, held, joined, folded):
    rank, _, _, levels, points = basis.shape
    total = rank + held.shape[0]
    for chunk in range(3 * levels):
        lanes = slice(chunk * points, (chunk + 1) * points)
        joined[0:rank, lanes] = basis[:, chunk // levels, 0, chunk % levels, :]
        joined[rank:total, lanes] = held[:, chunk // levels, 0, chunk % levels, :]
    sums = jnp.zeros((3 * total, total), jnp.float32)
    squares = jnp.zeros((total, total), jnp.float32)
    for chunk in range(3 * levels):
        high, middle, low = split(joined[:, chunk * points : (chunk + 1) * points])
        sums += matmul(jnp.concatenate([high, middle, low], axis=0), high, 1)
        squares += matmul(middle, middle, 1)
    half = total // 2
    wide = jnp.zeros((total, LANES - total), jnp.float32)
    cross = jnp.concatenate([sums[total : 2 * total] + sums[2 * total :], wide], axis=1)
    tall = jnp.concatenate([cross, jnp.zeros((LANES - total, LANES), jnp.float32)], axis=0)
    values = jnp.concatenate([sums[:total] + squares, wide], axis=1)
    values = values + (cross + tall.T[:total])
    lane, sub = iota((half, LANES), 1), iota((half, LANES), 0)
    lower = pltpu.roll(values[half:], LANES - half, 1)
    diagonal = jnp.sum(jnp.where(lane == sub, lower, 0.0), axis=1, keepdims=True)
    values = jnp.where(lane < sub, lower, values[:half])
    values = jnp.where(lane == total, jnp.broadcast_to(diagonal, (half, LANES)), values)
    folded[0:half, :] = jnp.where(lane <= total, values, 0.0)
    folded[half:, :] = jnp.zeros((folded.shape[0] - half, LANES), jnp.float32)


def first_kernel(
    diffusivity, folded, current, x_pair_in, x_next_in, y_halo, z_pair_in, z_next_in,
    first, x_pair, x_next, y_row, z_pair, z_next, *edges,
):
    count, cells = current.shape[:2]
    upper = lax.axis_index("zl") > 0
    y_row[:, cells:, :] = jnp.zeros((count, y_row.shape[1] - cells, y_row.shape[2]), jnp.float32)
    for group in range(3):
        lanes = slice(group % 2 * LANES, (group % 2 + 1) * LANES)
        y_row[group // 2, cells:, lanes] = jnp.where(
            upper, folded[group * 8 : group * 8 + 8], folded[group * 8 + 24 : group * 8 + 32]
        )

    def finish(x, centre, steps):
        for (f, tile, half), value in centre.items():
            first[f, x, tile * 8 : tile * 8 + 8, half * LANES : (half + 1) * LANES] = (
                value + steps[f, tile, half]
            )

    halos = (x_pair_in, x_next_in, y_halo, z_pair_in, z_next_in, *edges)
    planes = Planes(current, halos, diffusivity, finish)
    planes.ends()
    planes.interior()
    pack(first, row_shifts(upper), x_pair, x_next, y_row, z_pair, z_next)


def pick(picked, plane, column, keep, shift):
    for f in range(3):
        for tile in range(2):
            rows = pltpu.roll(plane(f, slice(tile * 8, tile * 8 + 8)), shift, 0)
            for part in range(2):
                row = column * 16 + f * 4 + tile * 2 + part
                value = rows[part * STRIDE : part * STRIDE + 1, :]
                if keep is not None:
                    value = jnp.where(keep, picked[row : row + 1, :], value)
                picked[row : row + 1, :] = value


def average(start, value, step):
    return 0.5 * (start + value + step)


def inner_kernel(
    diffusivity, offsets, start, current, y_halo, z_pair, z_next,
    target, picked, y_low, y_high, z_before, z_after, result, semaphores,
):
    cells = current.shape[1]
    blocks = (cells - 2) // BLOCK

    def finish(x, centre, steps):
        for (f, tile, half), value in centre.items():
            at = (f, x, slice(tile * 8, tile * 8 + 8), slice(half * LANES, (half + 1) * LANES))
            result[at] = average(start[at], value, steps[f, tile, half])

    def copied(step):
        part = pl.ds(step * BLOCK + 1, BLOCK)
        return pltpu.make_async_copy(result.at[:, part], target.at[:, part], semaphores.at[step])

    halos = (None, None, y_halo, z_pair, z_next, y_low, y_high, z_before, z_after)
    Planes(current, halos, diffusivity, finish).interior(lambda step: copied(step).start())
    picked[...] = jnp.zeros_like(picked)
    shift = (8 - offsets[1]) % 8
    for column in range(cells // STRIDE):
        x = jnp.clip(column * STRIDE + offsets[2], 1, cells - 2)
        pick(picked, lambda f, rows: result[f, x, rows, :], column, None, shift)

    def settle(step, carry):
        copied(step).wait()
        return carry

    lax.fori_loop(0, blocks, settle, 0)


def outer_kernel(
    diffusivity, offsets, folded, start, current, x_pair, x_next, y_halo, z_pair, z_next,
    picked_in, target_in, target, snapshot, y_low, y_high, z_before, z_after, picked, result,
    semaphores,
):
    _, cells, _, width = current.shape

    def finish(x, centre, steps):
        slot = 0 if x == 0 else 1
        for (f, tile, half), value in centre.items():
            rows, lanes = slice(tile * 8, tile * 8 + 8), slice(half * LANES, (half + 1) * LANES)
            result[f, slot, rows, lanes] = average(
                start[f, x, rows, lanes], value, steps[f, tile, half]
            )

    halos = (x_pair, x_next, y_halo, z_pair, z_next, y_low, y_high, z_before, z_after)
    Planes(current, halos, diffusivity, finish).ends()
    copies = [
        pltpu.make_async_copy(
            result.at[:, pl.ds(slot, 1)], target.at[:, pl.ds(x, 1)], semaphores.at[slot]
        )
        for slot, x in ((0, 0), (1, cells - 1))
    ]
    for copy in copies:
        copy.start()
    picked[...] = picked_in[...]
    shift = (8 - offsets[1]) % 8
    pick(picked, lambda f, rows: result[f, 0, rows, :], 0, offsets[2] > 0, shift)
    pick(
        picked, lambda f, rows: result[f, 1, rows, :], cells // STRIDE - 1,
        offsets[2] < STRIDE - 1, shift,
    )
    points = width // STRIDE
    choose = iota((width, LANES), 0) == STRIDE * (iota((width, LANES), 1) % points) + offsets[0]
    choose = choose.astype(jnp.float32).astype(jnp.bfloat16)
    high, middle, low = split(picked[...])
    snapshot[...] = matmul(high, choose, 0) + matmul(middle, choose, 0) + matmul(low, choose, 0)
    upper = lax.axis_index("zl") > 0
    for group in range(3):
        lanes = slice(group % 2 * LANES, (group % 2 + 1) * LANES)
        kept = jnp.where(
            upper, folded[group * 8 + 24 : group * 8 + 32], folded[group * 8 : group * 8 + 8]
        )
        kept = kept + y_halo[group // 2, cells:, lanes]
        for column in range(cells // STRIDE):
            row = column * 16 + 12 + group
            snapshot[row : row + 1, :] = kept[column : column + 1]
    for copy in copies:
        copy.wait()


def product_kernel(relayed, joined, message, column, partial):
    total = joined.shape[0]
    groups = total // 8
    low = iota((1, LANES), 1) < LANES // 2
    sums = [jnp.zeros((8, LANES), jnp.float32) for _ in range(groups + 1)]
    for row in range(12):
        for pair in range(4):
            tile = row * 4 + pair
            lanes = slice(tile * LANES, (tile + 1) * LANES)
            values = jnp.where(
                low,
                relayed[2 * pair, row : row + 1, :],
                relayed[2 * pair + 1, row : row + 1, :],
            )
            values = jnp.broadcast_to(values, (8, LANES))
            column[:, lanes] = values
            for group in range(groups):
                sums[group] += joined[group * 8 : group * 8 + 8, lanes] * values
            sums[groups] += values * values
    partial[...] = jnp.zeros_like(partial)
    for group in range(groups + 1):
        partial[group * 8 : group * 8 + 8, :] = sums[group]
    products = dot(jnp.ones((8, LANES), jnp.float32), partial[...], 1, 1)
    own = jnp.sum(relayed[:, 8:16, :], axis=0)
    lane, which = iota((24, LANES), 1), iota((24, LANES), 0) % 3
    values = jnp.zeros((24, LANES), jnp.float32)
    for piece in range(3):
        moved = pltpu.roll(products, 88 - 40 * piece if piece < 2 else 8, 1)[0:1]
        row = jnp.where(lane[0:1] < 88, own[4 + piece : 5 + piece], moved)
        values = jnp.where(which == piece, row, values)
    count = message.shape[0]
    message[...] = jnp.broadcast_to(values[None], (count // 24, 24, LANES)).reshape(count, LANES)


def middle_kernel(received, message):
    rows = jnp.sum(received[...].reshape(-1, 24, LANES), axis=0)
    count = message.shape[0]
    message[...] = jnp.broadcast_to(rows[None], (count // 24, 24, LANES)).reshape(count, LANES)


def final_kernel(
    rows_total, column_id, gathered, joined, column,
    coefficients, r_factor, columns_out, stacked,
):
    total = joined.shape[0]
    count, rank = coefficients.shape
    _, _, _, levels, points = columns_out.shape
    chosen = column_id[0]
    half = total // 2
    stacked[...] = jnp.sum(gathered[...].reshape(-1, 48, LANES), axis=0)
    pieces = [
        [stacked[pl.ds(part * 24 + piece, 8, stride=3), :] for piece in range(3)]
        for part in range(2)
    ]
    sums = [jnp.sum(pieces[0][i] + pieces[1][i], axis=0, keepdims=True) for i in range(3)]
    sums = [pltpu.roll(row, shift, 1) for row, shift in zip(sums, (40, 80, 120))]
    lane = iota((1, LANES), 1)
    sums = jnp.where(lane < 40, sums[0], jnp.where(lane < 80, sums[1], sums[2])) / rows_total
    folded = jnp.concatenate(pieces[0] + pieces[1][:2], axis=0) / rows_total
    turned = jnp.concatenate([folded, jnp.zeros((LANES - half, LANES), jnp.float32)], axis=0).T
    lane, sub = iota((half, LANES), 1), iota((half, LANES), 0)
    diagonal = jnp.broadcast_to(folded[:, total : total + 1], (half, LANES))
    upper = jnp.where((lane >= sub), folded, turned[:half])
    lower = jnp.where(lane < sub, folded, jnp.where(lane > sub, turned[:half], diagonal))
    gram = jnp.concatenate(
        [
            upper,
            jnp.where(lane < half, turned[half:total], pltpu.roll(lower, half, 1)),
        ],
        axis=0,
    )
    lane = iota((total, LANES), 1)
    down = jnp.broadcast_to(sums, (LANES, LANES)).T
    modes = gram[:rank, :rank]
    shifted = pltpu.roll(gram, LANES - rank, 1)
    first = jnp.where(lane[:rank] == chosen, down[:rank], shifted[:rank])[:, :count]
    block_lane, block_sub = iota((count, LANES), 1), iota((count, LANES), 0)
    square = jnp.broadcast_to(sums[:, total : total + 1], (1, LANES))
    across = jnp.where(
        block_lane[0:1] == chosen, square, pltpu.roll(sums, LANES - rank, 1)
    )
    block = jnp.where(block_lane == chosen, down[rank:total], shifted[rank:total])
    block = jnp.where(block_sub == chosen, jnp.broadcast_to(across, (count, LANES)), block)
    second = first - dot(modes, first, 1, 0)
    both = first + second
    third = first - dot(modes, both, 1, 0)
    square = dot(
        jnp.concatenate([first, both], axis=0), jnp.concatenate([both, third], axis=0), 0, 0
    )
    square = jnp.concatenate([square, jnp.zeros((count, LANES - count), jnp.float32)], axis=1)
    state = jnp.where(block_lane < count, block - square, 0.0)
    state = jnp.where(block_lane == block_sub + count, 1.0, state)
    for step in range(count - 1):
        row = state[step : step + 1, :]
        scale = state[:, step : step + 1] / row[:, step : step + 1]
        scale = jnp.where(block_sub > step, jnp.broadcast_to(scale, (count, LANES)), 0.0)
        state = state - scale * row
    diagonal = jnp.sum(jnp.where(block_lane == block_sub, state, 0.0), axis=1, keepdims=True)
    state = state / jnp.sqrt(diagonal)
    r_factor[...] = jnp.where(block_lane >= block_sub, state, 0.0)[:, :count]
    padded = jnp.concatenate([both, jnp.zeros((rank, LANES - count), jnp.float32)], axis=1)
    padded = jnp.concatenate([padded, jnp.zeros((LANES - rank, LANES), jnp.float32)], axis=0)
    coefficients[...] = padded.T[:count, :rank]
    inverse = pltpu.roll(state, LANES - count, 1)
    inverse = jnp.where(block_lane < count, inverse, 0.0)
    onto_modes = dot(inverse[:, :count], both, 1, 1)
    own = jnp.sum(jnp.where(block_lane == chosen, inverse, 0.0), axis=1, keepdims=True)
    onto_block = pltpu.roll(jnp.where(block_lane == chosen, 0.0, inverse), rank, 1)
    onto_modes = jnp.concatenate(
        [-onto_modes, jnp.zeros((count, LANES - rank), jnp.float32)], axis=1
    )
    weights = jnp.where(block_lane < rank, onto_modes, onto_block)[:, :total]
    weights = jnp.concatenate(split(weights), axis=0)
    for chunk in range(3 * levels):
        lanes = slice(chunk * points, (chunk + 1) * points)
        high, middle, low = split(joined[:, lanes])
        first = matmul(weights, high, 0)
        second = matmul(weights[: 2 * count], middle, 0)
        third = matmul(weights[:count], low, 0)
        columns_out[:, chunk // levels, 0, chunk % levels, :] = (
            (first[:count] + own * column[0:1, lanes])
            + (first[count : 2 * count] + second[:count])
            + (first[2 * count :] + second[count:] + third)
        )


def moved(value, axes, target):
    sizes = [lax.axis_size(axis) for axis in axes]
    places = list(itertools.product(*(range(size) for size in sizes)))
    flat = {place: i for i, place in enumerate(places)}
    pairs = [
        (flat[place], flat[tuple(i % size for i, size in zip(target(*place), sizes))])
        for place in places
    ]
    return lax.ppermute(value, axes, pairs)


def exchange(faces):
    x_pair, x_next, y_row, z_pair, z_next = faces

    def along(zh, x):
        step = x + 1 if x % 2 else x - 1
        return zh + step // 4, step

    def swap(core):
        return (core ^ 1,)

    z_next = moved(z_next, ("y", "core"), lambda y, core: (y + 2 * core - 1, core))
    return (
        moved(x_pair, ("x",), lambda x: (x ^ 1,)),
        moved(x_next, ("zh", "x"), along),
        moved(y_row, ("zl",), lambda zl: (zl + 1,)),
        moved(z_pair, ("core",), swap),
        moved(z_next, ("core",), swap),
    )


def everyone(message, axes):
    rows = message.shape[0]
    message = lax.all_to_all(message.reshape(rows, 1, LANES), axes, 0, 0, tiled=True)
    return message.reshape(rows, LANES)


def on_device(fields, diffusivity, subsample_offsets, column_id, pod_basis, held_block):
    count, cells, height, width = fields.shape
    rank, columns = pod_basis.shape[0], held_block.shape[0]
    devices = 1
    for axis in AXES:
        devices *= lax.axis_size(axis)
    points = held_block.shape[-1]
    chunks = 3 * held_block.shape[3]
    length = chunks * points
    total = rank + columns
    faces = (
        struct(count, height, width),
        struct(count, height, width),
        struct(count, cells, width),
        struct(count, height, LANES),
        struct(count, height, LANES),
    )
    wall = pltpu.VMEM((count, cells, width), jnp.float32)
    edge = pltpu.VMEM((count, height, LANES), jnp.float32)
    busy = pl.CostEstimate(flops=2 * 10**7, bytes_accessed=2 * 10**7, transcendentals=0)

    packed = pl.pallas_call(
        pack_kernel, in_specs=[VMEM], out_specs=[VMEM] * 5, out_shape=faces,
        compiler_params=params(16),
    )(fields)
    halos = exchange(packed)

    joined, folded = pl.pallas_call(
        gram_kernel, in_specs=[VMEM] * 2, out_specs=[VMEM] * 2,
        out_shape=(struct(total, length), struct(48, LANES)),
        compiler_params=params(16),
    )(pod_basis, held_block)

    first, *packed = pl.pallas_call(
        first_kernel, in_specs=[SMEM] + [VMEM] * 7, out_specs=[VMEM] * 6,
        out_shape=(struct(*fields.shape),) + faces[:2] + (struct(count, cells + 8, width),)
        + faces[3:],
        scratch_shapes=[wall, wall, edge, edge], compiler_params=params(24),
    )(diffusivity, folded, fields, *halos)
    halos = exchange(packed)

    x_pair, x_next, *halos = halos
    sides = [wall, wall, edge, edge]
    fields_out, picked = pl.pallas_call(
        inner_kernel, in_specs=[SMEM] * 2 + [VMEM] * 5, out_specs=[ANY, VMEM],
        out_shape=(struct(*fields.shape), struct(LANES, width)),
        scratch_shapes=sides + [
            pltpu.VMEM(fields.shape, jnp.float32), pltpu.SemaphoreType.DMA((10,)),
        ],
        cost_estimate=busy, compiler_params=params(24),
    )(diffusivity, subsample_offsets, fields, first, *halos)
    fields_out, snapshot = pl.pallas_call(
        outer_kernel, in_specs=[SMEM] * 2 + [VMEM] * 9 + [ANY], out_specs=[ANY, VMEM],
        out_shape=(struct(*fields.shape), struct(LANES, LANES)),
        scratch_shapes=sides + [
            pltpu.VMEM((LANES, width), jnp.float32),
            pltpu.VMEM((count, 2, height, width), jnp.float32),
            pltpu.SemaphoreType.DMA((2,)),
        ],
        input_output_aliases={11: 0}, compiler_params=params(24),
    )(
        diffusivity, subsample_offsets, folded, fields, first, x_pair, x_next, *halos,
        picked, fields_out,
    )
    relayed = lax.all_to_all(snapshot.reshape(8, 16, LANES), ("y", "core"), 0, 0, tiled=True)

    message, column = pl.pallas_call(
        product_kernel, in_specs=[VMEM] * 2, out_specs=[VMEM] * 2,
        out_shape=(struct(96, LANES), struct(8, length)),
        scratch_shapes=[pltpu.VMEM((LANES, LANES), jnp.float32)],
        compiler_params=params(16),
    )(relayed, joined)
    message = pl.pallas_call(
        middle_kernel, in_specs=[VMEM], out_specs=VMEM, out_shape=struct(192, LANES),
        compiler_params=params(4),
    )(everyone(message, ("x", "y", "core")))
    gathered = everyone(message, ("zh", "zl"))

    coefficients, r_factor, new_columns = pl.pallas_call(
        functools.partial(final_kernel, float(devices * length)),
        in_specs=[SMEM] + [VMEM] * 3, out_specs=[VMEM] * 3,
        out_shape=(
            struct(columns, rank), struct(columns, columns), struct(*held_block.shape)
        ),
        scratch_shapes=[
            pltpu.VMEM((48, LANES), jnp.float32),
        ],
        compiler_params=params(24),
    )(column_id, gathered, joined, column)
    return fields_out, coefficients.T, r_factor, new_columns


def solution(mesh):
    mesh = jax.sharding.Mesh(mesh.devices.reshape(4, 4, 4, 2, 2), AXES)
    block = P(None, ("zh", "x"), "zl", ("y", "core"))
    rows = P(None, None, ("zh", "x", "y", "core"), "zl", None)
    return jax.shard_map(
        on_device,
        mesh=mesh,
        in_specs=(block, P(), P(), P(), rows, rows),
        out_specs=(block, P(), P(), rows),
        check_vma=False,
    )
```

```python
import functools
import itertools

import jax
import jax.numpy as jnp
from jax import lax
from jax.experimental import pallas as pl
from jax.experimental.pallas import tpu as pltpu
from jax.sharding import PartitionSpec as P

STRIDE = 4
LANES = 128
BLOCK = 5

time_step = 0.1
smagorinsky = 0.02

VMEM = pl.BlockSpec(memory_space=pltpu.VMEM)
ANY = pl.BlockSpec(memory_space=pl.ANY)
SMEM = pl.BlockSpec(memory_space=pltpu.SMEM)
HIGH = lax.Precision.HIGHEST
AXES = ("zh", "x", "y", "core", "zl")


def params(mib):
    return pltpu.CompilerParams(vmem_limit_bytes=mib * 1024 * 1024)


def struct(*shape):
    return jax.ShapeDtypeStruct(shape, jnp.float32)


def iota(shape, dim):
    return lax.broadcasted_iota(jnp.int32, shape, dim)


def dot(left, right, left_dim, right_dim):
    return lax.dot_general(
        left,
        right,
        (((left_dim,), (right_dim,)), ((), ())),
        precision=HIGH,
        preferred_element_type=jnp.float32,
    )


def split(value):
    high = value.astype(jnp.bfloat16)
    value = value - high.astype(jnp.float32)
    middle = value.astype(jnp.bfloat16)
    return high, middle, (value - middle.astype(jnp.float32)).astype(jnp.bfloat16)


def matmul(left, right, right_dim):
    return lax.dot_general(
        left, right, (((1,), (right_dim,)), ((), ())), preferred_element_type=jnp.float32
    )


def odd(axis):
    return lax.rem(lax.axis_index(axis), 2) > 0


def pack(fields, rows, x_pair, x_next, y_row, z_pair, z_next):
    count, cells, height, _ = fields.shape
    upper = lax.axis_index("zl") > 0
    lane, sub = iota((8, LANES), 1), iota((8, LANES), 0)
    keys = [(f, half, tile) for f in range(count) for half in range(2) for tile in range(2)]

    def body(group, faces):
        faces = dict(zip(keys, faces))
        y_rows = {}
        for i in range(8):
            x = group * 8 + i
            for f in range(count):
                for half in range(2):
                    lanes = slice(half * LANES, (half + 1) * LANES)
                    values = (fields[f, x, 0:8, lanes], fields[f, x, height - 8 : height, lanes])
                    row = pltpu.roll(jnp.where(upper, values[0], values[1]), rows[i], 0)
                    y_rows[f, half] = row if i == 0 else jnp.where(sub == i, row, y_rows[f, half])
                    shift = (x + half) % LANES
                    for tile in range(2):
                        face = pltpu.roll(values[tile], shift, 1)
                        faces[f, half, tile] = jnp.where(lane == x, face, faces[f, half, tile])
        for f in range(count):
            for half in range(2):
                place = pl.ds(pl.multiple_of(group * 8, 8), 8)
                y_row[f, place, half * LANES : (half + 1) * LANES] = y_rows[f, half]
        return tuple(faces[key] for key in keys)

    zero = jnp.zeros((8, LANES), jnp.float32)
    faces = lax.fori_loop(0, cells // 8, body, tuple(zero for _ in keys))
    x_odd, second = odd("x"), odd("core")
    for (f, half, tile), face in zip(keys, faces):
        if half == 0:
            other = faces[keys.index((f, 1, tile))]
            place = slice(tile * 8, tile * 8 + 8)
            z_pair[f, place, :] = jnp.where(second, face, other)
            z_next[f, place, :] = jnp.where(second, other, face)
    low, high = fields[:, 0], fields[:, cells - 1]
    x_pair[...] = jnp.where(x_odd, low, high)
    x_next[...] = jnp.where(x_odd, high, low)


def row_shifts(upper):
    return [(i + jnp.where(upper, 0, 1)) % 8 for i in range(8)]


def pack_kernel(fields, x_pair, x_next, y_row, z_pair, z_next):
    rows = row_shifts(lax.axis_index("zl") > 0)
    pack(fields, rows, x_pair, x_next, y_row, z_pair, z_next)


def plane(x, current, before, after, y_low, y_high, z_before, z_after, diffusivity):
    count = current.shape[0]
    lane, sub = iota((8, LANES), 1), iota((8, LANES), 0)
    first_lane, last_lane = lane == 0, lane == LANES - 1
    first_sub, last_sub = sub == 0, sub == 7
    tile_rows = (slice(0, 8), slice(8, 16))
    half_lanes = (slice(0, LANES), slice(LANES, 2 * LANES))
    quarters = [(tile, half) for tile in range(2) for half in range(2)]
    group = pl.ds(pl.multiple_of(x // 8 * 8, 8), 8)
    to_first, to_last = (8 - x % 8) % 8, 7 - x % 8
    centre = {
        (f, tile, half): current[f, x, tile_rows[tile], half_lanes[half]]
        for f in range(count)
        for tile, half in quarters
    }
    speeds = {
        (f, *at): (0.5 * time_step) * centre[f, *at] for f in range(3) for at in quarters
    }
    strain = dict.fromkeys(quarters, 0.0)
    laplace, advect = {}, {}
    for f in range(count):
        y_minus, y_plus, z_minus, z_plus = {}, {}, {}, {}
        for half in range(2):
            lanes = half_lanes[half]
            low = pltpu.roll(y_low[f, group, lanes], to_first, 0)
            high = pltpu.roll(y_high[f, group, lanes], to_last, 0)
            down = [pltpu.roll(centre[f, tile, half], 1, 0) for tile in range(2)]
            up = [pltpu.roll(centre[f, tile, half], 7, 0) for tile in range(2)]
            y_minus[0, half] = jnp.where(first_sub, low, down[0])
            y_minus[1, half] = jnp.where(first_sub, down[0], down[1])
            y_plus[0, half] = jnp.where(last_sub, up[1], up[0])
            y_plus[1, half] = jnp.where(last_sub, high, up[1])
        for tile in range(2):
            low = pltpu.roll(z_before[f, tile_rows[tile], :], (LANES - x) % LANES, 1)
            high = pltpu.roll(z_after[f, tile_rows[tile], :], LANES - 1 - x, 1)
            right = [pltpu.roll(centre[f, tile, half], 1, 1) for half in range(2)]
            left = [pltpu.roll(centre[f, tile, half], LANES - 1, 1) for half in range(2)]
            z_minus[tile, 0] = jnp.where(first_lane, low, right[0])
            z_minus[tile, 1] = jnp.where(first_lane, right[0], right[1])
            z_plus[tile, 0] = jnp.where(last_lane, left[1], left[0])
            z_plus[tile, 1] = jnp.where(last_lane, high, left[1])
        for at in quarters:
            rows, lanes = tile_rows[at[0]], half_lanes[at[1]]
            x_minus, x_plus = before(f, rows, lanes), after(f, rows, lanes)
            slope_x = x_plus - x_minus
            slope_y = y_plus[at] - y_minus[at]
            slope_z = z_plus[at] - z_minus[at]
            laplace[f, *at] = (
                (x_plus + x_minus)
                + (y_plus[at] + y_minus[at])
                + (z_plus[at] + z_minus[at])
                - 6.0 * centre[f, *at]
            )
            if f < 3:
                strain[at] = strain[at] + (
                    slope_x * slope_x + slope_y * slope_y + slope_z * slope_z
                )
            advect[f, *at] = (
                speeds[0, *at] * slope_x + speeds[1, *at] * slope_y + speeds[2, *at] * slope_z
            )
    steps = {}
    for at in quarters:
        eddy = (0.5 * time_step * smagorinsky) * jnp.sqrt(strain[at])
        for f in range(count):
            mixing = time_step * diffusivity[f] + eddy
            steps[f, *at] = mixing * laplace[f, *at] - advect[f, *at]
    return centre, steps


class Planes:
    def __init__(self, current, halos, diffusivity, finish):
        self.x_pair, self.x_next, y_halo, z_pair, z_next, y_low, y_high, z_before, z_after = halos
        self.current, self.finish = current, finish
        self.rest = (y_low, y_high, z_before, z_after, diffusivity)
        cells = current.shape[1]
        upper, second = lax.axis_index("zl") > 0, odd("core")
        z_before[...] = jnp.where(second, z_pair[...], z_next[...])
        z_after[...] = jnp.where(second, z_next[...], z_pair[...])
        y_low[...] = jnp.where(upper, y_halo[:, :cells], 0.0)
        y_high[...] = jnp.where(upper, 0.0, y_halo[:, :cells])

    def one(self, x, before, after):
        self.finish(x, *plane(x, self.current, before, after, *self.rest))

    def inside(self, x):
        return lambda f, rows, lanes: self.current[f, x, rows, lanes]

    def outside(self, here, there):
        x_odd = odd("x")
        return lambda f, rows, lanes: jnp.where(x_odd, here[f, rows, lanes], there[f, rows, lanes])

    def ends(self):
        last = self.current.shape[1] - 1
        self.one(0, self.outside(self.x_pair, self.x_next), self.inside(1))
        self.one(last, self.inside(last - 1), self.outside(self.x_next, self.x_pair))

    def interior(self, after_block=lambda step: None):
        def body(step, carry):
            for i in range(BLOCK):
                x = step * BLOCK + 1 + i
                self.one(x, self.inside(x - 1), self.inside(x + 1))
            after_block(step)
            return carry

        lax.fori_loop(0, (self.current.shape[1] - 2) // BLOCK, body, 0)


def gram_kernel(basis, held, joined, folded):
    rank, _, _, levels, points = basis.shape
    total = rank + held.shape[0]
    for chunk in range(3 * levels):
        lanes = slice(chunk * points, (chunk + 1) * points)
        joined[0:rank, lanes] = basis[:, chunk // levels, 0, chunk % levels, :]
        joined[rank:total, lanes] = held[:, chunk // levels, 0, chunk % levels, :]
    sums = jnp.zeros((3 * total, total), jnp.float32)
    squares = jnp.zeros((total, total), jnp.float32)
    for chunk in range(3 * levels):
        high, middle, low = split(joined[:, chunk * points : (chunk + 1) * points])
        sums += matmul(jnp.concatenate([high, middle, low], axis=0), high, 1)
        squares += matmul(middle, middle, 1)
    half = total // 2
    wide = jnp.zeros((total, LANES - total), jnp.float32)
    cross = jnp.concatenate([sums[total : 2 * total] + sums[2 * total :], wide], axis=1)
    tall = jnp.concatenate([cross, jnp.zeros((LANES - total, LANES), jnp.float32)], axis=0)
    values = jnp.concatenate([sums[:total] + squares, wide], axis=1)
    values = values + (cross + tall.T[:total])
    lane, sub = iota((half, LANES), 1), iota((half, LANES), 0)
    lower = pltpu.roll(values[half:], LANES - half, 1)
    diagonal = jnp.sum(jnp.where(lane == sub, lower, 0.0), axis=1, keepdims=True)
    values = jnp.where(lane < sub, lower, values[:half])
    values = jnp.where(lane == total, jnp.broadcast_to(diagonal, (half, LANES)), values)
    folded[0:half, :] = jnp.where(lane <= total, values, 0.0)
    folded[half:, :] = jnp.zeros((folded.shape[0] - half, LANES), jnp.float32)


def first_kernel(
    diffusivity, folded, current, x_pair_in, x_next_in, y_halo, z_pair_in, z_next_in,
    first, x_pair, x_next, y_row, z_pair, z_next, *edges,
):
    count, cells = current.shape[:2]
    upper = lax.axis_index("zl") > 0
    y_row[:, cells:, :] = jnp.zeros((count, y_row.shape[1] - cells, y_row.shape[2]), jnp.float32)
    for group in range(3):
        lanes = slice(group % 2 * LANES, (group % 2 + 1) * LANES)
        y_row[group // 2, cells:, lanes] = jnp.where(
            upper, folded[group * 8 : group * 8 + 8], folded[group * 8 + 24 : group * 8 + 32]
        )

    def finish(x, centre, steps):
        for (f, tile, half), value in centre.items():
            first[f, x, tile * 8 : tile * 8 + 8, half * LANES : (half + 1) * LANES] = (
                value + steps[f, tile, half]
            )

    halos = (x_pair_in, x_next_in, y_halo, z_pair_in, z_next_in, *edges)
    planes = Planes(current, halos, diffusivity, finish)
    planes.ends()
    planes.interior()
    pack(first, row_shifts(upper), x_pair, x_next, y_row, z_pair, z_next)


def pick(picked, plane, column, keep, shift):
    for f in range(3):
        for tile in range(2):
            rows = pltpu.roll(plane(f, slice(tile * 8, tile * 8 + 8)), shift, 0)
            for part in range(2):
                row = column * 16 + f * 4 + tile * 2 + part
                value = rows[part * STRIDE : part * STRIDE + 1, :]
                if keep is not None:
                    value = jnp.where(keep, picked[row : row + 1, :], value)
                picked[row : row + 1, :] = value


def average(start, value, step):
    return 0.5 * (start + value + step)


def inner_kernel(
    diffusivity, offsets, start, current, y_halo, z_pair, z_next,
    target, picked, y_low, y_high, z_before, z_after, result, semaphores,
):
    cells = current.shape[1]
    blocks = (cells - 2) // BLOCK

    def finish(x, centre, steps):
        for (f, tile, half), value in centre.items():
            at = (f, x, slice(tile * 8, tile * 8 + 8), slice(half * LANES, (half + 1) * LANES))
            result[at] = average(start[at], value, steps[f, tile, half])

    def copied(step):
        part = pl.ds(step * BLOCK + 1, BLOCK)
        return pltpu.make_async_copy(result.at[:, part], target.at[:, part], semaphores.at[step])

    halos = (None, None, y_halo, z_pair, z_next, y_low, y_high, z_before, z_after)
    Planes(current, halos, diffusivity, finish).interior(lambda step: copied(step).start())
    picked[...] = jnp.zeros_like(picked)
    shift = (8 - offsets[1]) % 8
    for column in range(cells // STRIDE):
        x = jnp.clip(column * STRIDE + offsets[2], 1, cells - 2)
        pick(picked, lambda f, rows: result[f, x, rows, :], column, None, shift)

    def settle(step, carry):
        copied(step).wait()
        return carry

    lax.fori_loop(0, blocks, settle, 0)


def outer_kernel(
    diffusivity, offsets, column_id, folded, start, current, x_pair, x_next, y_halo, z_pair,
    z_next, picked_in, target_in, target, snapshot, chosen, y_low, y_high, z_before, z_after, picked, result,
    semaphores,
):
    _, cells, _, width = current.shape

    def finish(x, centre, steps):
        slot = 0 if x == 0 else 1
        for (f, tile, half), value in centre.items():
            rows, lanes = slice(tile * 8, tile * 8 + 8), slice(half * LANES, (half + 1) * LANES)
            result[f, slot, rows, lanes] = average(
                start[f, x, rows, lanes], value, steps[f, tile, half]
            )

    halos = (x_pair, x_next, y_halo, z_pair, z_next, y_low, y_high, z_before, z_after)
    Planes(current, halos, diffusivity, finish).ends()
    copies = [
        pltpu.make_async_copy(
            result.at[:, pl.ds(slot, 1)], target.at[:, pl.ds(x, 1)], semaphores.at[slot]
        )
        for slot, x in ((0, 0), (1, cells - 1))
    ]
    for copy in copies:
        copy.start()
    chosen[...] = jnp.full(chosen.shape, column_id[0], jnp.int32)
    picked[...] = picked_in[...]
    shift = (8 - offsets[1]) % 8
    pick(picked, lambda f, rows: result[f, 0, rows, :], 0, offsets[2] > 0, shift)
    pick(
        picked, lambda f, rows: result[f, 1, rows, :], cells // STRIDE - 1,
        offsets[2] < STRIDE - 1, shift,
    )
    points = width // STRIDE
    choose = iota((width, LANES), 0) == STRIDE * (iota((width, LANES), 1) % points) + offsets[0]
    choose = choose.astype(jnp.float32).astype(jnp.bfloat16)
    high, middle, low = split(picked[...])
    snapshot[...] = matmul(high, choose, 0) + matmul(middle, choose, 0) + matmul(low, choose, 0)
    upper = lax.axis_index("zl") > 0
    for group in range(3):
        lanes = slice(group % 2 * LANES, (group % 2 + 1) * LANES)
        kept = jnp.where(
            upper, folded[group * 8 + 24 : group * 8 + 32], folded[group * 8 : group * 8 + 8]
        )
        kept = kept + y_halo[group // 2, cells:, lanes]
        for column in range(cells // STRIDE):
            row = column * 16 + 12 + group
            snapshot[row : row + 1, :] = kept[column : column + 1]
    for copy in copies:
        copy.wait()


def product_kernel(relayed, joined, message, column, partial):
    total = joined.shape[0]
    groups = total // 8
    low = iota((1, LANES), 1) < LANES // 2
    sums = [jnp.zeros((8, LANES), jnp.float32) for _ in range(groups + 1)]
    for row in range(12):
        for pair in range(4):
            tile = row * 4 + pair
            lanes = slice(tile * LANES, (tile + 1) * LANES)
            values = jnp.where(
                low,
                relayed[2 * pair, row : row + 1, :],
                relayed[2 * pair + 1, row : row + 1, :],
            )
            values = jnp.broadcast_to(values, (8, LANES))
            column[:, lanes] = values
            for group in range(groups):
                sums[group] += joined[group * 8 : group * 8 + 8, lanes] * values
            sums[groups] += values * values
    partial[...] = jnp.zeros_like(partial)
    for group in range(groups + 1):
        partial[group * 8 : group * 8 + 8, :] = sums[group]
    products = dot(jnp.ones((8, LANES), jnp.float32), partial[...], 1, 1)
    own = jnp.sum(relayed[:, 8:16, :], axis=0)
    lane = iota((1, LANES), 1)
    rows = [own[4 + piece : 5 + piece] for piece in range(3)]
    rows = [
        jnp.where(lane < 81, rows[0], pltpu.roll(rows[2], 81, 1)),
        jnp.where(lane < 81, rows[1], pltpu.roll(rows[2], 34, 1)),
        products[0:1],
    ]
    which = iota((24, LANES), 0) % 3
    values = jnp.where(which == 0, rows[0], jnp.where(which == 1, rows[1], rows[2]))
    count = message.shape[0]
    message[...] = jnp.broadcast_to(values[None], (count // 24, 24, LANES)).reshape(count, LANES)


def middle_kernel(received, message, stacked):
    stacked[...] = jnp.sum(received[...].reshape(-1, 24, LANES), axis=0)
    first, second, third = (stacked[pl.ds(piece, 8, stride=3), :] for piece in range(3))
    third = jnp.sum(third, axis=0, keepdims=True)
    for target in range(message.shape[0] // 17):
        message[target * 17 : target * 17 + 8, :] = first
        message[target * 17 + 8 : target * 17 + 16, :] = second
        message[target * 17 + 16 : target * 17 + 17, :] = third


def final_kernel(
    rows_total, chosen_column, gathered, joined, column,
    coefficients, r_factor, columns_out,
):
    total = joined.shape[0]
    count, rank = coefficients.shape
    _, _, _, levels, points = columns_out.shape
    chosen = chosen_column[0:1, :]
    half = total // 2
    lane = iota((8, LANES), 1)
    pieces = []
    for part in range(2):
        first, second = (
            sum(gathered[17 * (2 * i + part) + at : 17 * (2 * i + part) + at + 8, :] for i in range(4))
            for at in (0, 8)
        )
        third = jnp.where(lane < 47, pltpu.roll(first, 47, 1), pltpu.roll(second, 94, 1))
        pieces.append([first, second, third])
    sums = sum(gathered[17 * i + 16 : 17 * i + 17, :] for i in range(8)) / rows_total
    folded = jnp.concatenate(pieces[0] + pieces[1][:2], axis=0) / rows_total
    turned = jnp.concatenate([folded, jnp.zeros((LANES - half, LANES), jnp.float32)], axis=0).T
    lane, sub = iota((half, LANES), 1), iota((half, LANES), 0)
    diagonal = jnp.broadcast_to(folded[:, total : total + 1], (half, LANES))
    upper = jnp.where((lane >= sub), folded, turned[:half])
    lower = jnp.where(lane < sub, folded, jnp.where(lane > sub, turned[:half], diagonal))
    gram = jnp.concatenate(
        [
            upper,
            jnp.where(lane < half, turned[half:total], pltpu.roll(lower, half, 1)),
        ],
        axis=0,
    )
    lane = iota((total, LANES), 1)
    down = jnp.broadcast_to(sums, (LANES, LANES)).T
    modes = gram[:rank, :rank]
    shifted = pltpu.roll(gram, LANES - rank, 1)
    first = jnp.where(lane[:rank] == chosen, down[:rank], shifted[:rank])[:, :count]
    block_lane, block_sub = iota((count, LANES), 1), iota((count, LANES), 0)
    square = jnp.broadcast_to(sums[:, total : total + 1], (1, LANES))
    across = jnp.where(
        block_lane[0:1] == chosen, square, pltpu.roll(sums, LANES - rank, 1)
    )
    block = jnp.where(block_lane == chosen, down[rank:total], shifted[rank:total])
    block = jnp.where(block_sub == chosen, jnp.broadcast_to(across, (count, LANES)), block)
    second = first - dot(modes, first, 1, 0)
    both = first + second
    third = first - dot(modes, both, 1, 0)
    square = dot(
        jnp.concatenate([first, both], axis=0), jnp.concatenate([both, third], axis=0), 0, 0
    )
    square = jnp.concatenate([square, jnp.zeros((count, LANES - count), jnp.float32)], axis=1)
    state = jnp.where(block_lane < count, block - square, 0.0)
    state = jnp.where(block_lane == block_sub + count, 1.0, state)
    for step in range(count - 1):
        row = state[step : step + 1, :]
        scale = state[:, step : step + 1] / row[:, step : step + 1]
        scale = jnp.where(block_sub > step, jnp.broadcast_to(scale, (count, LANES)), 0.0)
        state = state - scale * row
    diagonal = jnp.sum(jnp.where(block_lane == block_sub, state, 0.0), axis=1, keepdims=True)
    state = state / jnp.sqrt(diagonal)
    r_factor[...] = jnp.where(block_lane >= block_sub, state, 0.0)[:, :count]
    padded = jnp.concatenate([both, jnp.zeros((rank, LANES - count), jnp.float32)], axis=1)
    padded = jnp.concatenate([padded, jnp.zeros((LANES - rank, LANES), jnp.float32)], axis=0)
    coefficients[...] = padded.T[:count, :rank]
    inverse = pltpu.roll(state, LANES - count, 1)
    inverse = jnp.where(block_lane < count, inverse, 0.0)
    onto_modes = dot(inverse[:, :count], both, 1, 1)
    own = jnp.sum(jnp.where(block_lane == chosen, inverse, 0.0), axis=1, keepdims=True)
    onto_block = pltpu.roll(jnp.where(block_lane == chosen, 0.0, inverse), rank, 1)
    onto_modes = jnp.concatenate(
        [-onto_modes, jnp.zeros((count, LANES - rank), jnp.float32)], axis=1
    )
    weights = jnp.where(block_lane < rank, onto_modes, onto_block)[:, :total]
    weights = jnp.concatenate(split(weights), axis=0)
    for chunk in range(3 * levels):
        lanes = slice(chunk * points, (chunk + 1) * points)
        high, middle, low = split(joined[:, lanes])
        first = matmul(weights, high, 0)
        second = matmul(weights[: 2 * count], middle, 0)
        third = matmul(weights[:count], low, 0)
        columns_out[:, chunk // levels, 0, chunk % levels, :] = (
            (first[:count] + own * column[0:1, lanes])
            + (first[count : 2 * count] + second[:count])
            + (first[2 * count :] + second[count:] + third)
        )


def moved(value, axes, target):
    sizes = [lax.axis_size(axis) for axis in axes]
    places = list(itertools.product(*(range(size) for size in sizes)))
    flat = {place: i for i, place in enumerate(places)}
    pairs = [
        (flat[place], flat[tuple(i % size for i, size in zip(target(*place), sizes))])
        for place in places
    ]
    return lax.ppermute(value, axes, pairs)


def exchange(faces):
    x_pair, x_next, y_row, z_pair, z_next = faces

    def along(zh, x):
        step = x + 1 if x % 2 else x - 1
        return zh + step // 4, step

    def swap(core):
        return (core ^ 1,)

    z_next = moved(z_next, ("y", "core"), lambda y, core: (y + 2 * core - 1, core))
    return (
        moved(x_pair, ("x",), lambda x: (x ^ 1,)),
        moved(x_next, ("zh", "x"), along),
        moved(y_row, ("zl",), lambda zl: (zl + 1,)),
        moved(z_pair, ("core",), swap),
        moved(z_next, ("core",), swap),
    )


def everyone(message, axes):
    rows = message.shape[0]
    message = lax.all_to_all(message.reshape(rows, 1, LANES), axes, 0, 0, tiled=True)
    return message.reshape(rows, LANES)


def on_device(fields, diffusivity, subsample_offsets, column_id, pod_basis, held_block):
    count, cells, height, width = fields.shape
    rank, columns = pod_basis.shape[0], held_block.shape[0]
    devices = 1
    for axis in AXES:
        devices *= lax.axis_size(axis)
    points = held_block.shape[-1]
    chunks = 3 * held_block.shape[3]
    length = chunks * points
    total = rank + columns
    faces = (
        struct(count, height, width),
        struct(count, height, width),
        struct(count, cells, width),
        struct(count, height, LANES),
        struct(count, height, LANES),
    )
    wall = pltpu.VMEM((count, cells, width), jnp.float32)
    edge = pltpu.VMEM((count, height, LANES), jnp.float32)
    busy = pl.CostEstimate(flops=2 * 10**7, bytes_accessed=2 * 10**7, transcendentals=0)

    packed = pl.pallas_call(
        pack_kernel, in_specs=[VMEM], out_specs=[VMEM] * 5, out_shape=faces,
        compiler_params=params(16),
    )(fields)
    halos = exchange(packed)

    joined, folded = pl.pallas_call(
        gram_kernel, in_specs=[VMEM] * 2, out_specs=[VMEM] * 2,
        out_shape=(struct(total, length), struct(48, LANES)),
        compiler_params=params(16),
    )(pod_basis, held_block)

    first, *packed = pl.pallas_call(
        first_kernel, in_specs=[SMEM] + [VMEM] * 7, out_specs=[VMEM] * 6,
        out_shape=(struct(*fields.shape),) + faces[:2] + (struct(count, cells + 8, width),)
        + faces[3:],
        scratch_shapes=[wall, wall, edge, edge], compiler_params=params(24),
    )(diffusivity, folded, fields, *halos)
    halos = exchange(packed)

    x_pair, x_next, *halos = halos
    sides = [wall, wall, edge, edge]
    fields_out, picked = pl.pallas_call(
        inner_kernel, in_specs=[SMEM] * 2 + [VMEM] * 5, out_specs=[ANY, VMEM],
        out_shape=(struct(*fields.shape), struct(LANES, width)),
        scratch_shapes=sides + [
            pltpu.VMEM(fields.shape, jnp.float32), pltpu.SemaphoreType.DMA((10,)),
        ],
        cost_estimate=busy, compiler_params=params(24),
    )(diffusivity, subsample_offsets, fields, first, *halos)
    fields_out, snapshot, chosen = pl.pallas_call(
        outer_kernel, in_specs=[SMEM] * 3 + [VMEM] * 9 + [ANY], out_specs=[ANY, VMEM, VMEM],
        out_shape=(
            struct(*fields.shape), struct(LANES, LANES),
            jax.ShapeDtypeStruct((8, LANES), jnp.int32),
        ),
        scratch_shapes=sides + [
            pltpu.VMEM((LANES, width), jnp.float32),
            pltpu.VMEM((count, 2, height, width), jnp.float32),
            pltpu.SemaphoreType.DMA((2,)),
        ],
        input_output_aliases={12: 0}, compiler_params=params(24),
    )(
        diffusivity, subsample_offsets, column_id, folded, fields, first, x_pair, x_next,
        *halos, picked, fields_out,
    )
    relayed = lax.all_to_all(snapshot.reshape(8, 16, LANES), ("y", "core"), 0, 0, tiled=True)

    message, column = pl.pallas_call(
        product_kernel, in_specs=[VMEM] * 2, out_specs=[VMEM] * 2,
        out_shape=(struct(96, LANES), struct(8, length)),
        scratch_shapes=[pltpu.VMEM((LANES, LANES), jnp.float32)],
        compiler_params=params(16),
    )(relayed, joined)
    message = pl.pallas_call(
        middle_kernel, in_specs=[VMEM], out_specs=VMEM, out_shape=struct(136, LANES),
        scratch_shapes=[pltpu.VMEM((24, LANES), jnp.float32)],
        compiler_params=params(4),
    )(everyone(message, ("x", "y", "core")))
    gathered = everyone(message, ("zh", "zl"))

    coefficients, r_factor, new_columns = pl.pallas_call(
        functools.partial(final_kernel, float(devices * length)),
        in_specs=[VMEM] * 4, out_specs=[VMEM] * 3,
        out_shape=(
            struct(columns, rank), struct(columns, columns), struct(*held_block.shape)
        ),
        compiler_params=params(24),
    )(chosen, gathered, joined, column)
    return fields_out, coefficients.T, r_factor, new_columns


def solution(mesh):
    mesh = jax.sharding.Mesh(mesh.devices.reshape(4, 4, 4, 2, 2), AXES)
    block = P(None, ("zh", "x"), "zl", ("y", "core"))
    rows = P(None, None, ("zh", "x", "y", "core"), "zl", None)
    return jax.shard_map(
        on_device,
        mesh=mesh,
        in_specs=(block, P(), P(), P(), rows, rows),
        out_specs=(block, P(), P(), rows),
        check_vma=False,
    )
```

```python
import functools
import itertools

import jax
import jax.numpy as jnp
from jax import lax
from jax.experimental import pallas as pl
from jax.experimental.pallas import tpu as pltpu
from jax.sharding import PartitionSpec as P

STRIDE = 4
LANES = 128
BLOCK = 5

time_step = 0.1
smagorinsky = 0.02

VMEM = pl.BlockSpec(memory_space=pltpu.VMEM)
ANY = pl.BlockSpec(memory_space=pl.ANY)
SMEM = pl.BlockSpec(memory_space=pltpu.SMEM)
HIGH = lax.Precision.HIGHEST
AXES = ("zh", "x", "y", "core", "zl")


def params(mib):
    return pltpu.CompilerParams(vmem_limit_bytes=mib * 1024 * 1024)


def struct(*shape):
    return jax.ShapeDtypeStruct(shape, jnp.float32)


def iota(shape, dim):
    return lax.broadcasted_iota(jnp.int32, shape, dim)


def dot(left, right, left_dim, right_dim):
    return lax.dot_general(
        left,
        right,
        (((left_dim,), (right_dim,)), ((), ())),
        precision=HIGH,
        preferred_element_type=jnp.float32,
    )


def split(value):
    high = value.astype(jnp.bfloat16)
    value = value - high.astype(jnp.float32)
    middle = value.astype(jnp.bfloat16)
    return high, middle, (value - middle.astype(jnp.float32)).astype(jnp.bfloat16)


def matmul(left, right, right_dim):
    return lax.dot_general(
        left, right, (((1,), (right_dim,)), ((), ())), preferred_element_type=jnp.float32
    )


def odd(axis):
    return lax.rem(lax.axis_index(axis), 2) > 0


def pack(fields, rows, x_pair, x_next, y_row, z_pair, z_next):
    count, cells, height, _ = fields.shape
    upper = lax.axis_index("zl") > 0
    lane, sub = iota((8, LANES), 1), iota((8, LANES), 0)
    keys = [(f, half, tile) for f in range(count) for half in range(2) for tile in range(2)]

    def body(group, faces):
        faces = dict(zip(keys, faces))
        y_rows = {}
        for i in range(8):
            x = group * 8 + i
            for f in range(count):
                for half in range(2):
                    lanes = slice(half * LANES, (half + 1) * LANES)
                    values = (fields[f, x, 0:8, lanes], fields[f, x, height - 8 : height, lanes])
                    row = pltpu.roll(jnp.where(upper, values[0], values[1]), rows[i], 0)
                    y_rows[f, half] = row if i == 0 else jnp.where(sub == i, row, y_rows[f, half])
                    shift = (x + half) % LANES
                    for tile in range(2):
                        face = pltpu.roll(values[tile], shift, 1)
                        faces[f, half, tile] = jnp.where(lane == x, face, faces[f, half, tile])
        for f in range(count):
            for half in range(2):
                place = pl.ds(pl.multiple_of(group * 8, 8), 8)
                y_row[f, place, half * LANES : (half + 1) * LANES] = y_rows[f, half]
        return tuple(faces[key] for key in keys)

    zero = jnp.zeros((8, LANES), jnp.float32)
    faces = lax.fori_loop(0, cells // 8, body, tuple(zero for _ in keys))
    x_odd, second = odd("x"), odd("core")
    for (f, half, tile), face in zip(keys, faces):
        if half == 0:
            other = faces[keys.index((f, 1, tile))]
            place = slice(tile * 8, tile * 8 + 8)
            z_pair[f, place, :] = jnp.where(second, face, other)
            z_next[f, place, :] = jnp.where(second, other, face)
    low, high = fields[:, 0], fields[:, cells - 1]
    x_pair[...] = jnp.where(x_odd, low, high)
    x_next[...] = jnp.where(x_odd, high, low)


def row_shifts(upper):
    return [(i + jnp.where(upper, 0, 1)) % 8 for i in range(8)]


def pack_kernel(fields, x_pair, x_next, y_row, z_pair, z_next):
    rows = row_shifts(lax.axis_index("zl") > 0)
    pack(fields, rows, x_pair, x_next, y_row, z_pair, z_next)


def plane(x, current, before, after, y_low, y_high, z_before, z_after, diffusivity):
    count = current.shape[0]
    lane, sub = iota((8, LANES), 1), iota((8, LANES), 0)
    first_lane, last_lane = lane == 0, lane == LANES - 1
    first_sub, last_sub = sub == 0, sub == 7
    tile_rows = (slice(0, 8), slice(8, 16))
    half_lanes = (slice(0, LANES), slice(LANES, 2 * LANES))
    quarters = [(tile, half) for tile in range(2) for half in range(2)]
    group = pl.ds(pl.multiple_of(x // 8 * 8, 8), 8)
    to_first, to_last = (8 - x % 8) % 8, 7 - x % 8
    centre = {
        (f, tile, half): current[f, x, tile_rows[tile], half_lanes[half]]
        for f in range(count)
        for tile, half in quarters
    }
    speeds = {
        (f, *at): (0.5 * time_step) * centre[f, *at] for f in range(3) for at in quarters
    }
    strain = dict.fromkeys(quarters, 0.0)
    laplace, advect = {}, {}
    for f in range(count):
        y_minus, y_plus, z_minus, z_plus = {}, {}, {}, {}
        for half in range(2):
            lanes = half_lanes[half]
            low = pltpu.roll(y_low[f, group, lanes], to_first, 0)
            high = pltpu.roll(y_high[f, group, lanes], to_last, 0)
            down = [pltpu.roll(centre[f, tile, half], 1, 0) for tile in range(2)]
            up = [pltpu.roll(centre[f, tile, half], 7, 0) for tile in range(2)]
            y_minus[0, half] = jnp.where(first_sub, low, down[0])
            y_minus[1, half] = jnp.where(first_sub, down[0], down[1])
            y_plus[0, half] = jnp.where(last_sub, up[1], up[0])
            y_plus[1, half] = jnp.where(last_sub, high, up[1])
        for tile in range(2):
            low = pltpu.roll(z_before[f, tile_rows[tile], :], (LANES - x) % LANES, 1)
            high = pltpu.roll(z_after[f, tile_rows[tile], :], LANES - 1 - x, 1)
            right = [pltpu.roll(centre[f, tile, half], 1, 1) for half in range(2)]
            left = [pltpu.roll(centre[f, tile, half], LANES - 1, 1) for half in range(2)]
            z_minus[tile, 0] = jnp.where(first_lane, low, right[0])
            z_minus[tile, 1] = jnp.where(first_lane, right[0], right[1])
            z_plus[tile, 0] = jnp.where(last_lane, left[1], left[0])
            z_plus[tile, 1] = jnp.where(last_lane, high, left[1])
        for at in quarters:
            rows, lanes = tile_rows[at[0]], half_lanes[at[1]]
            x_minus, x_plus = before(f, rows, lanes), after(f, rows, lanes)
            slope_x = x_plus - x_minus
            slope_y = y_plus[at] - y_minus[at]
            slope_z = z_plus[at] - z_minus[at]
            laplace[f, *at] = (
                (x_plus + x_minus)
                + (y_plus[at] + y_minus[at])
                + (z_plus[at] + z_minus[at])
                - 6.0 * centre[f, *at]
            )
            if f < 3:
                strain[at] = strain[at] + (
                    slope_x * slope_x + slope_y * slope_y + slope_z * slope_z
                )
            advect[f, *at] = (
                speeds[0, *at] * slope_x + speeds[1, *at] * slope_y + speeds[2, *at] * slope_z
            )
    steps = {}
    for at in quarters:
        eddy = (0.5 * time_step * smagorinsky) * jnp.sqrt(strain[at])
        for f in range(count):
            mixing = time_step * diffusivity[f] + eddy
            steps[f, *at] = mixing * laplace[f, *at] - advect[f, *at]
    return centre, steps


class Planes:
    def __init__(self, current, halos, diffusivity, finish):
        self.x_pair, self.x_next, y_halo, z_pair, z_next, y_low, y_high, z_before, z_after = halos
        self.current, self.finish = current, finish
        self.rest = (y_low, y_high, z_before, z_after, diffusivity)
        cells = current.shape[1]
        upper, second = lax.axis_index("zl") > 0, odd("core")
        z_before[...] = jnp.where(second, z_pair[...], z_next[...])
        z_after[...] = jnp.where(second, z_next[...], z_pair[...])
        y_low[...] = jnp.where(upper, y_halo[:, :cells], 0.0)
        y_high[...] = jnp.where(upper, 0.0, y_halo[:, :cells])

    def one(self, x, before, after):
        self.finish(x, *plane(x, self.current, before, after, *self.rest))

    def inside(self, x):
        return lambda f, rows, lanes: self.current[f, x, rows, lanes]

    def outside(self, here, there):
        x_odd = odd("x")
        return lambda f, rows, lanes: jnp.where(x_odd, here[f, rows, lanes], there[f, rows, lanes])

    def ends(self):
        last = self.current.shape[1] - 1
        self.one(0, self.outside(self.x_pair, self.x_next), self.inside(1))
        self.one(last, self.inside(last - 1), self.outside(self.x_next, self.x_pair))

    def interior(self, after_block=lambda step: None):
        def body(step, carry):
            for i in range(BLOCK):
                x = step * BLOCK + 1 + i
                self.one(x, self.inside(x - 1), self.inside(x + 1))
            after_block(step)
            return carry

        lax.fori_loop(0, (self.current.shape[1] - 2) // BLOCK, body, 0)


def gram_kernel(basis, held, joined, folded):
    rank, _, _, levels, points = basis.shape
    total = rank + held.shape[0]
    for chunk in range(3 * levels):
        lanes = slice(chunk * points, (chunk + 1) * points)
        joined[0:rank, lanes] = basis[:, chunk // levels, 0, chunk % levels, :]
        joined[rank:total, lanes] = held[:, chunk // levels, 0, chunk % levels, :]
    sums = jnp.zeros((3 * total, total), jnp.float32)
    squares = jnp.zeros((total, total), jnp.float32)
    for chunk in range(3 * levels):
        high, middle, low = split(joined[:, chunk * points : (chunk + 1) * points])
        sums += matmul(jnp.concatenate([high, middle, low], axis=0), high, 1)
        squares += matmul(middle, middle, 1)
    half = total // 2
    wide = jnp.zeros((total, LANES - total), jnp.float32)
    cross = jnp.concatenate([sums[total : 2 * total] + sums[2 * total :], wide], axis=1)
    tall = jnp.concatenate([cross, jnp.zeros((LANES - total, LANES), jnp.float32)], axis=0)
    values = jnp.concatenate([sums[:total] + squares, wide], axis=1)
    values = values + (cross + tall.T[:total])
    lane, sub = iota((half, LANES), 1), iota((half, LANES), 0)
    lower = pltpu.roll(values[half:], LANES - half, 1)
    diagonal = jnp.sum(jnp.where(lane == sub, lower, 0.0), axis=1, keepdims=True)
    values = jnp.where(lane < sub, lower, values[:half])
    values = jnp.where(lane == total, jnp.broadcast_to(diagonal, (half, LANES)), values)
    folded[0:half, :] = jnp.where(lane <= total, values, 0.0)
    folded[half:, :] = jnp.zeros((folded.shape[0] - half, LANES), jnp.float32)


def first_kernel(
    diffusivity, folded, current, x_pair_in, x_next_in, y_halo, z_pair_in, z_next_in,
    first, x_pair, x_next, y_row, z_pair, z_next, *edges,
):
    count, cells = current.shape[:2]
    upper = lax.axis_index("zl") > 0
    y_row[:, cells:, :] = jnp.zeros((count, y_row.shape[1] - cells, y_row.shape[2]), jnp.float32)
    for group in range(3):
        lanes = slice(group % 2 * LANES, (group % 2 + 1) * LANES)
        y_row[group // 2, cells:, lanes] = jnp.where(
            upper, folded[group * 8 : group * 8 + 8], folded[group * 8 + 24 : group * 8 + 32]
        )

    def finish(x, centre, steps):
        for (f, tile, half), value in centre.items():
            first[f, x, tile * 8 : tile * 8 + 8, half * LANES : (half + 1) * LANES] = (
                value + steps[f, tile, half]
            )

    halos = (x_pair_in, x_next_in, y_halo, z_pair_in, z_next_in, *edges)
    planes = Planes(current, halos, diffusivity, finish)
    planes.ends()
    planes.interior()
    pack(first, row_shifts(upper), x_pair, x_next, y_row, z_pair, z_next)


def pick(picked, plane, column, keep, shift):
    for f in range(3):
        for tile in range(2):
            rows = pltpu.roll(plane(f, slice(tile * 8, tile * 8 + 8)), shift, 0)
            for part in range(2):
                row = part * 64 + column * 8 + f * 2 + tile
                value = rows[part * STRIDE : part * STRIDE + 1, :]
                if keep is not None:
                    value = jnp.where(keep, picked[row : row + 1, :], value)
                picked[row : row + 1, :] = value


def average(start, value, step):
    return 0.5 * (start + value + step)


def inner_kernel(
    diffusivity, offsets, start, current, y_halo, z_pair, z_next,
    target, picked, y_low, y_high, z_before, z_after, result, semaphores,
):
    cells = current.shape[1]
    blocks = (cells - 2) // BLOCK

    def finish(x, centre, steps):
        for (f, tile, half), value in centre.items():
            at = (f, x, slice(tile * 8, tile * 8 + 8), slice(half * LANES, (half + 1) * LANES))
            result[at] = average(start[at], value, steps[f, tile, half])

    def copied(step):
        part = pl.ds(step * BLOCK + 1, BLOCK)
        return pltpu.make_async_copy(result.at[:, part], target.at[:, part], semaphores.at[step])

    halos = (None, None, y_halo, z_pair, z_next, y_low, y_high, z_before, z_after)
    Planes(current, halos, diffusivity, finish).interior(lambda step: copied(step).start())
    picked[...] = jnp.zeros_like(picked)
    shift = (8 - offsets[1]) % 8
    for column in range(cells // STRIDE):
        x = jnp.clip(column * STRIDE + offsets[2], 1, cells - 2)
        pick(picked, lambda f, rows: result[f, x, rows, :], column, None, shift)

    def settle(step, carry):
        copied(step).wait()
        return carry

    lax.fori_loop(0, blocks, settle, 0)


def outer_kernel(
    diffusivity, offsets, column_id, folded, start, current, x_pair, x_next, y_halo, z_pair,
    z_next, picked_in, target_in, target, snapshot, chosen, y_low, y_high, z_before, z_after, picked, result,
    semaphores,
):
    _, cells, _, width = current.shape

    def finish(x, centre, steps):
        slot = 0 if x == 0 else 1
        for (f, tile, half), value in centre.items():
            rows, lanes = slice(tile * 8, tile * 8 + 8), slice(half * LANES, (half + 1) * LANES)
            result[f, slot, rows, lanes] = average(
                start[f, x, rows, lanes], value, steps[f, tile, half]
            )

    halos = (x_pair, x_next, y_halo, z_pair, z_next, y_low, y_high, z_before, z_after)
    Planes(current, halos, diffusivity, finish).ends()
    copies = [
        pltpu.make_async_copy(
            result.at[:, pl.ds(slot, 1)], target.at[:, pl.ds(x, 1)], semaphores.at[slot]
        )
        for slot, x in ((0, 0), (1, cells - 1))
    ]
    for copy in copies:
        copy.start()
    chosen[...] = jnp.full(chosen.shape, column_id[0], jnp.int32)
    picked[...] = picked_in[...]
    shift = (8 - offsets[1]) % 8
    pick(picked, lambda f, rows: result[f, 0, rows, :], 0, offsets[2] > 0, shift)
    pick(
        picked, lambda f, rows: result[f, 1, rows, :], cells // STRIDE - 1,
        offsets[2] < STRIDE - 1, shift,
    )
    points = width // STRIDE
    choose = iota((width, LANES), 0) == STRIDE * (iota((width, LANES), 1) % points) + offsets[0]
    choose = choose.astype(jnp.float32).astype(jnp.bfloat16)
    high, middle, low = split(picked[...])
    sampled = matmul(high, choose, 0) + matmul(middle, choose, 0) + matmul(low, choose, 0)
    half = snapshot.shape[0]
    snapshot[...] = jnp.where(iota((half, LANES), 1) < points, sampled[:half], sampled[half:])
    upper = lax.axis_index("zl") > 0
    kept = []
    for group in range(3):
        lanes = slice(group % 2 * LANES, (group % 2 + 1) * LANES)
        kept.append(
            jnp.where(
                upper, folded[group * 8 + 24 : group * 8 + 32], folded[group * 8 : group * 8 + 8]
            )
            + y_halo[group // 2, cells:, lanes]
        )
    lane = iota((8, LANES), 1)
    kept = [
        jnp.where(lane < 81, kept[0], pltpu.roll(kept[2], 81, 1)),
        jnp.where(lane < 81, kept[1], pltpu.roll(kept[2], 34, 1)),
    ]
    for column in range(cells // STRIDE):
        for i in range(2):
            row = column * 8 + 6 + i
            snapshot[row : row + 1, :] = kept[i][column : column + 1]
    for copy in copies:
        copy.wait()


def product_kernel(relayed, joined, message, column, partial):
    total = joined.shape[0]
    groups = total // 8
    low = iota((1, LANES), 1) < LANES // 2
    sums = [jnp.zeros((8, LANES), jnp.float32) for _ in range(groups + 1)]
    here = [relayed[source] for source in range(8)]
    turned = [pltpu.roll(rows, LANES // 2, 1) for rows in here]
    for row in range(12):
        left, right = (here, turned) if row % 2 == 0 else (turned, here)
        place = slice(row // 2, row // 2 + 1)
        for pair in range(4):
            tile = row * 4 + pair
            lanes = slice(tile * LANES, (tile + 1) * LANES)
            values = jnp.where(low, left[2 * pair][place], right[2 * pair + 1][place])
            values = jnp.broadcast_to(values, (8, LANES))
            column[:, lanes] = values
            for group in range(groups):
                sums[group] += joined[group * 8 : group * 8 + 8, lanes] * values
            sums[groups] += values * values
    partial[...] = jnp.zeros_like(partial)
    for group in range(groups + 1):
        partial[group * 8 : group * 8 + 8, :] = sums[group]
    products = dot(jnp.ones((8, LANES), jnp.float32), partial[...], 1, 1)
    own = sum(here)
    rows = (own[6:7], own[7:8], products[0:1])
    which = iota((24, LANES), 0) % 3
    values = jnp.where(which == 0, rows[0], jnp.where(which == 1, rows[1], rows[2]))
    count = message.shape[0]
    message[...] = jnp.broadcast_to(values[None], (count // 24, 24, LANES)).reshape(count, LANES)


def middle_kernel(received, message, stacked):
    stacked[...] = jnp.sum(received[...].reshape(-1, 24, LANES), axis=0)
    first, second, third = (stacked[pl.ds(piece, 8, stride=3), :] for piece in range(3))
    third = jnp.sum(third, axis=0, keepdims=True)
    for target in range(message.shape[0] // 17):
        message[target * 17 : target * 17 + 8, :] = first
        message[target * 17 + 8 : target * 17 + 16, :] = second
        message[target * 17 + 16 : target * 17 + 17, :] = third


def final_kernel(
    rows_total, chosen_column, gathered, joined, column,
    coefficients, r_factor, columns_out,
):
    total = joined.shape[0]
    count, rank = coefficients.shape
    _, _, _, levels, points = columns_out.shape
    chosen = chosen_column[0:1, :]
    half = total // 2
    lane = iota((8, LANES), 1)
    pieces = []
    for part in range(2):
        first, second = (
            sum(gathered[17 * (2 * i + part) + at : 17 * (2 * i + part) + at + 8, :] for i in range(4))
            for at in (0, 8)
        )
        third = jnp.where(lane < 47, pltpu.roll(first, 47, 1), pltpu.roll(second, 94, 1))
        pieces.append([first, second, third])
    sums = sum(gathered[17 * i + 16 : 17 * i + 17, :] for i in range(8)) / rows_total
    folded = jnp.concatenate(pieces[0] + pieces[1][:2], axis=0) / rows_total
    turned = jnp.concatenate([folded, jnp.zeros((LANES - half, LANES), jnp.float32)], axis=0).T
    lane, sub = iota((half, LANES), 1), iota((half, LANES), 0)
    diagonal = jnp.broadcast_to(folded[:, total : total + 1], (half, LANES))
    upper = jnp.where((lane >= sub), folded, turned[:half])
    lower = jnp.where(lane < sub, folded, jnp.where(lane > sub, turned[:half], diagonal))
    gram = jnp.concatenate(
        [
            upper,
            jnp.where(lane < half, turned[half:total], pltpu.roll(lower, half, 1)),
        ],
        axis=0,
    )
    lane = iota((total, LANES), 1)
    down = jnp.broadcast_to(sums, (LANES, LANES)).T
    modes = gram[:rank, :rank]
    shifted = pltpu.roll(gram, LANES - rank, 1)
    first = jnp.where(lane[:rank] == chosen, down[:rank], shifted[:rank])[:, :count]
    block_lane, block_sub = iota((count, LANES), 1), iota((count, LANES), 0)
    square = jnp.broadcast_to(sums[:, total : total + 1], (1, LANES))
    across = jnp.where(
        block_lane[0:1] == chosen, square, pltpu.roll(sums, LANES - rank, 1)
    )
    block = jnp.where(block_lane == chosen, down[rank:total], shifted[rank:total])
    block = jnp.where(block_sub == chosen, jnp.broadcast_to(across, (count, LANES)), block)
    second = first - dot(modes, first, 1, 0)
    both = first + second
    third = first - dot(modes, both, 1, 0)
    square = dot(
        jnp.concatenate([first, both], axis=0), jnp.concatenate([both, third], axis=0), 0, 0
    )
    square = jnp.concatenate([square, jnp.zeros((count, LANES - count), jnp.float32)], axis=1)
    state = jnp.where(block_lane < count, block - square, 0.0)
    state = jnp.where(block_lane == block_sub + count, 1.0, state)
    for step in range(count - 1):
        row = state[step : step + 1, :]
        scale = state[:, step : step + 1] / row[:, step : step + 1]
        scale = jnp.where(block_sub > step, jnp.broadcast_to(scale, (count, LANES)), 0.0)
        state = state - scale * row
    diagonal = jnp.sum(jnp.where(block_lane == block_sub, state, 0.0), axis=1, keepdims=True)
    state = state / jnp.sqrt(diagonal)
    r_factor[...] = jnp.where(block_lane >= block_sub, state, 0.0)[:, :count]
    padded = jnp.concatenate([both, jnp.zeros((rank, LANES - count), jnp.float32)], axis=1)
    padded = jnp.concatenate([padded, jnp.zeros((LANES - rank, LANES), jnp.float32)], axis=0)
    coefficients[...] = padded.T[:count, :rank]
    inverse = pltpu.roll(state, LANES - count, 1)
    inverse = jnp.where(block_lane < count, inverse, 0.0)
    onto_modes = dot(inverse[:, :count], both, 1, 1)
    own = jnp.sum(jnp.where(block_lane == chosen, inverse, 0.0), axis=1, keepdims=True)
    onto_block = pltpu.roll(jnp.where(block_lane == chosen, 0.0, inverse), rank, 1)
    onto_modes = jnp.concatenate(
        [-onto_modes, jnp.zeros((count, LANES - rank), jnp.float32)], axis=1
    )
    weights = jnp.where(block_lane < rank, onto_modes, onto_block)[:, :total]
    weights = jnp.concatenate(split(weights), axis=0)
    for chunk in range(3 * levels):
        lanes = slice(chunk * points, (chunk + 1) * points)
        high, middle, low = split(joined[:, lanes])
        first = matmul(weights, high, 0)
        second = matmul(weights[: 2 * count], middle, 0)
        third = matmul(weights[:count], low, 0)
        columns_out[:, chunk // levels, 0, chunk % levels, :] = (
            (first[:count] + own * column[0:1, lanes])
            + (first[count : 2 * count] + second[:count])
            + (first[2 * count :] + second[count:] + third)
        )


def moved(value, axes, target):
    sizes = [lax.axis_size(axis) for axis in axes]
    places = list(itertools.product(*(range(size) for size in sizes)))
    flat = {place: i for i, place in enumerate(places)}
    pairs = [
        (flat[place], flat[tuple(i % size for i, size in zip(target(*place), sizes))])
        for place in places
    ]
    return lax.ppermute(value, axes, pairs)


def exchange(faces):
    x_pair, x_next, y_row, z_pair, z_next = faces

    def along(zh, x):
        step = x + 1 if x % 2 else x - 1
        return zh + step // 4, step

    def swap(core):
        return (core ^ 1,)

    z_next = moved(z_next, ("y", "core"), lambda y, core: (y + 2 * core - 1, core))
    return (
        moved(x_pair, ("x",), lambda x: (x ^ 1,)),
        moved(x_next, ("zh", "x"), along),
        moved(y_row, ("zl",), lambda zl: (zl + 1,)),
        moved(z_pair, ("core",), swap),
        moved(z_next, ("core",), swap),
    )


def everyone(message, axes):
    rows = message.shape[0]
    message = lax.all_to_all(message.reshape(rows, 1, LANES), axes, 0, 0, tiled=True)
    return message.reshape(rows, LANES)


def on_device(fields, diffusivity, subsample_offsets, column_id, pod_basis, held_block):
    count, cells, height, width = fields.shape
    rank, columns = pod_basis.shape[0], held_block.shape[0]
    devices = 1
    for axis in AXES:
        devices *= lax.axis_size(axis)
    points = held_block.shape[-1]
    chunks = 3 * held_block.shape[3]
    length = chunks * points
    total = rank + columns
    faces = (
        struct(count, height, width),
        struct(count, height, width),
        struct(count, cells, width),
        struct(count, height, LANES),
        struct(count, height, LANES),
    )
    wall = pltpu.VMEM((count, cells, width), jnp.float32)
    edge = pltpu.VMEM((count, height, LANES), jnp.float32)
    busy = pl.CostEstimate(flops=2 * 10**7, bytes_accessed=2 * 10**7, transcendentals=0)

    packed = pl.pallas_call(
        pack_kernel, in_specs=[VMEM], out_specs=[VMEM] * 5, out_shape=faces,
        compiler_params=params(16),
    )(fields)
    halos = exchange(packed)

    joined, folded = pl.pallas_call(
        gram_kernel, in_specs=[VMEM] * 2, out_specs=[VMEM] * 2,
        out_shape=(struct(total, length), struct(48, LANES)),
        compiler_params=params(16),
    )(pod_basis, held_block)

    first, *packed = pl.pallas_call(
        first_kernel, in_specs=[SMEM] + [VMEM] * 7, out_specs=[VMEM] * 6,
        out_shape=(struct(*fields.shape),) + faces[:2] + (struct(count, cells + 8, width),)
        + faces[3:],
        scratch_shapes=[wall, wall, edge, edge], compiler_params=params(24),
    )(diffusivity, folded, fields, *halos)
    halos = exchange(packed)

    x_pair, x_next, *halos = halos
    sides = [wall, wall, edge, edge]
    fields_out, picked = pl.pallas_call(
        inner_kernel, in_specs=[SMEM] * 2 + [VMEM] * 5, out_specs=[ANY, VMEM],
        out_shape=(struct(*fields.shape), struct(LANES, width)),
        scratch_shapes=sides + [
            pltpu.VMEM(fields.shape, jnp.float32), pltpu.SemaphoreType.DMA((10,)),
        ],
        cost_estimate=busy, compiler_params=params(24),
    )(diffusivity, subsample_offsets, fields, first, *halos)
    fields_out, snapshot, chosen = pl.pallas_call(
        outer_kernel, in_specs=[SMEM] * 3 + [VMEM] * 9 + [ANY], out_specs=[ANY, VMEM, VMEM],
        out_shape=(
            struct(*fields.shape), struct(LANES // 2, LANES),
            jax.ShapeDtypeStruct((8, LANES), jnp.int32),
        ),
        scratch_shapes=sides + [
            pltpu.VMEM((LANES, width), jnp.float32),
            pltpu.VMEM((count, 2, height, width), jnp.float32),
            pltpu.SemaphoreType.DMA((2,)),
        ],
        input_output_aliases={12: 0}, compiler_params=params(24),
    )(
        diffusivity, subsample_offsets, column_id, folded, fields, first, x_pair, x_next,
        *halos, picked, fields_out,
    )
    relayed = lax.all_to_all(snapshot.reshape(8, 8, LANES), ("y", "core"), 0, 0, tiled=True)

    message, column = pl.pallas_call(
        product_kernel, in_specs=[VMEM] * 2, out_specs=[VMEM] * 2,
        out_shape=(struct(96, LANES), struct(8, length)),
        scratch_shapes=[pltpu.VMEM((LANES, LANES), jnp.float32)],
        compiler_params=params(16),
    )(relayed, joined)
    message = pl.pallas_call(
        middle_kernel, in_specs=[VMEM], out_specs=VMEM, out_shape=struct(136, LANES),
        scratch_shapes=[pltpu.VMEM((24, LANES), jnp.float32)],
        compiler_params=params(4),
    )(everyone(message, ("x", "y", "core")))
    gathered = everyone(message, ("zh", "zl"))

    coefficients, r_factor, new_columns = pl.pallas_call(
        functools.partial(final_kernel, float(devices * length)),
        in_specs=[VMEM] * 4, out_specs=[VMEM] * 3,
        out_shape=(
            struct(columns, rank), struct(columns, columns), struct(*held_block.shape)
        ),
        compiler_params=params(24),
    )(chosen, gathered, joined, column)
    return fields_out, coefficients.T, r_factor, new_columns


def solution(mesh):
    mesh = jax.sharding.Mesh(mesh.devices.reshape(4, 4, 4, 2, 2), AXES)
    block = P(None, ("zh", "x"), "zl", ("y", "core"))
    rows = P(None, None, ("zh", "x", "y", "core"), "zl", None)
    return jax.shard_map(
        on_device,
        mesh=mesh,
        in_specs=(block, P(), P(), P(), rows, rows),
        out_specs=(block, P(), P(), rows),
        check_vma=False,
    )
```

```python
import functools
import itertools

import jax
import jax.numpy as jnp
from jax import lax
from jax.experimental import pallas as pl
from jax.experimental.pallas import tpu as pltpu
from jax.sharding import PartitionSpec as P

STRIDE = 4
LANES = 128
BLOCK = 5

time_step = 0.1
smagorinsky = 0.02

VMEM = pl.BlockSpec(memory_space=pltpu.VMEM)
ANY = pl.BlockSpec(memory_space=pl.ANY)
SMEM = pl.BlockSpec(memory_space=pltpu.SMEM)
HIGH = lax.Precision.HIGHEST
AXES = ("zh", "x", "y", "core", "zl")


def params(mib):
    return pltpu.CompilerParams(vmem_limit_bytes=mib * 1024 * 1024)


def struct(*shape):
    return jax.ShapeDtypeStruct(shape, jnp.float32)


def iota(shape, dim):
    return lax.broadcasted_iota(jnp.int32, shape, dim)


def dot(left, right, left_dim, right_dim):
    return lax.dot_general(
        left,
        right,
        (((left_dim,), (right_dim,)), ((), ())),
        precision=HIGH,
        preferred_element_type=jnp.float32,
    )


def split(value):
    high = value.astype(jnp.bfloat16)
    value = value - high.astype(jnp.float32)
    middle = value.astype(jnp.bfloat16)
    return high, middle, (value - middle.astype(jnp.float32)).astype(jnp.bfloat16)


def matmul(left, right, right_dim):
    return lax.dot_general(
        left, right, (((1,), (right_dim,)), ((), ())), preferred_element_type=jnp.float32
    )


def odd(axis):
    return lax.rem(lax.axis_index(axis), 2) > 0


def pack(fields, rows, x_pair, x_next, y_row, z_pair, z_next):
    count, cells, height, _ = fields.shape
    upper = lax.axis_index("zl") > 0
    lane, sub = iota((8, LANES), 1), iota((8, LANES), 0)
    keys = [(f, half, tile) for f in range(count) for half in range(2) for tile in range(2)]

    def body(group, faces):
        faces = dict(zip(keys, faces))
        y_rows = {}
        for i in range(8):
            x = group * 8 + i
            for f in range(count):
                for half in range(2):
                    lanes = slice(half * LANES, (half + 1) * LANES)
                    values = (fields[f, x, 0:8, lanes], fields[f, x, height - 8 : height, lanes])
                    row = pltpu.roll(jnp.where(upper, values[0], values[1]), rows[i], 0)
                    y_rows[f, half] = row if i == 0 else jnp.where(sub == i, row, y_rows[f, half])
                    shift = (x + half) % LANES
                    for tile in range(2):
                        face = pltpu.roll(values[tile], shift, 1)
                        faces[f, half, tile] = jnp.where(lane == x, face, faces[f, half, tile])
        for f in range(count):
            for half in range(2):
                place = pl.ds(pl.multiple_of(group * 8, 8), 8)
                y_row[f, place, half * LANES : (half + 1) * LANES] = y_rows[f, half]
        return tuple(faces[key] for key in keys)

    zero = jnp.zeros((8, LANES), jnp.float32)
    faces = lax.fori_loop(0, cells // 8, body, tuple(zero for _ in keys))
    x_odd, second = odd("x"), odd("core")
    for (f, half, tile), face in zip(keys, faces):
        if half == 0:
            other = faces[keys.index((f, 1, tile))]
            place = slice(tile * 8, tile * 8 + 8)
            z_pair[f, place, :] = jnp.where(second, face, other)
            z_next[f, place, :] = jnp.where(second, other, face)
    low, high = fields[:, 0], fields[:, cells - 1]
    x_pair[...] = jnp.where(x_odd, low, high)
    x_next[...] = jnp.where(x_odd, high, low)


def row_shifts(upper):
    return [(i + jnp.where(upper, 0, 1)) % 8 for i in range(8)]


def pack_kernel(fields, x_next, x_pair, y_row, z_pair, z_next):
    rows = row_shifts(lax.axis_index("zl") > 0)
    pack(fields, rows, x_pair, x_next, y_row, z_pair, z_next)


def plane(x, current, before, after, y_low, y_high, z_before, z_after, diffusivity):
    count = current.shape[0]
    lane, sub = iota((8, LANES), 1), iota((8, LANES), 0)
    first_lane, last_lane = lane == 0, lane == LANES - 1
    first_sub, last_sub = sub == 0, sub == 7
    tile_rows = (slice(0, 8), slice(8, 16))
    half_lanes = (slice(0, LANES), slice(LANES, 2 * LANES))
    quarters = [(tile, half) for tile in range(2) for half in range(2)]
    group = pl.ds(pl.multiple_of(x // 8 * 8, 8), 8)
    to_first, to_last = (8 - x % 8) % 8, 7 - x % 8
    centre = {
        (f, tile, half): current[f, x, tile_rows[tile], half_lanes[half]]
        for f in range(count)
        for tile, half in quarters
    }
    speeds = {
        (f, *at): (0.5 * time_step) * centre[f, *at] for f in range(3) for at in quarters
    }
    strain = dict.fromkeys(quarters, 0.0)
    laplace, advect = {}, {}
    for f in range(count):
        y_minus, y_plus, z_minus, z_plus = {}, {}, {}, {}
        for half in range(2):
            lanes = half_lanes[half]
            low = pltpu.roll(y_low[f, group, lanes], to_first, 0)
            high = pltpu.roll(y_high[f, group, lanes], to_last, 0)
            down = [pltpu.roll(centre[f, tile, half], 1, 0) for tile in range(2)]
            up = [pltpu.roll(centre[f, tile, half], 7, 0) for tile in range(2)]
            y_minus[0, half] = jnp.where(first_sub, low, down[0])
            y_minus[1, half] = jnp.where(first_sub, down[0], down[1])
            y_plus[0, half] = jnp.where(last_sub, up[1], up[0])
            y_plus[1, half] = jnp.where(last_sub, high, up[1])
        for tile in range(2):
            low = pltpu.roll(z_before[f, tile_rows[tile], :], (LANES - x) % LANES, 1)
            high = pltpu.roll(z_after[f, tile_rows[tile], :], LANES - 1 - x, 1)
            right = [pltpu.roll(centre[f, tile, half], 1, 1) for half in range(2)]
            left = [pltpu.roll(centre[f, tile, half], LANES - 1, 1) for half in range(2)]
            z_minus[tile, 0] = jnp.where(first_lane, low, right[0])
            z_minus[tile, 1] = jnp.where(first_lane, right[0], right[1])
            z_plus[tile, 0] = jnp.where(last_lane, left[1], left[0])
            z_plus[tile, 1] = jnp.where(last_lane, high, left[1])
        for at in quarters:
            rows, lanes = tile_rows[at[0]], half_lanes[at[1]]
            x_minus, x_plus = before(f, rows, lanes), after(f, rows, lanes)
            slope_x = x_plus - x_minus
            slope_y = y_plus[at] - y_minus[at]
            slope_z = z_plus[at] - z_minus[at]
            laplace[f, *at] = (
                (x_plus + x_minus)
                + (y_plus[at] + y_minus[at])
                + (z_plus[at] + z_minus[at])
                - 6.0 * centre[f, *at]
            )
            if f < 3:
                strain[at] = strain[at] + (
                    slope_x * slope_x + slope_y * slope_y + slope_z * slope_z
                )
            advect[f, *at] = (
                speeds[0, *at] * slope_x + speeds[1, *at] * slope_y + speeds[2, *at] * slope_z
            )
    steps = {}
    for at in quarters:
        eddy = (0.5 * time_step * smagorinsky) * jnp.sqrt(strain[at])
        for f in range(count):
            mixing = time_step * diffusivity[f] + eddy
            steps[f, *at] = mixing * laplace[f, *at] - advect[f, *at]
    return centre, steps


class Planes:
    def __init__(self, current, halos, diffusivity, finish):
        self.x_pair, self.x_next, y_halo, z_pair, z_next, y_low, y_high, z_before, z_after = halos
        self.current, self.finish = current, finish
        self.rest = (y_low, y_high, z_before, z_after, diffusivity)
        cells = current.shape[1]
        upper, second = lax.axis_index("zl") > 0, odd("core")
        z_before[...] = jnp.where(second, z_pair[...], z_next[...])
        z_after[...] = jnp.where(second, z_next[...], z_pair[...])
        y_low[...] = jnp.where(upper, y_halo[:, :cells], 0.0)
        y_high[...] = jnp.where(upper, 0.0, y_halo[:, :cells])

    def one(self, x, before, after):
        self.finish(x, *plane(x, self.current, before, after, *self.rest))

    def inside(self, x):
        return lambda f, rows, lanes: self.current[f, x, rows, lanes]

    def outside(self, here, there):
        x_odd = odd("x")
        return lambda f, rows, lanes: jnp.where(x_odd, here[f, rows, lanes], there[f, rows, lanes])

    def ends(self):
        last = self.current.shape[1] - 1
        self.one(0, self.outside(self.x_pair, self.x_next), self.inside(1))
        self.one(last, self.inside(last - 1), self.outside(self.x_next, self.x_pair))

    def interior(self, after_block=lambda step: None):
        def body(step, carry):
            for i in range(BLOCK):
                x = step * BLOCK + 1 + i
                self.one(x, self.inside(x - 1), self.inside(x + 1))
            after_block(step)
            return carry

        lax.fori_loop(0, (self.current.shape[1] - 2) // BLOCK, body, 0)


def gram_kernel(basis, held, joined, folded):
    rank, _, _, levels, points = basis.shape
    total = rank + held.shape[0]
    for chunk in range(3 * levels):
        lanes = slice(chunk * points, (chunk + 1) * points)
        joined[0:rank, lanes] = basis[:, chunk // levels, 0, chunk % levels, :]
        joined[rank:total, lanes] = held[:, chunk // levels, 0, chunk % levels, :]
    sums = jnp.zeros((3 * total, total), jnp.float32)
    squares = jnp.zeros((total, total), jnp.float32)
    for chunk in range(3 * levels):
        high, middle, low = split(joined[:, chunk * points : (chunk + 1) * points])
        sums += matmul(jnp.concatenate([high, middle, low], axis=0), high, 1)
        squares += matmul(middle, middle, 1)
    half = total // 2
    wide = jnp.zeros((total, LANES - total), jnp.float32)
    cross = jnp.concatenate([sums[total : 2 * total] + sums[2 * total :], wide], axis=1)
    tall = jnp.concatenate([cross, jnp.zeros((LANES - total, LANES), jnp.float32)], axis=0)
    values = jnp.concatenate([sums[:total] + squares, wide], axis=1)
    values = values + (cross + tall.T[:total])
    lane, sub = iota((half, LANES), 1), iota((half, LANES), 0)
    lower = pltpu.roll(values[half:], LANES - half, 1)
    diagonal = jnp.sum(jnp.where(lane == sub, lower, 0.0), axis=1, keepdims=True)
    values = jnp.where(lane < sub, lower, values[:half])
    values = jnp.where(lane == total, jnp.broadcast_to(diagonal, (half, LANES)), values)
    folded[0:half, :] = jnp.where(lane <= total, values, 0.0)
    folded[half:, :] = jnp.zeros((folded.shape[0] - half, LANES), jnp.float32)


def first_kernel(
    diffusivity, folded, current, x_next_in, x_pair_in, y_halo, z_pair_in, z_next_in,
    first, x_next, x_pair, y_row, z_pair, z_next, *edges,
):
    count, cells = current.shape[:2]
    upper = lax.axis_index("zl") > 0
    y_row[:, cells:, :] = jnp.zeros((count, y_row.shape[1] - cells, y_row.shape[2]), jnp.float32)
    for group in range(3):
        lanes = slice(group % 2 * LANES, (group % 2 + 1) * LANES)
        y_row[group // 2, cells:, lanes] = jnp.where(
            upper, folded[group * 8 : group * 8 + 8], folded[group * 8 + 24 : group * 8 + 32]
        )

    def finish(x, centre, steps):
        for (f, tile, half), value in centre.items():
            first[f, x, tile * 8 : tile * 8 + 8, half * LANES : (half + 1) * LANES] = (
                value + steps[f, tile, half]
            )

    halos = (x_pair_in, x_next_in, y_halo, z_pair_in, z_next_in, *edges)
    planes = Planes(current, halos, diffusivity, finish)
    planes.ends()
    planes.interior()
    pack(first, row_shifts(upper), x_pair, x_next, y_row, z_pair, z_next)


def pick(picked, plane, column, keep, shift):
    for f in range(3):
        for tile in range(2):
            rows = pltpu.roll(plane(f, slice(tile * 8, tile * 8 + 8)), shift, 0)
            for part in range(2):
                row = part * 64 + column * 8 + f * 2 + tile
                value = rows[part * STRIDE : part * STRIDE + 1, :]
                if keep is not None:
                    value = jnp.where(keep, picked[row : row + 1, :], value)
                picked[row : row + 1, :] = value


def average(start, value, step):
    return 0.5 * (start + value + step)


def inner_kernel(
    diffusivity, offsets, start, current, y_halo, z_pair, z_next,
    target, picked, y_low, y_high, z_before, z_after, result, semaphores,
):
    cells = current.shape[1]
    blocks = (cells - 2) // BLOCK

    def finish(x, centre, steps):
        for (f, tile, half), value in centre.items():
            at = (f, x, slice(tile * 8, tile * 8 + 8), slice(half * LANES, (half + 1) * LANES))
            result[at] = average(start[at], value, steps[f, tile, half])

    def copied(step):
        part = pl.ds(step * BLOCK + 1, BLOCK)
        return pltpu.make_async_copy(result.at[:, part], target.at[:, part], semaphores.at[step])

    halos = (None, None, y_halo, z_pair, z_next, y_low, y_high, z_before, z_after)
    Planes(current, halos, diffusivity, finish).interior(lambda step: copied(step).start())
    picked[...] = jnp.zeros_like(picked)
    shift = (8 - offsets[1]) % 8
    for column in range(cells // STRIDE):
        x = jnp.clip(column * STRIDE + offsets[2], 1, cells - 2)
        pick(picked, lambda f, rows: result[f, x, rows, :], column, None, shift)

    def settle(step, carry):
        copied(step).wait()
        return carry

    lax.fori_loop(0, blocks, settle, 0)


def outer_kernel(
    diffusivity, offsets, column_id, folded, start, current, x_next, x_pair, y_halo, z_pair,
    z_next, picked_in, target_in, target, snapshot, chosen, y_low, y_high, z_before, z_after, picked, result,
    semaphores,
):
    _, cells, _, width = current.shape

    def finish(x, centre, steps):
        slot = 0 if x == 0 else 1
        for (f, tile, half), value in centre.items():
            rows, lanes = slice(tile * 8, tile * 8 + 8), slice(half * LANES, (half + 1) * LANES)
            result[f, slot, rows, lanes] = average(
                start[f, x, rows, lanes], value, steps[f, tile, half]
            )

    halos = (x_pair, x_next, y_halo, z_pair, z_next, y_low, y_high, z_before, z_after)
    Planes(current, halos, diffusivity, finish).ends()
    copies = [
        pltpu.make_async_copy(
            result.at[:, pl.ds(slot, 1)], target.at[:, pl.ds(x, 1)], semaphores.at[slot]
        )
        for slot, x in ((0, 0), (1, cells - 1))
    ]
    for copy in copies:
        copy.start()
    chosen[...] = jnp.full(chosen.shape, column_id[0], jnp.int32)
    picked[...] = picked_in[...]
    shift = (8 - offsets[1]) % 8
    pick(picked, lambda f, rows: result[f, 0, rows, :], 0, offsets[2] > 0, shift)
    pick(
        picked, lambda f, rows: result[f, 1, rows, :], cells // STRIDE - 1,
        offsets[2] < STRIDE - 1, shift,
    )
    points = width // STRIDE
    choose = iota((width, LANES), 0) == STRIDE * (iota((width, LANES), 1) % points) + offsets[0]
    choose = choose.astype(jnp.float32).astype(jnp.bfloat16)
    high, middle, low = split(picked[...])
    sampled = matmul(high, choose, 0) + matmul(middle, choose, 0) + matmul(low, choose, 0)
    half = snapshot.shape[0]
    snapshot[...] = jnp.where(iota((half, LANES), 1) < points, sampled[:half], sampled[half:])
    upper = lax.axis_index("zl") > 0
    kept = []
    for group in range(3):
        lanes = slice(group % 2 * LANES, (group % 2 + 1) * LANES)
        kept.append(
            jnp.where(
                upper, folded[group * 8 + 24 : group * 8 + 32], folded[group * 8 : group * 8 + 8]
            )
            + y_halo[group // 2, cells:, lanes]
        )
    lane = iota((8, LANES), 1)
    kept = [
        jnp.where(lane < 81, kept[0], pltpu.roll(kept[2], 81, 1)),
        jnp.where(lane < 81, kept[1], pltpu.roll(kept[2], 34, 1)),
    ]
    for column in range(cells // STRIDE):
        for i in range(2):
            row = column * 8 + 6 + i
            snapshot[row : row + 1, :] = kept[i][column : column + 1]
    for copy in copies:
        copy.wait()


def product_kernel(relayed, joined, message, column, partial):
    total = joined.shape[0]
    groups = total // 8
    low = iota((1, LANES), 1) < LANES // 2
    sums = [jnp.zeros((8, LANES), jnp.float32) for _ in range(groups + 1)]
    here = [relayed[source] for source in range(8)]
    turned = [pltpu.roll(rows, LANES // 2, 1) for rows in here]
    for row in range(12):
        left, right = (here, turned) if row % 2 == 0 else (turned, here)
        place = slice(row // 2, row // 2 + 1)
        for pair in range(4):
            tile = row * 4 + pair
            lanes = slice(tile * LANES, (tile + 1) * LANES)
            values = jnp.where(low, left[2 * pair][place], right[2 * pair + 1][place])
            values = jnp.broadcast_to(values, (8, LANES))
            column[:, lanes] = values
            for group in range(groups):
                sums[group] += joined[group * 8 : group * 8 + 8, lanes] * values
            sums[groups] += values * values
    partial[...] = jnp.zeros_like(partial)
    for group in range(groups + 1):
        partial[group * 8 : group * 8 + 8, :] = sums[group]
    products = dot(jnp.ones((8, LANES), jnp.float32), partial[...], 1, 1)
    own = sum(here)
    rows = (own[6:7], own[7:8], products[0:1])
    which = iota((24, LANES), 0) % 3
    values = jnp.where(which == 0, rows[0], jnp.where(which == 1, rows[1], rows[2]))
    count = message.shape[0]
    message[...] = jnp.broadcast_to(values[None], (count // 24, 24, LANES)).reshape(count, LANES)


def middle_kernel(received, message, stacked):
    stacked[...] = jnp.sum(received[...].reshape(-1, 24, LANES), axis=0)
    first, second, third = (stacked[pl.ds(piece, 8, stride=3), :] for piece in range(3))
    third = jnp.sum(third, axis=0, keepdims=True)
    for target in range(message.shape[0] // 17):
        message[target * 17 : target * 17 + 8, :] = first
        message[target * 17 + 8 : target * 17 + 16, :] = second
        message[target * 17 + 16 : target * 17 + 17, :] = third


def final_kernel(
    rows_total, chosen_column, gathered, joined, column,
    coefficients, r_factor, columns_out,
):
    total = joined.shape[0]
    count, rank = coefficients.shape
    _, _, _, levels, points = columns_out.shape
    chosen = chosen_column[0:1, :]
    half = total // 2
    lane = iota((8, LANES), 1)
    pieces = []
    for part in range(2):
        first, second = (
            sum(gathered[17 * (2 * i + part) + at : 17 * (2 * i + part) + at + 8, :] for i in range(4))
            for at in (0, 8)
        )
        third = jnp.where(lane < 47, pltpu.roll(first, 47, 1), pltpu.roll(second, 94, 1))
        pieces.append([first, second, third])
    sums = sum(gathered[17 * i + 16 : 17 * i + 17, :] for i in range(8)) / rows_total
    folded = jnp.concatenate(pieces[0] + pieces[1][:2], axis=0) / rows_total
    turned = jnp.concatenate([folded, jnp.zeros((LANES - half, LANES), jnp.float32)], axis=0).T
    lane, sub = iota((half, LANES), 1), iota((half, LANES), 0)
    diagonal = jnp.broadcast_to(folded[:, total : total + 1], (half, LANES))
    upper = jnp.where((lane >= sub), folded, turned[:half])
    lower = jnp.where(lane < sub, folded, jnp.where(lane > sub, turned[:half], diagonal))
    gram = jnp.concatenate(
        [
            upper,
            jnp.where(lane < half, turned[half:total], pltpu.roll(lower, half, 1)),
        ],
        axis=0,
    )
    lane = iota((total, LANES), 1)
    down = jnp.broadcast_to(sums, (LANES, LANES)).T
    modes = gram[:rank, :rank]
    shifted = pltpu.roll(gram, LANES - rank, 1)
    first = jnp.where(lane[:rank] == chosen, down[:rank], shifted[:rank])[:, :count]
    block_lane, block_sub = iota((count, LANES), 1), iota((count, LANES), 0)
    square = jnp.broadcast_to(sums[:, total : total + 1], (1, LANES))
    across = jnp.where(
        block_lane[0:1] == chosen, square, pltpu.roll(sums, LANES - rank, 1)
    )
    block = jnp.where(block_lane == chosen, down[rank:total], shifted[rank:total])
    block = jnp.where(block_sub == chosen, jnp.broadcast_to(across, (count, LANES)), block)
    second = first - dot(modes, first, 1, 0)
    both = first + second
    third = first - dot(modes, both, 1, 0)
    square = dot(
        jnp.concatenate([first, both], axis=0), jnp.concatenate([both, third], axis=0), 0, 0
    )
    square = jnp.concatenate([square, jnp.zeros((count, LANES - count), jnp.float32)], axis=1)
    state = jnp.where(block_lane < count, block - square, 0.0)
    state = jnp.where(block_lane == block_sub + count, 1.0, state)
    for step in range(count - 1):
        row = state[step : step + 1, :]
        scale = state[:, step : step + 1] / row[:, step : step + 1]
        scale = jnp.where(block_sub > step, jnp.broadcast_to(scale, (count, LANES)), 0.0)
        state = state - scale * row
    diagonal = jnp.sum(jnp.where(block_lane == block_sub, state, 0.0), axis=1, keepdims=True)
    state = state / jnp.sqrt(diagonal)
    r_factor[...] = jnp.where(block_lane >= block_sub, state, 0.0)[:, :count]
    padded = jnp.concatenate([both, jnp.zeros((rank, LANES - count), jnp.float32)], axis=1)
    padded = jnp.concatenate([padded, jnp.zeros((LANES - rank, LANES), jnp.float32)], axis=0)
    coefficients[...] = padded.T[:count, :rank]
    inverse = pltpu.roll(state, LANES - count, 1)
    inverse = jnp.where(block_lane < count, inverse, 0.0)
    onto_modes = dot(inverse[:, :count], both, 1, 1)
    own = jnp.sum(jnp.where(block_lane == chosen, inverse, 0.0), axis=1, keepdims=True)
    onto_block = pltpu.roll(jnp.where(block_lane == chosen, 0.0, inverse), rank, 1)
    onto_modes = jnp.concatenate(
        [-onto_modes, jnp.zeros((count, LANES - rank), jnp.float32)], axis=1
    )
    weights = jnp.where(block_lane < rank, onto_modes, onto_block)[:, :total]
    weights = jnp.concatenate(split(weights), axis=0)
    for chunk in range(3 * levels):
        lanes = slice(chunk * points, (chunk + 1) * points)
        high, middle, low = split(joined[:, lanes])
        first = matmul(weights, high, 0)
        second = matmul(weights[: 2 * count], middle, 0)
        third = matmul(weights[:count], low, 0)
        columns_out[:, chunk // levels, 0, chunk % levels, :] = (
            (first[:count] + own * column[0:1, lanes])
            + (first[count : 2 * count] + second[:count])
            + (first[2 * count :] + second[count:] + third)
        )


def moved(value, axes, target):
    sizes = [lax.axis_size(axis) for axis in axes]
    places = list(itertools.product(*(range(size) for size in sizes)))
    flat = {place: i for i, place in enumerate(places)}
    pairs = [
        (flat[place], flat[tuple(i % size for i, size in zip(target(*place), sizes))])
        for place in places
    ]
    return lax.ppermute(value, axes, pairs)


def exchange(faces):
    x_next, x_pair, y_row, z_pair, z_next = faces

    def along(zh, x):
        step = x + 1 if x % 2 else x - 1
        return zh + step // 4, step

    def swap(core):
        return (core ^ 1,)

    z_next = moved(z_next, ("y", "core"), lambda y, core: (y + 2 * core - 1, core))
    return (
        moved(x_next, ("zh", "x"), along),
        moved(x_pair, ("x",), lambda x: (x ^ 1,)),
        moved(y_row, ("zl",), lambda zl: (zl + 1,)),
        moved(z_pair, ("core",), swap),
        moved(z_next, ("core",), swap),
    )


def everyone(message, axes):
    rows = message.shape[0]
    message = lax.all_to_all(message.reshape(rows, 1, LANES), axes, 0, 0, tiled=True)
    return message.reshape(rows, LANES)


def on_device(fields, diffusivity, subsample_offsets, column_id, pod_basis, held_block):
    count, cells, height, width = fields.shape
    rank, columns = pod_basis.shape[0], held_block.shape[0]
    devices = 1
    for axis in AXES:
        devices *= lax.axis_size(axis)
    points = held_block.shape[-1]
    chunks = 3 * held_block.shape[3]
    length = chunks * points
    total = rank + columns
    faces = (
        struct(count, height, width),
        struct(count, height, width),
        struct(count, cells, width),
        struct(count, height, LANES),
        struct(count, height, LANES),
    )
    wall = pltpu.VMEM((count, cells, width), jnp.float32)
    edge = pltpu.VMEM((count, height, LANES), jnp.float32)
    busy = pl.CostEstimate(flops=2 * 10**7, bytes_accessed=2 * 10**7, transcendentals=0)

    packed = pl.pallas_call(
        pack_kernel, in_specs=[VMEM], out_specs=[VMEM] * 5, out_shape=faces,
        compiler_params=params(16),
    )(fields)
    halos = exchange(packed)

    joined, folded = pl.pallas_call(
        gram_kernel, in_specs=[VMEM] * 2, out_specs=[VMEM] * 2,
        out_shape=(struct(total, length), struct(48, LANES)),
        compiler_params=params(16),
    )(pod_basis, held_block)

    first, *packed = pl.pallas_call(
        first_kernel, in_specs=[SMEM] + [VMEM] * 7, out_specs=[VMEM] * 6,
        out_shape=(struct(*fields.shape),) + faces[:2] + (struct(count, cells + 8, width),)
        + faces[3:],
        scratch_shapes=[wall, wall, edge, edge], compiler_params=params(24),
    )(diffusivity, folded, fields, *halos)
    halos = exchange(packed)

    x_next, x_pair, *halos = halos
    sides = [wall, wall, edge, edge]
    fields_out, picked = pl.pallas_call(
        inner_kernel, in_specs=[SMEM] * 2 + [VMEM] * 5, out_specs=[ANY, VMEM],
        out_shape=(struct(*fields.shape), struct(LANES, width)),
        scratch_shapes=sides + [
            pltpu.VMEM(fields.shape, jnp.float32), pltpu.SemaphoreType.DMA((10,)),
        ],
        cost_estimate=busy, compiler_params=params(24),
    )(diffusivity, subsample_offsets, fields, first, *halos)
    fields_out, snapshot, chosen = pl.pallas_call(
        outer_kernel, in_specs=[SMEM] * 3 + [VMEM] * 9 + [ANY], out_specs=[ANY, VMEM, VMEM],
        out_shape=(
            struct(*fields.shape), struct(LANES // 2, LANES),
            jax.ShapeDtypeStruct((8, LANES), jnp.int32),
        ),
        scratch_shapes=sides + [
            pltpu.VMEM((LANES, width), jnp.float32),
            pltpu.VMEM((count, 2, height, width), jnp.float32),
            pltpu.SemaphoreType.DMA((2,)),
        ],
        input_output_aliases={12: 0}, compiler_params=params(24),
    )(
        diffusivity, subsample_offsets, column_id, folded, fields, first, x_next, x_pair,
        *halos, picked, fields_out,
    )
    relayed = lax.all_to_all(snapshot.reshape(8, 8, LANES), ("y", "core"), 0, 0, tiled=True)

    message, column = pl.pallas_call(
        product_kernel, in_specs=[VMEM] * 2, out_specs=[VMEM] * 2,
        out_shape=(struct(96, LANES), struct(8, length)),
        scratch_shapes=[pltpu.VMEM((LANES, LANES), jnp.float32)],
        compiler_params=params(16),
    )(relayed, joined)
    message = pl.pallas_call(
        middle_kernel, in_specs=[VMEM], out_specs=VMEM, out_shape=struct(136, LANES),
        scratch_shapes=[pltpu.VMEM((24, LANES), jnp.float32)],
        compiler_params=params(4),
    )(everyone(message, ("x", "y", "core")))
    gathered = everyone(message, ("zh", "zl"))

    coefficients, r_factor, new_columns = pl.pallas_call(
        functools.partial(final_kernel, float(devices * length)),
        in_specs=[VMEM] * 4, out_specs=[VMEM] * 3,
        out_shape=(
            struct(columns, rank), struct(columns, columns), struct(*held_block.shape)
        ),
        compiler_params=params(24),
    )(chosen, gathered, joined, column)
    return fields_out, coefficients.T, r_factor, new_columns


def solution(mesh):
    mesh = jax.sharding.Mesh(mesh.devices.reshape(4, 4, 4, 2, 2), AXES)
    block = P(None, ("zh", "x"), "zl", ("y", "core"))
    rows = P(None, None, ("zh", "x", "y", "core"), "zl", None)
    return jax.shard_map(
        on_device,
        mesh=mesh,
        in_specs=(block, P(), P(), P(), rows, rows),
        out_specs=(block, P(), P(), rows),
        check_vma=False,
    )
```

```python
import functools
import itertools

import jax
import jax.numpy as jnp
from jax import lax
from jax.experimental import pallas as pl
from jax.experimental.pallas import tpu as pltpu
from jax.sharding import PartitionSpec as P

STRIDE = 4
LANES = 128
BLOCK = 5

time_step = 0.1
smagorinsky = 0.02

VMEM = pl.BlockSpec(memory_space=pltpu.VMEM)
ANY = pl.BlockSpec(memory_space=pl.ANY)
SMEM = pl.BlockSpec(memory_space=pltpu.SMEM)
HIGH = lax.Precision.HIGHEST
AXES = ("zh", "x", "y", "core", "zl")


def params(mib):
    return pltpu.CompilerParams(vmem_limit_bytes=mib * 1024 * 1024)


def struct(*shape):
    return jax.ShapeDtypeStruct(shape, jnp.float32)


def iota(shape, dim):
    return lax.broadcasted_iota(jnp.int32, shape, dim)


def dot(left, right, left_dim, right_dim):
    return lax.dot_general(
        left,
        right,
        (((left_dim,), (right_dim,)), ((), ())),
        precision=HIGH,
        preferred_element_type=jnp.float32,
    )


def split(value):
    high = value.astype(jnp.bfloat16)
    value = value - high.astype(jnp.float32)
    middle = value.astype(jnp.bfloat16)
    return high, middle, (value - middle.astype(jnp.float32)).astype(jnp.bfloat16)


def matmul(left, right, right_dim):
    return lax.dot_general(
        left, right, (((1,), (right_dim,)), ((), ())), preferred_element_type=jnp.float32
    )


def odd(axis):
    return lax.rem(lax.axis_index(axis), 2) > 0


def pack(fields, rows, x_pair, x_next, y_row, z_pair, z_next):
    count, cells, height, _ = fields.shape
    upper = lax.axis_index("zl") > 0
    lane, sub = iota((8, LANES), 1), iota((8, LANES), 0)
    keys = [(f, half, tile) for f in range(count) for half in range(2) for tile in range(2)]

    def body(group, faces):
        faces = dict(zip(keys, faces))
        y_rows = {}
        for i in range(8):
            x = group * 8 + i
            for f in range(count):
                for half in range(2):
                    lanes = slice(half * LANES, (half + 1) * LANES)
                    values = (fields[f, x, 0:8, lanes], fields[f, x, height - 8 : height, lanes])
                    row = pltpu.roll(jnp.where(upper, values[0], values[1]), rows[i], 0)
                    y_rows[f, half] = row if i == 0 else jnp.where(sub == i, row, y_rows[f, half])
                    shift = (x + half) % LANES
                    for tile in range(2):
                        face = pltpu.roll(values[tile], shift, 1)
                        faces[f, half, tile] = jnp.where(lane == x, face, faces[f, half, tile])
        for f in range(count):
            for half in range(2):
                place = pl.ds(pl.multiple_of(group * 8, 8), 8)
                y_row[f, place, half * LANES : (half + 1) * LANES] = y_rows[f, half]
        return tuple(faces[key] for key in keys)

    zero = jnp.zeros((8, LANES), jnp.float32)
    faces = lax.fori_loop(0, cells // 8, body, tuple(zero for _ in keys))
    x_odd, second = odd("x"), odd("core")
    for (f, half, tile), face in zip(keys, faces):
        if half == 0:
            other = faces[keys.index((f, 1, tile))]
            place = slice(tile * 8, tile * 8 + 8)
            z_pair[f, place, :] = jnp.where(second, face, other)
            z_next[f, place, :] = jnp.where(second, other, face)
    low, high = fields[:, 0], fields[:, cells - 1]
    x_pair[...] = jnp.where(x_odd, low, high)
    x_next[...] = jnp.where(x_odd, high, low)


def row_shifts(upper):
    return [(i + jnp.where(upper, 0, 1)) % 8 for i in range(8)]


def pack_kernel(fields, x_next, x_pair, y_row, z_pair, z_next):
    rows = row_shifts(lax.axis_index("zl") > 0)
    pack(fields, rows, x_pair, x_next, y_row, z_pair, z_next)


def plane(x, current, before, after, y_low, y_high, z_before, z_after, diffusivity):
    count = current.shape[0]
    lane, sub = iota((8, LANES), 1), iota((8, LANES), 0)
    first_lane, last_lane = lane == 0, lane == LANES - 1
    first_sub, last_sub = sub == 0, sub == 7
    tile_rows = (slice(0, 8), slice(8, 16))
    half_lanes = (slice(0, LANES), slice(LANES, 2 * LANES))
    quarters = [(tile, half) for tile in range(2) for half in range(2)]
    group = pl.ds(pl.multiple_of(x // 8 * 8, 8), 8)
    to_first, to_last = (8 - x % 8) % 8, 7 - x % 8
    centre = {
        (f, tile, half): current[f, x, tile_rows[tile], half_lanes[half]]
        for f in range(count)
        for tile, half in quarters
    }
    speeds = {
        (f, *at): (0.5 * time_step) * centre[f, *at] for f in range(3) for at in quarters
    }
    strain = dict.fromkeys(quarters, 0.0)
    laplace, advect = {}, {}
    for f in range(count):
        y_minus, y_plus, z_minus, z_plus = {}, {}, {}, {}
        for half in range(2):
            lanes = half_lanes[half]
            low = pltpu.roll(y_low[f, group, lanes], to_first, 0)
            high = pltpu.roll(y_high[f, group, lanes], to_last, 0)
            down = [pltpu.roll(centre[f, tile, half], 1, 0) for tile in range(2)]
            up = [pltpu.roll(centre[f, tile, half], 7, 0) for tile in range(2)]
            y_minus[0, half] = jnp.where(first_sub, low, down[0])
            y_minus[1, half] = jnp.where(first_sub, down[0], down[1])
            y_plus[0, half] = jnp.where(last_sub, up[1], up[0])
            y_plus[1, half] = jnp.where(last_sub, high, up[1])
        for tile in range(2):
            low = pltpu.roll(z_before[f, tile_rows[tile], :], (LANES - x) % LANES, 1)
            high = pltpu.roll(z_after[f, tile_rows[tile], :], LANES - 1 - x, 1)
            right = [pltpu.roll(centre[f, tile, half], 1, 1) for half in range(2)]
            left = [pltpu.roll(centre[f, tile, half], LANES - 1, 1) for half in range(2)]
            z_minus[tile, 0] = jnp.where(first_lane, low, right[0])
            z_minus[tile, 1] = jnp.where(first_lane, right[0], right[1])
            z_plus[tile, 0] = jnp.where(last_lane, left[1], left[0])
            z_plus[tile, 1] = jnp.where(last_lane, high, left[1])
        for at in quarters:
            rows, lanes = tile_rows[at[0]], half_lanes[at[1]]
            x_minus, x_plus = before(f, rows, lanes), after(f, rows, lanes)
            slope_x = x_plus - x_minus
            slope_y = y_plus[at] - y_minus[at]
            slope_z = z_plus[at] - z_minus[at]
            laplace[f, *at] = (
                (x_plus + x_minus)
                + (y_plus[at] + y_minus[at])
                + (z_plus[at] + z_minus[at])
                - 6.0 * centre[f, *at]
            )
            if f < 3:
                strain[at] = strain[at] + (
                    slope_x * slope_x + slope_y * slope_y + slope_z * slope_z
                )
            advect[f, *at] = (
                speeds[0, *at] * slope_x + speeds[1, *at] * slope_y + speeds[2, *at] * slope_z
            )
    steps = {}
    for at in quarters:
        eddy = (0.5 * time_step * smagorinsky) * jnp.sqrt(strain[at])
        for f in range(count):
            mixing = time_step * diffusivity[f] + eddy
            steps[f, *at] = mixing * laplace[f, *at] - advect[f, *at]
    return centre, steps


class Planes:
    def __init__(self, current, halos, diffusivity, finish):
        self.x_pair, self.x_next, y_halo, z_pair, z_next, y_low, y_high, z_before, z_after = halos
        self.current, self.finish = current, finish
        self.rest = (y_low, y_high, z_before, z_after, diffusivity)
        cells = current.shape[1]
        upper, second = lax.axis_index("zl") > 0, odd("core")
        z_before[...] = jnp.where(second, z_pair[...], z_next[...])
        z_after[...] = jnp.where(second, z_next[...], z_pair[...])
        y_low[...] = jnp.where(upper, y_halo[:, :cells], 0.0)
        y_high[...] = jnp.where(upper, 0.0, y_halo[:, :cells])

    def one(self, x, before, after):
        self.finish(x, *plane(x, self.current, before, after, *self.rest))

    def inside(self, x):
        return lambda f, rows, lanes: self.current[f, x, rows, lanes]

    def outside(self, here, there):
        x_odd = odd("x")
        return lambda f, rows, lanes: jnp.where(x_odd, here[f, rows, lanes], there[f, rows, lanes])

    def ends(self):
        last = self.current.shape[1] - 1
        self.one(0, self.outside(self.x_pair, self.x_next), self.inside(1))
        self.one(last, self.inside(last - 1), self.outside(self.x_next, self.x_pair))

    def interior(self, after_block=lambda step: None):
        def body(step, carry):
            for i in range(BLOCK):
                x = step * BLOCK + 1 + i
                self.one(x, self.inside(x - 1), self.inside(x + 1))
            after_block(step)
            return carry

        lax.fori_loop(0, (self.current.shape[1] - 2) // BLOCK, body, 0)


def gram_kernel(basis, held, joined, folded):
    rank, _, _, levels, points = basis.shape
    total = rank + held.shape[0]
    for chunk in range(3 * levels):
        lanes = slice(chunk * points, (chunk + 1) * points)
        joined[0:rank, lanes] = basis[:, chunk // levels, 0, chunk % levels, :]
        joined[rank:total, lanes] = held[:, chunk // levels, 0, chunk % levels, :]
    sums = jnp.zeros((3 * total, total), jnp.float32)
    squares = jnp.zeros((total, total), jnp.float32)
    for chunk in range(3 * levels):
        high, middle, low = split(joined[:, chunk * points : (chunk + 1) * points])
        sums += matmul(jnp.concatenate([high, middle, low], axis=0), high, 1)
        squares += matmul(middle, middle, 1)
    half = total // 2
    wide = jnp.zeros((total, LANES - total), jnp.float32)
    cross = jnp.concatenate([sums[total : 2 * total] + sums[2 * total :], wide], axis=1)
    tall = jnp.concatenate([cross, jnp.zeros((LANES - total, LANES), jnp.float32)], axis=0)
    values = jnp.concatenate([sums[:total] + squares, wide], axis=1)
    values = values + (cross + tall.T[:total])
    lane, sub = iota((half, LANES), 1), iota((half, LANES), 0)
    lower = pltpu.roll(values[half:], LANES - half, 1)
    diagonal = jnp.sum(jnp.where(lane == sub, lower, 0.0), axis=1, keepdims=True)
    values = jnp.where(lane < sub, lower, values[:half])
    values = jnp.where(lane == total, jnp.broadcast_to(diagonal, (half, LANES)), values)
    folded[0:half, :] = jnp.where(lane <= total, values, 0.0)
    folded[half:, :] = jnp.zeros((folded.shape[0] - half, LANES), jnp.float32)


def first_kernel(
    diffusivity, folded, current, x_next_in, x_pair_in, y_halo, z_pair_in, z_next_in,
    first, x_pair, x_next, y_row, z_pair, z_next, *edges,
):
    count, cells = current.shape[:2]
    upper = lax.axis_index("zl") > 0
    y_row[:, cells:, :] = jnp.zeros((count, y_row.shape[1] - cells, y_row.shape[2]), jnp.float32)
    for group in range(3):
        lanes = slice(group % 2 * LANES, (group % 2 + 1) * LANES)
        y_row[group // 2, cells:, lanes] = jnp.where(
            upper, folded[group * 8 : group * 8 + 8], folded[group * 8 + 24 : group * 8 + 32]
        )

    def finish(x, centre, steps):
        for (f, tile, half), value in centre.items():
            first[f, x, tile * 8 : tile * 8 + 8, half * LANES : (half + 1) * LANES] = (
                value + steps[f, tile, half]
            )

    halos = (x_pair_in, x_next_in, y_halo, z_pair_in, z_next_in, *edges)
    planes = Planes(current, halos, diffusivity, finish)
    planes.ends()
    planes.interior()
    pack(first, row_shifts(upper), x_pair, x_next, y_row, z_pair, z_next)


def pick(picked, plane, column, keep, shift):
    for f in range(3):
        for tile in range(2):
            rows = pltpu.roll(plane(f, slice(tile * 8, tile * 8 + 8)), shift, 0)
            for part in range(2):
                row = part * 64 + column * 8 + f * 2 + tile
                value = rows[part * STRIDE : part * STRIDE + 1, :]
                if keep is not None:
                    value = jnp.where(keep, picked[row : row + 1, :], value)
                picked[row : row + 1, :] = value


def average(start, value, step):
    return 0.5 * (start + value + step)


def inner_kernel(
    diffusivity, offsets, start, current, y_halo, z_pair, z_next,
    target, picked, y_low, y_high, z_before, z_after, result, semaphores,
):
    cells = current.shape[1]
    blocks = (cells - 2) // BLOCK

    def finish(x, centre, steps):
        for (f, tile, half), value in centre.items():
            at = (f, x, slice(tile * 8, tile * 8 + 8), slice(half * LANES, (half + 1) * LANES))
            result[at] = average(start[at], value, steps[f, tile, half])

    def copied(step):
        part = pl.ds(step * BLOCK + 1, BLOCK)
        return pltpu.make_async_copy(result.at[:, part], target.at[:, part], semaphores.at[step])

    halos = (None, None, y_halo, z_pair, z_next, y_low, y_high, z_before, z_after)
    Planes(current, halos, diffusivity, finish).interior(lambda step: copied(step).start())
    picked[...] = jnp.zeros_like(picked)
    shift = (8 - offsets[1]) % 8
    for column in range(cells // STRIDE):
        x = jnp.clip(column * STRIDE + offsets[2], 1, cells - 2)
        pick(picked, lambda f, rows: result[f, x, rows, :], column, None, shift)

    def settle(step, carry):
        copied(step).wait()
        return carry

    lax.fori_loop(0, blocks, settle, 0)


def outer_kernel(
    diffusivity, offsets, column_id, folded, start, current, x_pair, x_next, y_halo, z_pair,
    z_next, picked_in, target_in, target, snapshot, chosen, y_low, y_high, z_before, z_after, picked, result,
    semaphores,
):
    _, cells, _, width = current.shape

    def finish(x, centre, steps):
        slot = 0 if x == 0 else 1
        for (f, tile, half), value in centre.items():
            rows, lanes = slice(tile * 8, tile * 8 + 8), slice(half * LANES, (half + 1) * LANES)
            result[f, slot, rows, lanes] = average(
                start[f, x, rows, lanes], value, steps[f, tile, half]
            )

    halos = (x_pair, x_next, y_halo, z_pair, z_next, y_low, y_high, z_before, z_after)
    Planes(current, halos, diffusivity, finish).ends()
    copies = [
        pltpu.make_async_copy(
            result.at[:, pl.ds(slot, 1)], target.at[:, pl.ds(x, 1)], semaphores.at[slot]
        )
        for slot, x in ((0, 0), (1, cells - 1))
    ]
    for copy in copies:
        copy.start()
    chosen[...] = jnp.full(chosen.shape, column_id[0], jnp.int32)
    picked[...] = picked_in[...]
    shift = (8 - offsets[1]) % 8
    pick(picked, lambda f, rows: result[f, 0, rows, :], 0, offsets[2] > 0, shift)
    pick(
        picked, lambda f, rows: result[f, 1, rows, :], cells // STRIDE - 1,
        offsets[2] < STRIDE - 1, shift,
    )
    points = width // STRIDE
    choose = iota((width, LANES), 0) == STRIDE * (iota((width, LANES), 1) % points) + offsets[0]
    choose = choose.astype(jnp.float32).astype(jnp.bfloat16)
    high, middle, low = split(picked[...])
    sampled = matmul(high, choose, 0) + matmul(middle, choose, 0) + matmul(low, choose, 0)
    half = snapshot.shape[0]
    snapshot[...] = jnp.where(iota((half, LANES), 1) < points, sampled[:half], sampled[half:])
    upper = lax.axis_index("zl") > 0
    kept = []
    for group in range(3):
        lanes = slice(group % 2 * LANES, (group % 2 + 1) * LANES)
        kept.append(
            jnp.where(
                upper, folded[group * 8 + 24 : group * 8 + 32], folded[group * 8 : group * 8 + 8]
            )
            + y_halo[group // 2, cells:, lanes]
        )
    lane = iota((8, LANES), 1)
    kept = [
        jnp.where(lane < 81, kept[0], pltpu.roll(kept[2], 81, 1)),
        jnp.where(lane < 81, kept[1], pltpu.roll(kept[2], 34, 1)),
    ]
    for column in range(cells // STRIDE):
        for i in range(2):
            row = column * 8 + 6 + i
            snapshot[row : row + 1, :] = kept[i][column : column + 1]
    for copy in copies:
        copy.wait()


def product_kernel(relayed, joined, message, column, partial):
    total = joined.shape[0]
    groups = total // 8
    low = iota((1, LANES), 1) < LANES // 2
    sums = [jnp.zeros((8, LANES), jnp.float32) for _ in range(groups + 1)]
    here = [relayed[source] for source in range(8)]
    turned = [pltpu.roll(rows, LANES // 2, 1) for rows in here]
    for row in range(12):
        left, right = (here, turned) if row % 2 == 0 else (turned, here)
        place = slice(row // 2, row // 2 + 1)
        for pair in range(4):
            tile = row * 4 + pair
            lanes = slice(tile * LANES, (tile + 1) * LANES)
            values = jnp.where(low, left[2 * pair][place], right[2 * pair + 1][place])
            values = jnp.broadcast_to(values, (8, LANES))
            column[:, lanes] = values
            for group in range(groups):
                sums[group] += joined[group * 8 : group * 8 + 8, lanes] * values
            sums[groups] += values * values
    partial[...] = jnp.zeros_like(partial)
    for group in range(groups + 1):
        partial[group * 8 : group * 8 + 8, :] = sums[group]
    products = dot(jnp.ones((8, LANES), jnp.float32), partial[...], 1, 1)
    own = sum(here)
    rows = (own[6:7], own[7:8], products[0:1])
    which = iota((24, LANES), 0) % 3
    values = jnp.where(which == 0, rows[0], jnp.where(which == 1, rows[1], rows[2]))
    count = message.shape[0]
    message[...] = jnp.broadcast_to(values[None], (count // 24, 24, LANES)).reshape(count, LANES)


def middle_kernel(received, message, stacked):
    stacked[...] = jnp.sum(received[...].reshape(-1, 24, LANES), axis=0)
    first, second, third = (stacked[pl.ds(piece, 8, stride=3), :] for piece in range(3))
    third = jnp.sum(third, axis=0, keepdims=True)
    for target in range(message.shape[0] // 17):
        message[target * 17 : target * 17 + 8, :] = first
        message[target * 17 + 8 : target * 17 + 16, :] = second
        message[target * 17 + 16 : target * 17 + 17, :] = third


def final_kernel(
    rows_total, chosen_column, gathered, joined, column,
    coefficients, r_factor, columns_out,
):
    total = joined.shape[0]
    count, rank = coefficients.shape
    _, _, _, levels, points = columns_out.shape
    chosen = chosen_column[0:1, :]
    half = total // 2
    lane = iota((8, LANES), 1)
    pieces = []
    for part in range(2):
        first, second = (
            sum(gathered[17 * (2 * i + part) + at : 17 * (2 * i + part) + at + 8, :] for i in range(4))
            for at in (0, 8)
        )
        third = jnp.where(lane < 47, pltpu.roll(first, 47, 1), pltpu.roll(second, 94, 1))
        pieces.append([first, second, third])
    sums = sum(gathered[17 * i + 16 : 17 * i + 17, :] for i in range(8)) / rows_total
    folded = jnp.concatenate(pieces[0] + pieces[1][:2], axis=0) / rows_total
    turned = jnp.concatenate([folded, jnp.zeros((LANES - half, LANES), jnp.float32)], axis=0).T
    lane, sub = iota((half, LANES), 1), iota((half, LANES), 0)
    diagonal = jnp.broadcast_to(folded[:, total : total + 1], (half, LANES))
    upper = jnp.where((lane >= sub), folded, turned[:half])
    lower = jnp.where(lane < sub, folded, jnp.where(lane > sub, turned[:half], diagonal))
    gram = jnp.concatenate(
        [
            upper,
            jnp.where(lane < half, turned[half:total], pltpu.roll(lower, half, 1)),
        ],
        axis=0,
    )
    lane = iota((total, LANES), 1)
    down = jnp.broadcast_to(sums, (LANES, LANES)).T
    modes = gram[:rank, :rank]
    shifted = pltpu.roll(gram, LANES - rank, 1)
    first = jnp.where(lane[:rank] == chosen, down[:rank], shifted[:rank])[:, :count]
    block_lane, block_sub = iota((count, LANES), 1), iota((count, LANES), 0)
    square = jnp.broadcast_to(sums[:, total : total + 1], (1, LANES))
    across = jnp.where(
        block_lane[0:1] == chosen, square, pltpu.roll(sums, LANES - rank, 1)
    )
    block = jnp.where(block_lane == chosen, down[rank:total], shifted[rank:total])
    block = jnp.where(block_sub == chosen, jnp.broadcast_to(across, (count, LANES)), block)
    second = first - dot(modes, first, 1, 0)
    both = first + second
    third = first - dot(modes, both, 1, 0)
    square = dot(
        jnp.concatenate([first, both], axis=0), jnp.concatenate([both, third], axis=0), 0, 0
    )
    square = jnp.concatenate([square, jnp.zeros((count, LANES - count), jnp.float32)], axis=1)
    state = jnp.where(block_lane < count, block - square, 0.0)
    state = jnp.where(block_lane == block_sub + count, 1.0, state)
    for step in range(count - 1):
        row = state[step : step + 1, :]
        scale = state[:, step : step + 1] / row[:, step : step + 1]
        scale = jnp.where(block_sub > step, jnp.broadcast_to(scale, (count, LANES)), 0.0)
        state = state - scale * row
    diagonal = jnp.sum(jnp.where(block_lane == block_sub, state, 0.0), axis=1, keepdims=True)
    state = state / jnp.sqrt(diagonal)
    r_factor[...] = jnp.where(block_lane >= block_sub, state, 0.0)[:, :count]
    padded = jnp.concatenate([both, jnp.zeros((rank, LANES - count), jnp.float32)], axis=1)
    padded = jnp.concatenate([padded, jnp.zeros((LANES - rank, LANES), jnp.float32)], axis=0)
    coefficients[...] = padded.T[:count, :rank]
    inverse = pltpu.roll(state, LANES - count, 1)
    inverse = jnp.where(block_lane < count, inverse, 0.0)
    onto_modes = dot(inverse[:, :count], both, 1, 1)
    own = jnp.sum(jnp.where(block_lane == chosen, inverse, 0.0), axis=1, keepdims=True)
    onto_block = pltpu.roll(jnp.where(block_lane == chosen, 0.0, inverse), rank, 1)
    onto_modes = jnp.concatenate(
        [-onto_modes, jnp.zeros((count, LANES - rank), jnp.float32)], axis=1
    )
    weights = jnp.where(block_lane < rank, onto_modes, onto_block)[:, :total]
    weights = jnp.concatenate(split(weights), axis=0)
    for chunk in range(3 * levels):
        lanes = slice(chunk * points, (chunk + 1) * points)
        high, middle, low = split(joined[:, lanes])
        first = matmul(weights, high, 0)
        second = matmul(weights[: 2 * count], middle, 0)
        third = matmul(weights[:count], low, 0)
        columns_out[:, chunk // levels, 0, chunk % levels, :] = (
            (first[:count] + own * column[0:1, lanes])
            + (first[count : 2 * count] + second[:count])
            + (first[2 * count :] + second[count:] + third)
        )


def moved(value, axes, target):
    sizes = [lax.axis_size(axis) for axis in axes]
    places = list(itertools.product(*(range(size) for size in sizes)))
    flat = {place: i for i, place in enumerate(places)}
    pairs = [
        (flat[place], flat[tuple(i % size for i, size in zip(target(*place), sizes))])
        for place in places
    ]
    return lax.ppermute(value, axes, pairs)


def exchange(faces):
    x_next, x_pair, y_row, z_pair, z_next = faces

    def along(zh, x):
        step = x + 1 if x % 2 else x - 1
        return zh + step // 4, step

    def swap(core):
        return (core ^ 1,)

    z_next = moved(z_next, ("y", "core"), lambda y, core: (y + 2 * core - 1, core))
    return (
        moved(x_next, ("zh", "x"), along),
        moved(x_pair, ("x",), lambda x: (x ^ 1,)),
        moved(y_row, ("zl",), lambda zl: (zl + 1,)),
        moved(z_pair, ("core",), swap),
        moved(z_next, ("core",), swap),
    )


def everyone(message, axes):
    rows = message.shape[0]
    message = lax.all_to_all(message.reshape(rows, 1, LANES), axes, 0, 0, tiled=True)
    return message.reshape(rows, LANES)


def on_device(fields, diffusivity, subsample_offsets, column_id, pod_basis, held_block):
    count, cells, height, width = fields.shape
    rank, columns = pod_basis.shape[0], held_block.shape[0]
    devices = 1
    for axis in AXES:
        devices *= lax.axis_size(axis)
    points = held_block.shape[-1]
    chunks = 3 * held_block.shape[3]
    length = chunks * points
    total = rank + columns
    faces = (
        struct(count, height, width),
        struct(count, height, width),
        struct(count, cells, width),
        struct(count, height, LANES),
        struct(count, height, LANES),
    )
    wall = pltpu.VMEM((count, cells, width), jnp.float32)
    edge = pltpu.VMEM((count, height, LANES), jnp.float32)
    busy = pl.CostEstimate(flops=2 * 10**7, bytes_accessed=2 * 10**7, transcendentals=0)

    packed = pl.pallas_call(
        pack_kernel, in_specs=[VMEM], out_specs=[VMEM] * 5, out_shape=faces,
        compiler_params=params(16),
    )(fields)
    halos = exchange(packed)

    joined, folded = pl.pallas_call(
        gram_kernel, in_specs=[VMEM] * 2, out_specs=[VMEM] * 2,
        out_shape=(struct(total, length), struct(48, LANES)),
        compiler_params=params(16),
    )(pod_basis, held_block)

    first, *packed = pl.pallas_call(
        first_kernel, in_specs=[SMEM] + [VMEM] * 7, out_specs=[VMEM] * 6,
        out_shape=(struct(*fields.shape),) + faces[:2] + (struct(count, cells + 8, width),)
        + faces[3:],
        scratch_shapes=[wall, wall, edge, edge], compiler_params=params(24),
    )(diffusivity, folded, fields, *halos)
    x_pair, x_next, *packed = packed
    halos = exchange((x_next, x_pair, *packed))

    x_next, x_pair, *halos = halos
    sides = [wall, wall, edge, edge]
    fields_out, picked = pl.pallas_call(
        inner_kernel, in_specs=[SMEM] * 2 + [VMEM] * 5, out_specs=[ANY, VMEM],
        out_shape=(struct(*fields.shape), struct(LANES, width)),
        scratch_shapes=sides + [
            pltpu.VMEM(fields.shape, jnp.float32), pltpu.SemaphoreType.DMA((10,)),
        ],
        cost_estimate=busy, compiler_params=params(24),
    )(diffusivity, subsample_offsets, fields, first, *halos)
    fields_out, snapshot, chosen = pl.pallas_call(
        outer_kernel, in_specs=[SMEM] * 3 + [VMEM] * 9 + [ANY], out_specs=[ANY, VMEM, VMEM],
        out_shape=(
            struct(*fields.shape), struct(LANES // 2, LANES),
            jax.ShapeDtypeStruct((8, LANES), jnp.int32),
        ),
        scratch_shapes=sides + [
            pltpu.VMEM((LANES, width), jnp.float32),
            pltpu.VMEM((count, 2, height, width), jnp.float32),
            pltpu.SemaphoreType.DMA((2,)),
        ],
        input_output_aliases={12: 0}, compiler_params=params(24),
    )(
        diffusivity, subsample_offsets, column_id, folded, fields, first, x_pair, x_next,
        *halos, picked, fields_out,
    )
    relayed = lax.all_to_all(snapshot.reshape(8, 8, LANES), ("y", "core"), 0, 0, tiled=True)

    message, column = pl.pallas_call(
        product_kernel, in_specs=[VMEM] * 2, out_specs=[VMEM] * 2,
        out_shape=(struct(96, LANES), struct(8, length)),
        scratch_shapes=[pltpu.VMEM((LANES, LANES), jnp.float32)],
        compiler_params=params(16),
    )(relayed, joined)
    message = pl.pallas_call(
        middle_kernel, in_specs=[VMEM], out_specs=VMEM, out_shape=struct(136, LANES),
        scratch_shapes=[pltpu.VMEM((24, LANES), jnp.float32)],
        compiler_params=params(4),
    )(everyone(message, ("x", "y", "core")))
    gathered = everyone(message, ("zh", "zl"))

    coefficients, r_factor, new_columns = pl.pallas_call(
        functools.partial(final_kernel, float(devices * length)),
        in_specs=[VMEM] * 4, out_specs=[VMEM] * 3,
        out_shape=(
            struct(columns, rank), struct(columns, columns), struct(*held_block.shape)
        ),
        compiler_params=params(24),
    )(chosen, gathered, joined, column)
    return fields_out, coefficients.T, r_factor, new_columns


def solution(mesh):
    mesh = jax.sharding.Mesh(mesh.devices.reshape(4, 4, 4, 2, 2), AXES)
    block = P(None, ("zh", "x"), "zl", ("y", "core"))
    rows = P(None, None, ("zh", "x", "y", "core"), "zl", None)
    return jax.shard_map(
        on_device,
        mesh=mesh,
        in_specs=(block, P(), P(), P(), rows, rows),
        out_specs=(block, P(), P(), rows),
        check_vma=False,
    )
```
